32 devices in a mesh: tm: 32 (over z, y, x, core).
Axes of the slice: x: 2, y: 2, z: 4, core: 2. Of those that a mesh axis runs over, the one named last changes fastest.
Arguments:
- inv_diag: float32 [32, 384, 384], P('tm'), may hold values from -0.4 to 4.4, as said below
- low_coupling: float32 [32, 384, 384], P('tm'), may hold values from -0.09375 to 0.09375
- up_coupling: float32 [32, 384, 384], P('tm'), may hold values from -0.09375 to 0.09375
Outputs:
- diag_inverse: float32 [32, 384, 384], P('tm')
- cross_inverse: float32 [32, 384, 384], P('tm')
The draws below stay inside these ranges and needn't reach their ends.
Inputs may be any that keep to these rules, and one draw needn't show every extreme that they name: `inv_diag`: each block is symmetric.
All inputs are finite; a program needn't handle non-finite values.
Results may differ from the reference program's by a relative error of at most 0.00012.
Values sent between devices are 32-bit elements; how exact they have to be, the bound alone decides.
No kernel may reach another device: no remote copies, remote signals or barrier semaphores. Data moves between devices by JAX's collectives and lax.ppermute only.
A program may use at most 64 MiB of HBM per device.

```python
import math
import jax
import jax.numpy as jnp
import numpy as np
from jax import lax

B = 384
CHAIN = 32
BLOCKS = 32


def draw_inv_diag(key, part):
    first, second = jax.random.split(key, 2)
    noise = jnp.clip(jax.random.normal(first, (BLOCKS, B, B), jnp.float32), -4.0, 4.0)
    symmetric = (noise + jnp.swapaxes(noise, 1, 2)) * (0.35 / math.sqrt(B))
    identity = jnp.eye(B, dtype=jnp.float32)
    diagonal = jax.random.uniform(second, (BLOCKS, B), jnp.float32, 1.5, 3.0)
    symmetric = jnp.clip(symmetric, -0.36, 0.36)
    return symmetric + diagonal[:, :, None] * identity


def shard_levels(key, shape, cuts, least, largest):
    def one(axis_at, blocks):
        draws = jax.random.uniform(jax.random.fold_in(jax.random.fold_in(key, 6), axis_at), (blocks,), jnp.float32, least / len(cuts), largest / len(cuts))
        return jnp.repeat(jnp.exp(draws), shape[axis_at] // blocks).reshape((-1,) + (1,) * (len(shape) - axis_at - 1))

    loudness = one(*cuts[0])
    for cut in cuts[1:]:
        loudness = loudness * one(*cut)
    return loudness


def normal_values(stream_key, extent, spread, reach, pieces=(), held_as=jnp.bfloat16):
    drawn = spread * jax.random.normal(stream_key, extent, jnp.float32)
    if pieces:
        drawn = drawn * shard_levels(stream_key, extent, pieces, -0.22, 0.18)
    return jnp.clip(drawn, -reach, reach).astype(held_as)


def setup_inputs(seed: int = 0) -> dict:
    arg_keys = jax.random.split(jax.random.key(seed), 4)
    return {
        "inv_diag": draw_inv_diag(jax.random.fold_in(arg_keys[3], 71), 0),
        "low_coupling": normal_values(arg_keys[1], (BLOCKS, B, B), (10 * B) ** -0.5, 0.09375, ((0, 32),), jnp.float32),
        "up_coupling": normal_values(arg_keys[2], (BLOCKS, B, B), (10 * B) ** -0.5, 0.09375, ((0, 32),), jnp.float32),
    }


row_offset = 3


def multiply(left, right):
    return jnp.einsum("cnij,cnjk->cnik", left, right, precision=lax.Precision.HIGHEST)


def multiply_trans(left, right):
    return jnp.einsum("cnij,cnkj->cnik", left, right, precision=lax.Precision.HIGHEST)


def reference(inv_diag, low_coupling, up_coupling):
    levels = CHAIN.bit_length() - 1
    inverses = jnp.roll(inv_diag, row_offset, axis=0).reshape(1, CHAIN, B, B)
    lowers = jnp.roll(low_coupling, row_offset, axis=0).reshape(1, CHAIN, B, B)
    uppers = jnp.roll(up_coupling, row_offset, axis=0).reshape(1, CHAIN, B, B)
    sigma = jnp.zeros((1, CHAIN + 1, B, B), jnp.float32)
    sigma = sigma.at[:, 0].set(inverses[:, 0])
    cross = jnp.zeros((1, CHAIN + 1, B, B), jnp.float32)
    newest = jnp.zeros((1, CHAIN + 1, B, B), jnp.float32)
    for step_num in range(levels):
        stride = CHAIN // (2 ** (step_num + 1))
        eliminated = np.arange(stride, CHAIN, 2 * stride)
        below_idx = eliminated - stride
        above_idx = np.minimum(eliminated + stride, CHAIN)
        inverse = inverses[:, eliminated]
        g_mat = multiply(inverse, lowers[:, eliminated])
        h_mat = multiply(inverse, uppers[:, eliminated])
        sigma_low = sigma[:, below_idx]
        sigma_high = sigma[:, above_idx]
        sigma_ba = newest[:, above_idx]
        sigma_ab = jnp.swapaxes(sigma_ba, 2, 3)
        part_low = -(multiply(g_mat, sigma_low) + multiply(h_mat, sigma_ba))
        part_high = -(multiply(g_mat, sigma_ab) + multiply(h_mat, sigma_high))
        sigma_tt = inverse - multiply_trans(g_mat, part_low) - multiply_trans(h_mat, part_high)
        sigma = sigma.at[:, eliminated].set(sigma_tt)
        cross = cross.at[:, eliminated].set(part_low)
        newest = newest.at[:, eliminated].set(part_low)
        inside = eliminated + stride < CHAIN
        targets = (eliminated + stride)[inside]
        newest = newest.at[:, targets].set(jnp.swapaxes(part_high[:, inside], 2, 3))
    diag_out = jnp.roll(sigma[0, :CHAIN], -row_offset, axis=0)
    cross_out = jnp.roll(cross[0, :CHAIN], -row_offset, axis=0)
    return diag_out, cross_out
```

```python
import functools

import jax
import jax.numpy as jnp
from jax import lax
from jax.experimental import pallas as pl
from jax.experimental.pallas import tpu as pltpu
from jax.sharding import PartitionSpec as P

row_offset = 3
lanes = 128
group = 8
axis = "tm"
bf16 = jnp.bfloat16
f32 = jnp.float32


def sym_rows(width):
    blocks = width // lanes
    pairs = blocks // 2
    return (blocks * (blocks - 1) // 2 + blocks - pairs) * lanes + 8 * pairs


def full_rows(width):
    return width * (width // lanes)


def tri():
    r = lax.broadcasted_iota(jnp.int32, (lanes, lanes), 0)
    c = lax.broadcasted_iota(jnp.int32, (lanes, lanes), 1)
    return r, c


def put_sym(ref, at, mat):
    blocks = mat.shape[0] // lanes
    block = lambda i, j: mat[i * lanes : (i + 1) * lanes, j * lanes : (j + 1) * lanes]
    for i in range(blocks):
        for j in range(i):
            ref[pl.ds(at, lanes), :] = block(i, j)
            at += lanes
    r, c = tri()
    for i in range(0, blocks - 1, 2):
        one, two = block(i, i), block(i + 1, i + 1)
        ref[pl.ds(at, lanes), :] = jnp.where(r >= c, one, two)
        at += lanes
        line = jnp.sum(jnp.where(r == c, two, 0.0), axis=0, keepdims=True)
        ref[pl.ds(at, 8), :] = jnp.broadcast_to(line, (8, lanes))
        at += 8
    if blocks % 2:
        ref[pl.ds(at, lanes), :] = block(blocks - 1, blocks - 1)


def get_sym(ref, at, width):
    blocks = width // lanes
    got = {}
    for i in range(blocks):
        for j in range(i):
            got[i, j] = ref[pl.ds(at, lanes), :]
            got[j, i] = got[i, j].T
            at += lanes
    r, c = tri()
    for i in range(0, blocks - 1, 2):
        both = ref[pl.ds(at, lanes), :]
        turned = both.T
        at += lanes
        line = ref[pl.ds(at, 8), :][0:1, :]
        at += 8
        got[i, i] = jnp.where(r >= c, both, turned)
        got[i + 1, i + 1] = jnp.where(r == c, line, jnp.where(r < c, both, turned))
    if blocks % 2:
        got[blocks - 1, blocks - 1] = ref[pl.ds(at, lanes), :]
    return jnp.concatenate(
        [jnp.concatenate([got[i, j] for j in range(blocks)], axis=1) for i in range(blocks)], axis=0
    )


def put_full(ref, at, mat):
    width = mat.shape[0]
    for j in range(width // lanes):
        ref[pl.ds(at + j * width, width), :] = mat[:, j * lanes : (j + 1) * lanes]


def get_full(ref, at, width):
    return jnp.concatenate(
        [ref[pl.ds(at + j * width, width), :] for j in range(width // lanes)], axis=1
    )


def parts_of(mat):
    high = mat.astype(bf16)
    return high, (mat - high.astype(f32)).astype(bf16)


def times(left, right, turned=False):
    dims = (((1,), (1 if turned else 0,)), ((), ()))
    dot = lambda a, b: lax.dot_general(a, b, dims, preferred_element_type=f32)
    return dot(left[0], right[0]) + (dot(left[0], right[1]) + dot(left[1], right[0]))


def eliminate(node, state):
    diag, g_mat, h_mat = node
    aa, ba, bb = state
    low = times(g_mat, aa)
    if ba is not None:
        low = low + times(h_mat, ba)
        high = -(times(g_mat, ba, True) + times(h_mat, bb))
    low = -low
    low_parts = parts_of(low)
    own = diag - times(g_mat, low_parts, True)
    if ba is None:
        return own, low, low_parts, None, None
    high_parts = parts_of(high)
    own = own - times(h_mat, high_parts, True)
    return own, low, low_parts, high, high_parts


def place_now(length):
    return lax.rem(lax.axis_index(axis) + row_offset, length)


def fetch(source, target, sem):
    copy = pltpu.make_async_copy(source, target, sem)
    copy.start()
    copy.wait()


def prepare_kernel(inv_ref, low_ref, up_ref, node_ref, part_ref, sym_ref):
    width = inv_ref.shape[1]
    inverse = inv_ref[0]
    inv_parts = parts_of(inverse)
    put_sym(sym_ref, 0, inverse)
    ps, pf = sym_rows(width), full_rows(width)
    node_ref[pl.ds(0, ps), :] = sym_ref[...]
    part_ref[pl.ds(0, ps), :] = sym_ref[...]
    g_mat = times(inv_parts, parts_of(low_ref[0]))
    put_full(node_ref, ps, g_mat)
    put_full(part_ref, ps, g_mat)
    put_full(node_ref, ps + pf, times(inv_parts, parts_of(up_ref[0])))


def get_node(ref, width, whole=True):
    ps, pf = sym_rows(width), full_rows(width)
    return (
        get_sym(ref, 0, width),
        parts_of(get_full(ref, ps, width)),
        parts_of(get_full(ref, ps + pf, width)) if whole else None,
    )


def get_state(ref, width):
    ps, pf = sym_rows(width), full_rows(width)
    return (get_sym(ref, 0, width), get_full(ref, ps, width), get_sym(ref, ps + pf, width))


def put_state(ref, aa, ba, bb):
    width = aa.shape[0]
    ps, pf = sym_rows(width), full_rows(width)
    put_sym(ref, 0, aa)
    put_full(ref, ps, ba)
    put_sym(ref, ps + pf, bb)


def top_kernel(
    length,
    is_open,
    mid_node,
    mid_from_low,
    mid_from_high,
    own_node,
    low_node,
    root_mid,
    root_low,
    root_high,
    inv_ref,
    *refs,
):
    base_cross = None if is_open else refs[0]
    diag_ref, cross_ref, below_ref, above_ref, sym_ref = refs[-12:-7]
    first, second, root, aa_ref, ba_ref, bb_ref, sem = refs[-7:]
    width = inv_ref.shape[1]
    turn = lax.rem(place_now(length), 4 * group)
    at_low, at_mid, at_high = turn == group, turn == 2 * group, turn == 3 * group
    active = jnp.logical_or(at_low, jnp.logical_or(at_mid, at_high))

    @pl.when(jnp.logical_not(active))
    def _():
        diag_ref[0] = inv_ref[0]
        cross_ref[0] = jnp.zeros((width, width), f32) if is_open else base_cross[0]

    @pl.when(at_mid)
    def _():
        fetch(mid_node, first, sem)
        fetch(low_node, second, sem)
        fetch(root_mid, root, sem)

    @pl.when(at_low)
    def _():
        fetch(mid_from_high, first, sem)
        fetch(own_node, second, sem)
        fetch(root_low, root, sem)

    @pl.when(at_high)
    def _():
        fetch(mid_from_low, first, sem)
        fetch(own_node, second, sem)
        fetch(root_high, root, sem)

    @pl.when(active)
    def _():
        node = get_node(first, width, not is_open)
        if is_open:
            aa, ba, bb = get_sym(root, 0, width), None, None
            state = (parts_of(aa), None, None)
        else:
            aa, ba, bb = get_state(root, width)
            state = (parts_of(aa), parts_of(ba), parts_of(bb))
        own, low, _, high, _ = eliminate(node, state)

        @pl.when(at_mid)
        def _():
            diag_ref[0] = own
            cross_ref[0] = low

        @pl.when(jnp.logical_not(at_high))
        def _():
            aa_ref[...] = aa
            ba_ref[...] = low
            bb_ref[...] = own

        @pl.when(at_high)
        def _():
            aa_ref[...] = own
            if is_open:
                ba_ref[...] = jnp.zeros((width, width), f32)
                bb_ref[...] = jnp.zeros((width, width), f32)
            else:
                ba_ref[...] = high.T
                bb_ref[...] = bb

        aa2, ba2, bb2 = aa_ref[...], ba_ref[...], bb_ref[...]
        own2, low2, _, high2, _ = eliminate(
            get_node(second, width), (parts_of(aa2), parts_of(ba2), parts_of(bb2))
        )

        @pl.when(jnp.logical_not(at_mid))
        def _():
            diag_ref[0] = own2
            cross_ref[0] = low2
            put_state(below_ref, aa2, low2, own2)
            put_state(above_ref, own2, high2.T, bb2)
            put_sym(sym_ref, 0, own2)

        @pl.when(at_mid)
        def _():
            put_state(below_ref, own2, high2.T, bb2)


def offset_of(length):
    place = place_now(length)
    turn = lax.rem(place, 4 * group)
    offset = lax.rem(turn, group)
    return turn, offset, turn - offset == 3 * group


def choose_kernel(length, is_open, *refs):
    (from_low, from_high, to_three, to_five, to_seven, end_three, end_five, end_seven) = refs[:8]
    out_ref, zeros_ref, sem = refs[8:]
    rows, end_rows = out_ref.shape[0], end_three.shape[0]
    turn, offset, last = offset_of(length)
    lower = lax.rem(turn, 2 * group) < group

    def pick(condition, source):
        @pl.when(condition)
        def _():
            fetch(source, out_ref, sem)

    def pick_end(condition, source):
        if not is_open:
            return pick(condition, source)

        @pl.when(condition)
        def _():
            zeros_ref[...] = jnp.zeros(zeros_ref.shape, f32)
            fetch(source, out_ref.at[pl.ds(0, end_rows), :], sem)
            fetch(zeros_ref, out_ref.at[pl.ds(end_rows, rows - end_rows), :], sem)

    others = jnp.logical_not(last)
    pick(jnp.logical_and(offset == 1, lower), from_high)
    pick(jnp.logical_and(offset == 1, jnp.logical_not(lower)), from_low)
    for at, usual, end in ((3, to_three, end_three), (5, to_five, end_five), (7, to_seven, end_seven)):
        pick(jnp.logical_and(offset == at, others), usual)
        pick_end(jnp.logical_and(offset == at, last), end)


def go_down(node, refs, to_low):
    aa_ref, ba_ref, bb_ref = refs
    state = tuple(parts_of(ref[...]) for ref in refs)
    own, low, _, high, _ = eliminate(node, state)

    @pl.when(to_low)
    def _():
        ba_ref[...] = low
        bb_ref[...] = own

    @pl.when(jnp.logical_not(to_low))
    def _():
        aa_ref[...] = own
        ba_ref[...] = high.T


def odd_kernel(
    length, state, own_node, four_seven, four_five, four_one, near, nearer, _diag, _cross, diag_ref, cross_ref,
    state_ref, first, second, third, aa_ref, ba_ref, bb_ref, diag_out, cross_out, sem
):
    width = aa_ref.shape[0]
    _, offset, _ = offset_of(length)

    @pl.when(lax.rem(offset, 2) == 1)
    def _():
        fetch(state, state_ref, sem)
        fetch(own_node, third, sem)
        for at, four, two in ((1, four_one, near), (3, near, nearer), (5, four_five, near), (7, four_seven, nearer)):

            @pl.when(offset == at)
            def _(four=four, two=two):
                fetch(four, first, sem)
                fetch(two, second, sem)

        refs = (aa_ref, ba_ref, bb_ref)
        aa_ref[...], ba_ref[...], bb_ref[...] = get_state(state_ref, width)
        go_down(get_node(first, width), refs, offset < group // 2)
        go_down(get_node(second, width), refs, lax.rem(offset, group // 2) < group // 4)
        own, low, _, _, _ = eliminate(get_node(third, width), tuple(parts_of(ref[...]) for ref in refs))
        diag_out[...] = own
        cross_out[...] = low
        fetch(diag_out, diag_ref.at[0], sem)
        fetch(cross_out, cross_ref.at[0], sem)


def even_kernel(
    length, state, own_node, four_six, four_two, _diag, _cross, diag_ref, cross_ref,
    state_ref, first, third, aa_ref, ba_ref, bb_ref, diag_out, cross_out, sem,
):
    width = aa_ref.shape[0]
    _, offset, _ = offset_of(length)

    @pl.when(jnp.logical_and(lax.rem(offset, 2) == 0, offset > 0))
    def _():
        fetch(state, state_ref, sem)
        fetch(own_node, third, sem)
        refs = (aa_ref, ba_ref, bb_ref)
        aa_ref[...], ba_ref[...], bb_ref[...] = get_state(state_ref, width)

        @pl.when(offset != group // 2)
        def _():
            @pl.when(offset < group // 2)
            def _():
                fetch(four_two, first, sem)

            @pl.when(offset > group // 2)
            def _():
                fetch(four_six, first, sem)

            go_down(get_node(first, width), refs, offset < group // 2)

        own, low, _, _, _ = eliminate(get_node(third, width), tuple(parts_of(ref[...]) for ref in refs))
        diag_out[...] = own
        cross_out[...] = low
        fetch(diag_out, diag_ref.at[0], sem)
        fetch(cross_out, cross_ref.at[0], sem)


def pack_kernel(aa_ref, ba_ref, bb_ref, out_ref):
    put_state(out_ref, aa_ref[...], ba_ref[...], bb_ref[...])


def sent(array, length, by, wanted):
    device = lambda position: (position - row_offset) % length
    pairs = [(device(p), device(p + by)) for p in range(length) if wanted(p)]
    return lax.ppermute(array, axis, pairs)


def upper_levels(inverse, node_g, node_h, length):
    width = inverse.shape[0]
    place = (lax.axis_index(axis) + row_offset) % length
    product = functools.partial(jnp.dot, precision=lax.Precision.HIGHEST, preferred_element_type=f32)
    zeros = jnp.zeros((width, width), f32)
    sigma = jnp.where(place == 0, inverse, zeros)
    low_own, high_own, cross = zeros, zeros, zeros
    stride = length // 2
    while True:
        everywhere = lambda p: True
        from_low, owned_high = (sent(x, length, stride, everywhere) for x in (sigma, high_own))
        from_high, owned_low = (sent(x, length, -stride, everywhere) for x in (sigma, low_own))
        has_upper = place + stride < length
        sigma_high = jnp.where(has_upper, from_high, zeros)
        sigma_ba = jnp.where(has_upper, owned_high.T + owned_low, zeros)
        if stride == 2 * group:
            return sigma, cross, (from_low, sigma_ba, sigma_high)
        active = place % (2 * stride) == stride
        low = -(product(node_g, from_low) + product(node_h, sigma_ba))
        high = -(product(node_g, sigma_ba.T) + product(node_h, sigma_high))
        own = inverse - product(node_g, low.T) - product(node_h, high.T)
        sigma = jnp.where(active, own, sigma)
        low_own = jnp.where(active, low, zeros)
        high_own = jnp.where(active, high, zeros)
        cross = jnp.where(active, low, cross)
        stride //= 2


def body(inv_diag, low_coupling, up_coupling):
    width = inv_diag.shape[1]
    length = lax.axis_size(axis)
    is_open = length == 4 * group
    ps, pf = sym_rows(width), full_rows(width)
    node_rows, part_rows, state_rows = ps + 2 * pf, ps + pf, 2 * ps + pf
    rows_of = lambda rows: jax.ShapeDtypeStruct((rows, lanes), f32)
    square = (width, width)
    whole = jax.ShapeDtypeStruct((1,) + square, f32)
    vmem, anywhere = pl.BlockSpec(memory_space=pltpu.VMEM), pl.BlockSpec(memory_space=pl.ANY)
    room = lambda rows: pltpu.VMEM((rows, lanes), f32)
    params = pltpu.CompilerParams(vmem_limit_bytes=48 * 2**20)
    span = 4 * group

    def at(*turns):
        return lambda p: p % span in turns

    node, part, sym = pl.pallas_call(
        prepare_kernel,
        out_shape=(rows_of(node_rows), rows_of(part_rows), rows_of(ps)),
        in_specs=[vmem] * 3,
        out_specs=[vmem] * 3,
        compiler_params=params,
        name="prepare",
    )(inv_diag, low_coupling, up_coupling)

    mid = 2 * group
    if is_open:
        lead = part
        base_diag, base_cross = inv_diag, None
        root_mid, root_low, root_high = (sent(sym, length, by, at(0)) for by in (mid, group, 3 * group))
    else:
        lead = node
        g_mat, h_mat = (
            jnp.concatenate([node[ps + k * pf + j * width :][:width] for j in range(width // lanes)], axis=1)
            for k in (0, 1)
        )
        base_diag, base_cross, state = upper_levels(inv_diag[0], g_mat, h_mat, length)
        base_diag, base_cross = base_diag[None], base_cross[None]
        root_mid = pl.pallas_call(
            pack_kernel, out_shape=rows_of(state_rows), in_specs=[vmem] * 3, out_specs=vmem,
            compiler_params=params, name="pack",
        )(*state)
        root_low, root_high = (sent(root_mid, length, by, at(mid)) for by in (-group, group))
    mid_from_high = sent(lead, length, -group, at(mid))
    low_node = sent(node, length, group, at(group))
    mid_from_low = sent(lead, length, group, at(mid))

    half = group // 2
    inner = lambda *offsets: (lambda p: p % group in offsets)
    four_two = sent(node, length, -2, inner(half))
    four_six = sent(node, length, 2, inner(half))
    four_seven = sent(node, length, 3, inner(half))
    near = sent(node, length, -1, inner(2, 4, 6))
    nearer = sent(node, length, 1, inner(2, 6))
    four_one = sent(four_two, length, -1, inner(2))
    four_five = sent(four_six, length, -1, inner(6))

    top = functools.partial(top_kernel, length, is_open)
    root_rows = ps if is_open else state_rows
    diag, cross, below, above, end = pl.pallas_call(
        top,
        out_shape=(whole, whole, rows_of(state_rows), rows_of(state_rows), rows_of(ps)),
        in_specs=[anywhere] * 8 + [vmem] * (1 if is_open else 2),
        out_specs=[vmem] * 5,
        scratch_shapes=[room(lead.shape[0]), room(node_rows), room(root_rows)]
        + [pltpu.VMEM(square, f32)] * 3
        + [pltpu.SemaphoreType.DMA],
        compiler_params=params,
        name="upper",
    )(lead, mid_from_low, mid_from_high, node, low_node, root_mid, root_low, root_high, base_diag,
      *(() if is_open else (base_cross,)))

    to_three = sent(below, length, -5, at(group, mid, 3 * group))
    from_low = sent(above, length, 1, at(group, 3 * group))
    from_high = sent(below, length, -7, at(group, 3 * group))
    to_five = sent(below, length, -3, at(group, mid, 3 * group))
    to_seven = sent(below, length, -1, at(group, mid, 3 * group))
    end = end if is_open else above
    end_three, end_five, end_seven = (sent(end, length, by, at(3 * group)) for by in (3, 5, 7))
    state = pl.pallas_call(
        functools.partial(choose_kernel, length, is_open),
        out_shape=rows_of(state_rows),
        in_specs=[anywhere] * 8,
        out_specs=anywhere,
        scratch_shapes=[room(state_rows - ps), pltpu.SemaphoreType.DMA],
        compiler_params=params,
        name="choose",
    )(from_low, from_high, to_three, to_five, to_seven, end_three, end_five, end_seven)
    state_next = sent(state, length, 1, inner(1, 3, 5))

    def lower(kernel, name, inputs, nodes):
        count = len(inputs)
        return pl.pallas_call(
            functools.partial(kernel, length),
            out_shape=(whole, whole),
            in_specs=[anywhere] * (count + 2),
            out_specs=[anywhere] * 2,
            scratch_shapes=[room(state_rows)]
            + [room(node_rows)] * nodes
            + [pltpu.VMEM(square, f32)] * 5
            + [pltpu.SemaphoreType.DMA],
            input_output_aliases={count: 0, count + 1: 1},
            compiler_params=params,
            name=name,
        )(*inputs, diag, cross)

    diag, cross = lower(odd_kernel, "odd", (state, node, four_seven, four_five, four_one, near, nearer), 3)
    diag, cross = lower(even_kernel, "even", (state_next, node, four_six, four_two), 2)
    return diag, cross


def solution(mesh):
    placed = (P(axis, None, None),) * 3
    return jax.shard_map(
        body, mesh=mesh, in_specs=placed, out_specs=placed[:2], check_vma=False
    )
```

```python
import functools

import jax
import jax.numpy as jnp
from jax import lax
from jax.experimental import pallas as pl
from jax.experimental.pallas import tpu as pltpu
from jax.sharding import PartitionSpec as P

row_offset = 3
lanes = 128
group = 8
axis = "tm"
bf16 = jnp.bfloat16
f32 = jnp.float32


def sym_rows(width):
    blocks = width // lanes
    pairs = blocks // 2
    return (blocks * (blocks - 1) // 2 + blocks - pairs) * lanes + 8 * pairs


def full_rows(width):
    return width * (width // lanes)


def tri():
    r = lax.broadcasted_iota(jnp.int32, (lanes, lanes), 0)
    c = lax.broadcasted_iota(jnp.int32, (lanes, lanes), 1)
    return r, c


def put_sym(ref, at, mat):
    blocks = mat.shape[0] // lanes
    block = lambda i, j: mat[i * lanes : (i + 1) * lanes, j * lanes : (j + 1) * lanes]
    for i in range(blocks):
        for j in range(i):
            ref[pl.ds(at, lanes), :] = block(i, j)
            at += lanes
    r, c = tri()
    for i in range(0, blocks - 1, 2):
        one, two = block(i, i), block(i + 1, i + 1)
        ref[pl.ds(at, lanes), :] = jnp.where(r >= c, one, two)
        at += lanes
        line = jnp.sum(jnp.where(r == c, two, 0.0), axis=0, keepdims=True)
        ref[pl.ds(at, 8), :] = jnp.broadcast_to(line, (8, lanes))
        at += 8
    if blocks % 2:
        ref[pl.ds(at, lanes), :] = block(blocks - 1, blocks - 1)


def get_sym(ref, at, width):
    blocks = width // lanes
    got = {}
    for i in range(blocks):
        for j in range(i):
            got[i, j] = ref[pl.ds(at, lanes), :]
            got[j, i] = got[i, j].T
            at += lanes
    r, c = tri()
    for i in range(0, blocks - 1, 2):
        both = ref[pl.ds(at, lanes), :]
        turned = both.T
        at += lanes
        line = ref[pl.ds(at, 8), :][0:1, :]
        at += 8
        got[i, i] = jnp.where(r >= c, both, turned)
        got[i + 1, i + 1] = jnp.where(r == c, line, jnp.where(r < c, both, turned))
    if blocks % 2:
        got[blocks - 1, blocks - 1] = ref[pl.ds(at, lanes), :]
    return jnp.concatenate(
        [jnp.concatenate([got[i, j] for j in range(blocks)], axis=1) for i in range(blocks)], axis=0
    )


def put_full(ref, at, mat):
    width = mat.shape[0]
    for j in range(width // lanes):
        ref[pl.ds(at + j * width, width), :] = mat[:, j * lanes : (j + 1) * lanes]


def get_full(ref, at, width):
    return jnp.concatenate(
        [ref[pl.ds(at + j * width, width), :] for j in range(width // lanes)], axis=1
    )


def parts_of(mat):
    high = mat.astype(bf16)
    return high, (mat - high.astype(f32)).astype(bf16)


def times(left, right, turned=False):
    dims = (((1,), (1 if turned else 0,)), ((), ()))
    dot = lambda a, b: lax.dot_general(a, b, dims, preferred_element_type=f32)
    return dot(left[0], right[0]) + (dot(left[0], right[1]) + dot(left[1], right[0]))


def place_now(length):
    return lax.rem(lax.axis_index(axis) + row_offset, length)


def fetch(sems, *pairs):
    copies = [pltpu.make_async_copy(source, target, sems.at[i]) for i, (source, target) in enumerate(pairs)]
    for copy in copies:
        copy.start()
    for copy in copies:
        copy.wait()


def own_kernel(inv_ref, low_ref, up_ref, sym_ref, part_ref, node_ref, rooms, sems):
    width = inv_ref.shape[1]
    fetch(sems, *((ref.at[0], rooms.at[i]) for i, ref in enumerate((inv_ref, low_ref, up_ref))))
    inverse = rooms[0]
    inv_parts = parts_of(inverse)
    ps, pf = sym_rows(width), full_rows(width)
    put_sym(sym_ref, 0, inverse)
    part_ref[pl.ds(0, ps), :] = sym_ref[...]
    put_full(part_ref, ps, times(inv_parts, parts_of(rooms[1])))
    node_ref[pl.ds(0, ps + pf), :] = part_ref[...]
    put_full(node_ref, ps + pf, times(inv_parts, parts_of(rooms[2])))


def get_node(ref, width):
    ps, pf = sym_rows(width), full_rows(width)
    return get_sym(ref, 0, width), get_full(ref, ps, width), get_full(ref, ps + pf, width)


def put_state(ref, aa, ba, bb):
    ps = sym_rows(aa.shape[0])
    put_sym(ref, 0, aa)
    put_sym(ref, ps, bb)
    put_full(ref, 2 * ps, ba)


def roles_of(length):
    place = place_now(length)
    return place == 0, place == group, place == 2 * group, place == 3 * group


def ahead_kernel(length, node, came_part, came_root, out, sym_ref):
    width = out.shape[1]
    ps = sym_rows(width)
    _, at_low, at_mid, _ = roles_of(length)

    @pl.when(at_low)
    def _():
        own_d, own_g, own_h = get_node(node, width)
        h_parts = parts_of(own_h)
        out[0] = times(h_parts, parts_of(get_full(came_part, ps, width))) - own_g
        passed = times(h_parts, parts_of(get_sym(came_part, 0, width)))
        out[1] = own_d + times(parts_of(passed), h_parts, True)

    @pl.when(at_mid)
    def _():
        own_d, own_g, _ = get_node(node, width)
        own_parts = parts_of(own_g)
        cross = -times(own_parts, parts_of(get_sym(came_root, 0, width)))
        own = own_d - times(own_parts, parts_of(cross), True)
        put_sym(sym_ref, 0, own)
        out[0] = cross
        out[1] = own


def halve(four, state, low_ref, high_ref):
    aa, ba, bb = state
    width = aa.shape[0]
    diag, g_mat, h_mat = get_node(four, width)
    g_parts, h_parts = parts_of(g_mat), parts_of(h_mat)
    ba_parts = parts_of(ba)
    low = -(times(g_parts, parts_of(aa)) + times(h_parts, ba_parts))
    put_full(low_ref, 2 * sym_rows(width), low)
    high = -(times(g_parts, ba_parts, True) + times(h_parts, parts_of(bb)))
    put_full(high_ref, 2 * sym_rows(width), high.T)
    own = diag - times(g_parts, parts_of(low), True) - times(h_parts, parts_of(high), True)
    ps = sym_rows(width)
    put_sym(low_ref, 0, aa)
    put_sym(low_ref, ps, own)
    high_ref[pl.ds(0, ps), :] = low_ref[pl.ds(ps, ps), :]
    put_sym(high_ref, ps, bb)


def upper_kernel(
    length, ahead, root_mid, root_low, mid_high, mid_zero, node, came_node, came_four,
    diag_ref, cross_ref, low_ref, high_ref, aa_ref, ba_ref, bb_ref,
):
    width = aa_ref.shape[0]
    at_zero, at_low, at_mid, at_high = roles_of(length)

    @pl.when(at_low)
    def _():
        root = get_sym(root_low, 0, width)
        passed = parts_of(ahead[0])
        cross = times(passed, parts_of(root))
        own = ahead[1] + times(parts_of(cross), passed, True)
        diag_ref[0], cross_ref[0] = own, cross
        aa_ref[...], ba_ref[...], bb_ref[...] = root, cross, own

    @pl.when(at_mid)
    def _():
        mid_cross, mid = ahead[0], ahead[1]
        diag_ref[0], cross_ref[0] = mid, mid_cross
        low_d, low_g, low_h = get_node(came_node, width)
        low_g, low_h = parts_of(low_g), parts_of(low_h)
        cross_parts = parts_of(mid_cross)
        part_low = -(times(low_g, parts_of(get_sym(root_mid, 0, width))) + times(low_h, cross_parts))
        part_high = -(times(low_g, cross_parts, True) + times(low_h, parts_of(mid)))
        own = low_d - times(low_g, parts_of(part_low), True) - times(low_h, parts_of(part_high), True)
        aa_ref[...], ba_ref[...], bb_ref[...] = own, part_high.T, mid

    def above(mid_ref, node_ref):
        own_d, own_g, _ = get_node(node_ref, width)
        mid = get_sym(mid_ref, 0, width)
        own_g = parts_of(own_g)
        cross = -times(own_g, parts_of(mid))
        return mid, cross, own_d - times(own_g, parts_of(cross), True)

    @pl.when(at_high)
    def _():
        mid, cross, own = above(mid_high, node)
        diag_ref[0], cross_ref[0] = own, cross
        aa_ref[...], ba_ref[...], bb_ref[...] = mid, cross, own

    @pl.when(at_zero)
    def _():
        _, _, own = above(mid_zero, came_node)
        zeros = jnp.zeros((width, width), f32)
        diag_ref[0], cross_ref[0] = get_sym(node, 0, width), zeros
        aa_ref[...], ba_ref[...], bb_ref[...] = own, zeros, zeros

    @pl.when(lax.rem(place_now(length), group) == 0)
    def _():
        halve(came_four, (aa_ref[...], ba_ref[...], bb_ref[...]), low_ref, high_ref)


def halve_kernel(came_four, aa_ref, ba_ref, bb_ref, low_ref, high_ref):
    halve(came_four, (aa_ref[...], ba_ref[...], bb_ref[...]), low_ref, high_ref)


def offset_of(length):
    return lax.rem(place_now(length), group)


def near_kernel(length, node, came_near, came_far, came_back, f_high, f_low, rest_ref):
    width = rest_ref.shape[0]
    turn = lax.rem(offset_of(length), group // 2)
    first, second = slice(0, width), slice(width, 2 * width)

    def put(rows, columns, mat):
        f_high[rows, columns], f_low[rows, columns] = parts_of(mat)

    def put_unit():
        r = lax.broadcasted_iota(jnp.int32, (width, 2 * width), 0)
        c = lax.broadcasted_iota(jnp.int32, (width, 2 * width), 1)
        f_high[second, :] = jnp.where(r == c, 1.0, 0.0).astype(bf16)
        f_low[second, :] = jnp.zeros((width, 2 * width), bf16)
        rest_ref[:, second] = jnp.zeros((width, width), f32)

    @pl.when(turn == 2)
    def _():
        d_own, g_own, h_own = get_node(node, width)
        put(first, first, -g_own)
        put(first, second, -h_own)
        rest_ref[:, first] = d_own
        put_unit()

    def odd(below, two):
        d_own, g_own, h_own = get_node(node, width)
        d_two, g_two, h_two = get_node(two, width)
        inward, outward = (h_own, g_own) if below else (g_own, h_own)
        inward = parts_of(inward)
        to_low, to_high = times(inward, parts_of(g_two)), times(inward, parts_of(h_two))
        put(first, first, to_low - outward if below else to_low)
        put(first, second, to_high if below else to_high - outward)
        link = -times(inward, parts_of(d_two))
        rest_ref[:, first] = d_own - times(inward, parts_of(link), True)
        if below:
            put_unit()
        else:
            put(second, first, -g_two)
            put(second, second, -h_two)
            rest_ref[:, second] = link

    @pl.when(turn == 1)
    def _():
        odd(True, came_near)

    offset = offset_of(length)
    for at, two in ((3, came_far), (7, came_back)):

        @pl.when(offset == at)
        def _(two=two):
            odd(False, two)


def choose_kernel(length, *refs):
    out_ref = refs[4]
    offset = offset_of(length)
    for at, ref in zip((1, 3, 5, 7), refs[:4]):

        @pl.when(offset == at)
        def _(ref=ref):
            out_ref[...] = ref[...]


def lower_kernel(length, parity, state, fh, fl, rest, _diag, _cross, diag_ref, cross_ref, out, sh, sl, sems):
    width = rest.shape[0]
    ps = sym_rows(width)
    offset = offset_of(length)
    first, second = slice(0, width), slice(width, 2 * width)

    def hand_over():
        fetch(sems, (out.at[:, first], diag_ref.at[0]), (out.at[:, second], cross_ref.at[0]))

    if parity == 0:

        @pl.when(offset == group // 2)
        def _():
            out[:, first] = get_sym(state, ps, width)
            out[:, second] = get_full(state, 2 * ps, width)
            hand_over()

    @pl.when(jnp.logical_and(lax.rem(offset, 2) == parity, lax.rem(offset, group // 2) > 0))
    def _():
        ba = get_full(state, 2 * ps, width)
        for rows, columns, mat in (
            (first, first, get_sym(state, 0, width)),
            (second, first, ba),
            (first, second, ba.T),
            (second, second, get_sym(state, ps, width)),
        ):
            sh[rows, columns], sl[rows, columns] = parts_of(mat)
        eh, el = fh[first, :], fl[first, :]
        triple = lambda h, l, axis_at: jnp.concatenate([h, l, h], axis=axis_at)
        left = jnp.concatenate([eh, eh, el], axis=1)
        passed = jnp.dot(left, triple(sh[...], sl[...], 0), preferred_element_type=f32)
        high, low = parts_of(passed)
        left = jnp.concatenate([high, high, low], axis=1)
        whole = lax.dot_general(
            left, triple(fh[...], fl[...], 1), (((1,), (1,)), ((), ())), preferred_element_type=f32
        )
        out[...] = rest[...] + whole
        hand_over()


def sent(array, length, *moves):
    device = lambda position: (position - row_offset) % length
    pairs = [(device(p), device(p + by)) for by, wanted in moves for p in range(length) if wanted(p)]
    return lax.ppermute(array, axis, pairs)


def upper_levels(inverse, lowers, uppers, length):
    width = inverse.shape[0]
    place = (lax.axis_index(axis) + row_offset) % length
    product = functools.partial(jnp.dot, precision=lax.Precision.HIGHEST, preferred_element_type=f32)
    node_g, node_h = product(inverse, lowers), product(inverse, uppers)
    everywhere = lambda p: True
    zeros = jnp.zeros((width, width), f32)
    sigma = jnp.where(place == 0, inverse, zeros)
    low_own, high_own, cross = zeros, zeros, zeros
    stride = length // 2
    while stride >= group:
        from_low, owned_high = (sent(x, length, (stride, everywhere)) for x in (sigma, high_own))
        from_high, owned_low = (sent(x, length, (-stride, everywhere)) for x in (sigma, low_own))
        has_upper = place + stride < length
        sigma_high = jnp.where(has_upper, from_high, zeros)
        sigma_ba = jnp.where(has_upper, owned_high.T + owned_low, zeros)
        active = place % (2 * stride) == stride
        low = -(product(node_g, from_low) + product(node_h, sigma_ba))
        high = -(product(node_g, sigma_ba.T) + product(node_h, sigma_high))
        own = inverse - product(node_g, low.T) - product(node_h, high.T)
        sigma = jnp.where(active, own, sigma)
        low_own = jnp.where(active, low, zeros)
        high_own = jnp.where(active, high, zeros)
        cross = jnp.where(active, low, cross)
        stride //= 2
    newest = lambda p: p % (2 * group) == group
    below_aa, below_ba, below_bb = (sent(x, length, (group, newest)) for x in (sigma, high_own.T, sigma_high))
    return sigma, cross, tuple(
        jnp.where(active, *pair) for pair in ((from_low, below_aa), (low_own, below_ba), (sigma, below_bb))
    )


def body(inv_diag, low_coupling, up_coupling):
    width = inv_diag.shape[1]
    length = lax.axis_size(axis)
    span = 4 * group
    is_open = length == span
    ps, pf = sym_rows(width), full_rows(width)
    node_rows, state_rows = ps + 2 * pf, 2 * ps + pf
    rows_of = lambda rows: jax.ShapeDtypeStruct((rows, lanes), f32)
    square = (width, width)
    whole = jax.ShapeDtypeStruct((1,) + square, f32)
    vmem, anywhere = pl.BlockSpec(memory_space=pltpu.VMEM), pl.BlockSpec(memory_space=pl.ANY)
    room = lambda *shape, kind=f32: pltpu.VMEM(shape, kind)
    sems = pltpu.SemaphoreType.DMA((4,))
    run = lambda kernel, mib, **more: pl.pallas_call(
        kernel, compiler_params=pltpu.CompilerParams(vmem_limit_bytes=mib * 2**20),
        cost_estimate=pl.CostEstimate(flops=1, bytes_accessed=1, transcendentals=0), **more
    )
    at = lambda turn: (lambda p: p % span == turn)
    inner = lambda offset: (lambda p: p % group == offset)
    mid, half = 2 * group, group // 2

    sym, part, node = run(
        own_kernel, 60, out_shape=(rows_of(ps), rows_of(ps + pf), rows_of(node_rows)),
        in_specs=[anywhere] * 3, out_specs=[vmem] * 3,
        scratch_shapes=[room(3, *square), sems], name="own",
    )(inv_diag, low_coupling, up_coupling)

    close = ((-1, inner(2)), (-1, inner(6)))
    if is_open:
        root_mid = sent(sym, length, (mid, at(0)))
        came_part = sent(part, length, (-group, at(mid)))
        root_low = sent(sym, length, (group, at(0)))
        came_near = sent(node, length, (group, at(group)), (group, at(3 * group)), *close)
    else:
        came_near = sent(node, length, *close)
    came_far = sent(node, length, (half, inner(half)), (1, inner(2)), (4, inner(6)))
    came_back = sent(came_far, length, (-3, inner(2)))

    if is_open:
        ahead, mid_sym = run(
            functools.partial(ahead_kernel, length), 16,
            out_shape=(jax.ShapeDtypeStruct((2,) + square, f32), rows_of(ps)),
            in_specs=[vmem] * 3, out_specs=[vmem] * 2, name="ahead",
        )(node, came_part, root_mid)
        mid_high = sent(mid_sym, length, (group, at(mid)))
        mid_zero = sent(mid_sym, length, (mid, at(mid)))
        diag, cross, low_half, high_half = run(
            functools.partial(upper_kernel, length), 16,
            out_shape=(whole, whole, rows_of(state_rows), rows_of(state_rows)),
            in_specs=[vmem] * 8, out_specs=[vmem] * 4,
            scratch_shapes=[room(*square)] * 3, name="upper",
        )(ahead, root_mid, root_low, mid_high, mid_zero, node, came_near, came_far)
    else:
        diag, cross, below = upper_levels(inv_diag[0], low_coupling[0], up_coupling[0], length)
        diag, cross = diag[None], cross[None]
        low_half, high_half = run(
            halve_kernel, 16, out_shape=(rows_of(state_rows),) * 2,
            in_specs=[vmem] * 4, out_specs=[vmem] * 2, name="halve",
        )(came_far, *below)

    to_five = sent(high_half, length, (-3, inner(0)))
    to_three = sent(low_half, length, (-5, inner(0)))
    to_one = sent(low_half, length, (-7, inner(0)))
    to_seven = sent(high_half, length, (-1, inner(0)))

    f_high, f_low, rest = run(
        functools.partial(near_kernel, length), 16,
        out_shape=(jax.ShapeDtypeStruct((2 * width, 2 * width), bf16),) * 2
        + (jax.ShapeDtypeStruct((width, 2 * width), f32),),
        in_specs=[vmem] * 4, out_specs=[vmem] * 3, name="near",
    )(node, came_near, came_far, came_back)

    state = run(
        functools.partial(choose_kernel, length), 16,
        out_shape=rows_of(state_rows), in_specs=[vmem] * 4, out_specs=vmem, name="choose",
    )(to_one, to_three, to_five, to_seven)
    state_next = sent(state, length, (1, inner(1)), (1, inner(3)), (1, inner(5)))

    for parity, came in ((1, state), (0, state_next)):
        diag, cross = run(
            functools.partial(lower_kernel, length, parity), 20,
            out_shape=(whole, whole), in_specs=[vmem] * 4 + [anywhere] * 2, out_specs=[anywhere] * 2,
            scratch_shapes=[room(width, 2 * width)]
            + [room(2 * width, 2 * width, kind=bf16)] * 2
            + [sems],
            input_output_aliases={4: 0, 5: 1},
            name="lower",
        )(came, f_high, f_low, rest, diag, cross)
    return diag, cross


def solution(mesh):
    placed = (P(axis, None, None),) * 3
    return jax.shard_map(
        body, mesh=mesh, in_specs=placed, out_specs=placed[:2], check_vma=False
    )
```

```python
import functools

import jax
import jax.numpy as jnp
from jax import lax
from jax.experimental import pallas as pl
from jax.experimental.pallas import tpu as pltpu
from jax.sharding import PartitionSpec as P

row_offset = 3
lanes = 128
group = 8
axis = "tm"
bf16 = jnp.bfloat16
f32 = jnp.float32


def sym_rows(width):
    blocks = width // lanes
    pairs = blocks // 2
    return (blocks * (blocks - 1) // 2 + blocks - pairs) * lanes + 8 * pairs


def full_rows(width):
    return width * (width // lanes)


def tri():
    r = lax.broadcasted_iota(jnp.int32, (lanes, lanes), 0)
    c = lax.broadcasted_iota(jnp.int32, (lanes, lanes), 1)
    return r, c


def put_sym(ref, at, mat):
    blocks = mat.shape[0] // lanes
    block = lambda i, j: mat[i * lanes : (i + 1) * lanes, j * lanes : (j + 1) * lanes]
    for i in range(blocks):
        for j in range(i):
            ref[pl.ds(at, lanes), :] = block(i, j)
            at += lanes
    r, c = tri()
    for i in range(0, blocks - 1, 2):
        one, two = block(i, i), block(i + 1, i + 1)
        ref[pl.ds(at, lanes), :] = jnp.where(r >= c, one, two)
        at += lanes
        line = jnp.sum(jnp.where(r == c, two, 0.0), axis=0, keepdims=True)
        ref[pl.ds(at, 8), :] = jnp.broadcast_to(line, (8, lanes))
        at += 8
    if blocks % 2:
        ref[pl.ds(at, lanes), :] = block(blocks - 1, blocks - 1)


def get_sym(ref, at, width):
    blocks = width // lanes
    got = {}
    for i in range(blocks):
        for j in range(i):
            got[i, j] = ref[pl.ds(at, lanes), :]
            got[j, i] = got[i, j].T
            at += lanes
    r, c = tri()
    for i in range(0, blocks - 1, 2):
        both = ref[pl.ds(at, lanes), :]
        turned = both.T
        at += lanes
        line = ref[pl.ds(at, 8), :][0:1, :]
        at += 8
        got[i, i] = jnp.where(r >= c, both, turned)
        got[i + 1, i + 1] = jnp.where(r == c, line, jnp.where(r < c, both, turned))
    if blocks % 2:
        got[blocks - 1, blocks - 1] = ref[pl.ds(at, lanes), :]
    return jnp.concatenate(
        [jnp.concatenate([got[i, j] for j in range(blocks)], axis=1) for i in range(blocks)], axis=0
    )


def put_full(ref, at, mat):
    width = mat.shape[0]
    for j in range(width // lanes):
        ref[pl.ds(at + j * width, width), :] = mat[:, j * lanes : (j + 1) * lanes]


def get_full(ref, at, width):
    return jnp.concatenate(
        [ref[pl.ds(at + j * width, width), :] for j in range(width // lanes)], axis=1
    )


def parts_of(mat):
    high = mat.astype(bf16)
    return high, (mat - high.astype(f32)).astype(bf16)


def times(left, right, turned=False):
    dims = (((1,), (1 if turned else 0,)), ((), ()))
    dot = lambda a, b: lax.dot_general(a, b, dims, preferred_element_type=f32)
    return dot(left[0], right[0]) + (dot(left[0], right[1]) + dot(left[1], right[0]))


def long_left(parts):
    high, low = parts
    return jnp.concatenate([high, high, low], axis=1)


def long_right(parts, turned=False):
    high, low = parts
    return jnp.concatenate([high, low, high], axis=1 if turned else 0)


def long_times(left, right, turned=False):
    dims = (((1,), (1 if turned else 0,)), ((), ()))
    return lax.dot_general(left, right, dims, preferred_element_type=f32)


def symmetric_times(left, right):
    width = left.shape[0]
    most = width // (2 * lanes) * (2 * lanes)
    wide = long_times(left, right[:most], True)
    if most == width:
        return wide
    rest = long_times(left[most:], right[most:], True)
    return jnp.concatenate([wide, jnp.concatenate([wide[most:].T, rest], axis=0)], axis=1)


def set_state(sh, sl, aa, ba, bb):
    width = aa.shape[0]
    first, second = slice(0, width), slice(width, 2 * width)
    for rows, columns, mat in ((first, first, aa), (second, first, ba), (first, second, ba.T), (second, second, bb)):
        sh[rows, columns], sl[rows, columns] = parts_of(mat)


def eliminate(node, sh, sl):
    diag, g_mat, h_mat = node
    left = long_left(parts_of(jnp.concatenate([g_mat, h_mat], axis=1)))
    passed = -long_times(left, long_right((sh[...], sl[...])))
    return passed, diag - symmetric_times(left, long_right(parts_of(passed), True))


def place_now(length):
    return lax.rem(lax.axis_index(axis) + row_offset, length)


def fetch(sems, *pairs):
    copies = [pltpu.make_async_copy(source, target, sems.at[i]) for i, (source, target) in enumerate(pairs)]
    for copy in copies:
        copy.start()
    for copy in copies:
        copy.wait()


def own_kernel(inv_ref, low_ref, up_ref, sym_ref, part_ref, node_ref, rooms, sems):
    width = inv_ref.shape[1]
    fetch(sems, *((ref.at[0], rooms.at[i]) for i, ref in enumerate((inv_ref, low_ref, up_ref))))
    inverse = rooms[0]
    inv_parts = parts_of(inverse)
    ps, pf = sym_rows(width), full_rows(width)
    put_sym(sym_ref, 0, inverse)
    part_ref[pl.ds(0, ps), :] = sym_ref[...]
    put_full(part_ref, ps, times(inv_parts, parts_of(rooms[1])))
    node_ref[pl.ds(0, ps + pf), :] = part_ref[...]
    put_full(node_ref, ps + pf, times(inv_parts, parts_of(rooms[2])))


def get_node(ref, width):
    ps, pf = sym_rows(width), full_rows(width)
    return get_sym(ref, 0, width), get_full(ref, ps, width), get_full(ref, ps + pf, width)


def put_state(ref, aa, ba, bb):
    ps = sym_rows(aa.shape[0])
    put_sym(ref, 0, aa)
    put_sym(ref, ps, bb)
    put_full(ref, 2 * ps, ba)


def roles_of(length):
    place = place_now(length)
    return place == 0, place == group, place == 2 * group, place == 3 * group


def mid_kernel(length, part, came_root, out, sym_ref):
    width = out.shape[1]
    ps = sym_rows(width)
    _, _, at_mid, _ = roles_of(length)

    @pl.when(jnp.logical_not(at_mid))
    def _():
        sym_ref[...] = part[pl.ds(0, ps), :]

    @pl.when(at_mid)
    def _():
        own_parts = parts_of(get_full(part, ps, width))
        cross = -times(own_parts, parts_of(get_sym(came_root, 0, width)))
        own = get_sym(part, 0, width) - times(own_parts, parts_of(cross), True)
        put_sym(sym_ref, 0, own)
        out[0] = cross
        out[1] = own


def low_kernel(length, node, came_part, _after, out):
    width = out.shape[1]
    ps = sym_rows(width)
    _, at_low, _, _ = roles_of(length)

    @pl.when(at_low)
    def _():
        own_d, own_g, own_h = get_node(node, width)
        h_parts = parts_of(own_h)
        out[0] = times(h_parts, parts_of(get_full(came_part, ps, width))) - own_g
        passed = times(h_parts, parts_of(get_sym(came_part, 0, width)))
        out[1] = own_d + times(parts_of(passed), h_parts, True)


def halve(four, sh, sl, low_ref, low_cross_ref, high_ref):
    width = sh.shape[0] // 2
    ps = sym_rows(width)
    passed, own = eliminate(get_node(four, width), sh, sl)
    put_full(low_cross_ref, 0, passed[:, :width])
    put_full(high_ref, 2 * ps, passed[:, width:].T)
    put_sym(low_ref, ps, own)
    high_ref[pl.ds(0, ps), :] = low_ref[pl.ds(ps, ps), :]


def upper_kernel(
    length, at_m, at_l, root_mid, came_sym, mid_zero, node, came_node, came_four,
    diag_ref, cross_ref, low_ref, low_cross_ref, high_ref, sh, sl,
):
    width = diag_ref.shape[1]
    ps = sym_rows(width)
    at_zero, at_low, at_mid, at_high = roles_of(length)
    low_end, high_end = pl.ds(0, ps), pl.ds(ps, ps)

    @pl.when(at_low)
    def _():
        root = get_sym(came_sym, 0, width)
        passed = parts_of(at_l[0])
        cross = times(passed, parts_of(root))
        own = at_l[1] + symmetric_times(long_left(parts_of(cross)), long_right(passed, True))
        diag_ref[0], cross_ref[0] = own, cross
        low_ref[low_end, :] = came_sym[...]
        put_sym(high_ref, ps, own)
        set_state(sh, sl, root, cross, own)

    @pl.when(at_mid)
    def _():
        mid_cross, mid = at_m[0], at_m[1]
        diag_ref[0], cross_ref[0] = mid, mid_cross
        set_state(sh, sl, get_sym(root_mid, 0, width), mid_cross, mid)
        passed, own = eliminate(get_node(came_node, width), sh, sl)
        put_sym(low_ref, 0, own)
        put_sym(high_ref, ps, mid)
        set_state(sh, sl, own, passed[:, width:].T, mid)

    def above(mid_ref, node_ref):
        own_d, own_g, _ = get_node(node_ref, width)
        mid = get_sym(mid_ref, 0, width)
        own_g = parts_of(own_g)
        cross = -times(own_g, parts_of(mid))
        return mid, cross, own_d - times(own_g, parts_of(cross), True)

    @pl.when(at_high)
    def _():
        mid, cross, own = above(came_sym, node)
        diag_ref[0], cross_ref[0] = own, cross
        low_ref[low_end, :] = came_sym[...]
        put_sym(high_ref, ps, own)
        set_state(sh, sl, mid, cross, own)

    @pl.when(at_zero)
    def _():
        _, _, own = above(mid_zero, came_node)
        zeros = jnp.zeros((width, width), f32)
        diag_ref[0], cross_ref[0] = get_sym(node, 0, width), zeros
        put_sym(low_ref, 0, own)
        high_ref[high_end, :] = jnp.zeros((ps, lanes), f32)
        set_state(sh, sl, own, zeros, zeros)

    @pl.when(lax.rem(place_now(length), group) == 0)
    def _():
        halve(came_four, sh, sl, low_ref, low_cross_ref, high_ref)


def halve_kernel(came_four, aa_ref, ba_ref, bb_ref, low_ref, low_cross_ref, high_ref, sh, sl):
    aa, bb = aa_ref[...], bb_ref[...]
    put_sym(low_ref, 0, aa)
    put_sym(high_ref, sym_rows(aa.shape[0]), bb)
    set_state(sh, sl, aa, ba_ref[...], bb)
    halve(came_four, sh, sl, low_ref, low_cross_ref, high_ref)


def offset_of(length):
    return lax.rem(place_now(length), group)


def near_kernel(length, node, came_near, came_far, came_back, f_high, f_low, rest_ref):
    width = rest_ref.shape[0]
    turn = lax.rem(offset_of(length), group // 2)
    first, second = slice(0, width), slice(width, 2 * width)

    def put(rows, columns, mat):
        f_high[rows, columns], f_low[rows, columns] = parts_of(mat)

    @pl.when(turn == 2)
    def _():
        d_own, g_own, h_own = get_node(node, width)
        put(first, first, -g_own)
        put(first, second, -h_own)
        rest_ref[:, first] = d_own

    def odd(below, two):
        d_own, g_own, h_own = get_node(node, width)
        d_two, g_two, h_two = get_node(two, width)
        inward, outward = (h_own, g_own) if below else (g_own, h_own)
        inward = parts_of(inward)
        to_low, to_high = times(inward, parts_of(g_two)), times(inward, parts_of(h_two))
        put(first, first, to_low - outward if below else to_low)
        put(first, second, to_high if below else to_high - outward)
        link = -times(inward, parts_of(d_two))
        rest_ref[:, first] = d_own - times(inward, parts_of(link), True)
        if not below:
            put(second, first, -g_two)
            put(second, second, -h_two)
            rest_ref[:, second] = link

    @pl.when(turn == 1)
    def _():
        odd(True, came_near)

    offset = offset_of(length)
    for at, two in ((3, came_far), (7, came_back)):

        @pl.when(offset == at)
        def _(two=two):
            odd(False, two)


def choose_kernel(length, one, one_cross, three, three_cross, five, seven, _after, out_ref):
    offset = offset_of(length)
    for at, ends, cross in ((1, one, one_cross), (3, three, three_cross)):

        @pl.when(offset == at)
        def _(ends=ends, cross=cross):
            rows = ends.shape[0]
            out_ref[pl.ds(0, rows), :] = ends[...]
            out_ref[pl.ds(rows, cross.shape[0]), :] = cross[...]

    for at, ref in ((5, five), (7, seven)):

        @pl.when(offset == at)
        def _(ref=ref):
            out_ref[...] = ref[...]


def lower_kernel(length, parity, state, fh, fl, rest, _diag, _cross, diag_ref, cross_ref, diag_out, cross_out, sh, sl, sems):
    width = rest.shape[0]
    ps = sym_rows(width)
    offset = offset_of(length)
    turn = lax.rem(offset, group // 2)
    first, second = slice(0, width), slice(width, 2 * width)
    diag_copy = pltpu.make_async_copy(diag_out, diag_ref.at[0], sems.at[0])
    cross_copy = pltpu.make_async_copy(cross_out, cross_ref.at[0], sems.at[1])

    def passed_on():
        set_state(sh, sl, get_sym(state, 0, width), get_full(state, 2 * ps, width), get_sym(state, ps, width))
        left = long_left((fh[first, :], fl[first, :]))
        return long_times(left, long_right((sh[...], sl[...])))

    if parity == 0:

        @pl.when(offset == group // 2)
        def _():
            cross_out[...] = get_full(state, 2 * ps, width)
            cross_copy.start()
            diag_out[...] = get_sym(state, ps, width)
            diag_copy.start()
            diag_copy.wait()
            cross_copy.wait()

    @pl.when(turn == (1 if parity else 2))
    def _():
        passed = passed_on()
        cross_out[...] = passed[:, first]
        cross_copy.start()
        right = long_right((fh[first, :], fl[first, :]), True)
        diag_out[...] = rest[:, first] + symmetric_times(long_left(parts_of(passed)), right)
        diag_copy.start()
        diag_copy.wait()
        cross_copy.wait()

    if parity == 1:

        @pl.when(turn == 3)
        def _():
            left = long_left(parts_of(passed_on()))
            whole = long_times(left, long_right((fh[...], fl[...]), True), True) + rest[...]
            diag_out[...], cross_out[...] = whole[:, first], whole[:, second]
            diag_copy.start()
            cross_copy.start()
            diag_copy.wait()
            cross_copy.wait()


def sent(array, length, *moves):
    device = lambda position: (position - row_offset) % length
    pairs = [(device(p), device(p + by)) for by, wanted in moves for p in range(length) if wanted(p)]
    return lax.ppermute(array, axis, pairs)


def upper_levels(inverse, lowers, uppers, length):
    width = inverse.shape[0]
    place = (lax.axis_index(axis) + row_offset) % length
    product = functools.partial(jnp.dot, precision=lax.Precision.HIGHEST, preferred_element_type=f32)
    node_g, node_h = product(inverse, lowers), product(inverse, uppers)
    everywhere = lambda p: True
    zeros = jnp.zeros((width, width), f32)
    sigma = jnp.where(place == 0, inverse, zeros)
    low_own, high_own, cross = zeros, zeros, zeros
    stride = length // 2
    while stride >= group:
        from_low, owned_high = (sent(x, length, (stride, everywhere)) for x in (sigma, high_own))
        from_high, owned_low = (sent(x, length, (-stride, everywhere)) for x in (sigma, low_own))
        has_upper = place + stride < length
        sigma_high = jnp.where(has_upper, from_high, zeros)
        sigma_ba = jnp.where(has_upper, owned_high.T + owned_low, zeros)
        active = place % (2 * stride) == stride
        low = -(product(node_g, from_low) + product(node_h, sigma_ba))
        high = -(product(node_g, sigma_ba.T) + product(node_h, sigma_high))
        own = inverse - product(node_g, low.T) - product(node_h, high.T)
        sigma = jnp.where(active, own, sigma)
        low_own = jnp.where(active, low, zeros)
        high_own = jnp.where(active, high, zeros)
        cross = jnp.where(active, low, cross)
        stride //= 2
    newest = lambda p: p % (2 * group) == group
    below_aa, below_ba, below_bb = (sent(x, length, (group, newest)) for x in (sigma, high_own.T, sigma_high))
    return sigma, cross, tuple(
        jnp.where(active, *pair) for pair in ((from_low, below_aa), (low_own, below_ba), (sigma, below_bb))
    )


def body(inv_diag, low_coupling, up_coupling):
    width = inv_diag.shape[1]
    length = lax.axis_size(axis)
    span = 4 * group
    is_open = length == span
    ps, pf = sym_rows(width), full_rows(width)
    node_rows, state_rows = ps + 2 * pf, 2 * ps + pf
    rows_of = lambda rows: jax.ShapeDtypeStruct((rows, lanes), f32)
    square = (width, width)
    whole = jax.ShapeDtypeStruct((1,) + square, f32)
    vmem, anywhere = pl.BlockSpec(memory_space=pltpu.VMEM), pl.BlockSpec(memory_space=pl.ANY)
    room = lambda *shape, kind=f32: pltpu.VMEM(shape, kind)
    sems = pltpu.SemaphoreType.DMA((4,))
    run = lambda kernel, mib, **more: pl.pallas_call(
        kernel, compiler_params=pltpu.CompilerParams(vmem_limit_bytes=mib * 2**20),
        cost_estimate=pl.CostEstimate(flops=1, bytes_accessed=1, transcendentals=0), **more
    )
    at = lambda turn: (lambda p: p % span == turn)
    inner = lambda offset: (lambda p: p % group == offset)
    mid, half = 2 * group, group // 2

    sym, part, node = run(
        own_kernel, 60, out_shape=(rows_of(ps), rows_of(ps + pf), rows_of(node_rows)),
        in_specs=[anywhere] * 3, out_specs=[vmem] * 3,
        scratch_shapes=[room(3, *square), sems], name="own",
    )(inv_diag, low_coupling, up_coupling)

    close = ((-1, inner(2)), (-1, inner(6)))
    came_far = sent(node, length, (half, inner(half)), (1, inner(2)), (4, inner(6)))
    if is_open:
        came_near = sent(node, length, (group, at(group)), (group, at(3 * group)), *close)
        came_part = sent(part, length, (-group, at(mid)))
        root_mid = sent(sym, length, (mid, at(0)))
    else:
        came_near = sent(node, length, *close)

    state_room = [room(2 * width, 2 * width, kind=bf16)] * 2
    two = jax.ShapeDtypeStruct((2,) + square, f32)
    if is_open:
        at_m, mid_sym = run(
            functools.partial(mid_kernel, length), 16, out_shape=(two, rows_of(ps)),
            in_specs=[vmem] * 2, out_specs=[vmem] * 2, name="middle",
        )(part, root_mid)
        came_sym = sent(mid_sym, length, (group, at(mid)), (group, at(0)))
        mid_zero = sent(mid_sym, length, (mid, at(mid)))
        at_l = run(
            functools.partial(low_kernel, length), 16, out_shape=two,
            in_specs=[vmem] * 2 + [anywhere], out_specs=vmem, name="low",
        )(node, came_part, mid_sym)
        later, *_ = lax.optimization_barrier((came_far, at_l, came_sym, mid_zero))
        diag, cross, low_half, low_cross, high_half = run(
            functools.partial(upper_kernel, length), 16,
            out_shape=(whole, whole, rows_of(2 * ps), rows_of(pf), rows_of(state_rows)),
            in_specs=[vmem] * 8, out_specs=[vmem] * 5, scratch_shapes=state_room, name="upper",
        )(at_m, at_l, root_mid, came_sym, mid_zero, node, came_near, came_far)
    else:
        diag, cross, below = upper_levels(inv_diag[0], low_coupling[0], up_coupling[0], length)
        diag, cross = diag[None], cross[None]
        later = came_far
        low_half, low_cross, high_half = run(
            halve_kernel, 16, out_shape=(rows_of(2 * ps), rows_of(pf), rows_of(state_rows)),
            in_specs=[vmem] * 4, out_specs=[vmem] * 3, scratch_shapes=state_room, name="halve",
        )(came_far, *below)

    came_back = sent(later, length, (-3, inner(2)))
    three_cross = sent(low_cross, length, (-5, inner(0)))
    to_five = sent(high_half, length, (-3, inner(0)))
    to_one = sent(low_half, length, (-7, inner(0)))
    to_three = sent(low_half, length, (-5, inner(0)))
    to_seven = sent(high_half, length, (-1, inner(0)))
    one_cross = sent(three_cross, length, (-2, inner(3)))

    f_high, f_low, rest = run(
        functools.partial(near_kernel, length), 16,
        out_shape=(jax.ShapeDtypeStruct((2 * width, 2 * width), bf16),) * 2
        + (jax.ShapeDtypeStruct((width, 2 * width), f32),),
        in_specs=[vmem] * 4, out_specs=[vmem] * 3, name="near",
    )(node, came_near, came_far, came_back)

    state = run(
        functools.partial(choose_kernel, length), 16,
        out_shape=rows_of(state_rows), in_specs=[vmem] * 6 + [anywhere], out_specs=vmem, name="choose",
    )(to_one, one_cross, to_three, three_cross, to_five, to_seven, rest)
    state_next = sent(state, length, (1, inner(1)), (1, inner(3)), (1, inner(5)))

    for parity, came in ((1, state), (0, state_next)):
        diag, cross = run(
            functools.partial(lower_kernel, length, parity), 20,
            out_shape=(whole, whole), in_specs=[vmem] * 4 + [anywhere] * 2, out_specs=[anywhere] * 2,
            scratch_shapes=[room(*square)] * 2 + state_room + [sems],
            input_output_aliases={4: 0, 5: 1},
            name="lower",
        )(came, f_high, f_low, rest, diag, cross)
    return diag, cross


def solution(mesh):
    placed = (P(axis, None, None),) * 3
    return jax.shard_map(
        body, mesh=mesh, in_specs=placed, out_specs=placed[:2], check_vma=False
    )
```

```python
import functools

import jax
import jax.numpy as jnp
from jax import lax
from jax.experimental import pallas as pl
from jax.experimental.pallas import tpu as pltpu
from jax.sharding import PartitionSpec as P

row_offset = 3
lanes = 128
group = 8
axis = "tm"
bf16 = jnp.bfloat16
f32 = jnp.float32


def sym_rows(width):
    blocks = width // lanes
    pairs = blocks // 2
    return (blocks * (blocks - 1) // 2 + blocks - pairs) * lanes + 8 * pairs


def full_rows(width):
    return width * (width // lanes)


def tri():
    r = lax.broadcasted_iota(jnp.int32, (lanes, lanes), 0)
    c = lax.broadcasted_iota(jnp.int32, (lanes, lanes), 1)
    return r, c


def put_sym(ref, at, mat):
    blocks = mat.shape[0] // lanes
    block = lambda i, j: mat[i * lanes : (i + 1) * lanes, j * lanes : (j + 1) * lanes]
    for i in range(blocks):
        for j in range(i):
            ref[pl.ds(at, lanes), :] = block(i, j)
            at += lanes
    r, c = tri()
    for i in range(0, blocks - 1, 2):
        one, two = block(i, i), block(i + 1, i + 1)
        ref[pl.ds(at, lanes), :] = jnp.where(r >= c, one, two)
        at += lanes
        line = jnp.sum(jnp.where(r == c, two, 0.0), axis=0, keepdims=True)
        ref[pl.ds(at, 8), :] = jnp.broadcast_to(line, (8, lanes))
        at += 8
    if blocks % 2:
        ref[pl.ds(at, lanes), :] = block(blocks - 1, blocks - 1)


def get_sym(ref, at, width):
    blocks = width // lanes
    got = {}
    for i in range(blocks):
        for j in range(i):
            got[i, j] = ref[pl.ds(at, lanes), :]
            got[j, i] = got[i, j].T
            at += lanes
    r, c = tri()
    for i in range(0, blocks - 1, 2):
        both = ref[pl.ds(at, lanes), :]
        turned = both.T
        at += lanes
        line = ref[pl.ds(at, 8), :][0:1, :]
        at += 8
        got[i, i] = jnp.where(r >= c, both, turned)
        got[i + 1, i + 1] = jnp.where(r == c, line, jnp.where(r < c, both, turned))
    if blocks % 2:
        got[blocks - 1, blocks - 1] = ref[pl.ds(at, lanes), :]
    return jnp.concatenate(
        [jnp.concatenate([got[i, j] for j in range(blocks)], axis=1) for i in range(blocks)], axis=0
    )


def put_full(ref, at, mat):
    width = mat.shape[0]
    for j in range(width // lanes):
        ref[pl.ds(at + j * width, width), :] = mat[:, j * lanes : (j + 1) * lanes]


def get_full(ref, at, width):
    return jnp.concatenate(
        [ref[pl.ds(at + j * width, width), :] for j in range(width // lanes)], axis=1
    )


def parts_of(mat):
    high = mat.astype(bf16)
    return high, (mat - high.astype(f32)).astype(bf16)


def times(left, right, turned=False):
    dims = (((1,), (1 if turned else 0,)), ((), ()))
    dot = lambda a, b: lax.dot_general(a, b, dims, preferred_element_type=f32)
    return dot(left[0], right[0]) + (dot(left[0], right[1]) + dot(left[1], right[0]))


def long_left(parts):
    high, low = parts
    return jnp.concatenate([high, high, low], axis=1)


def long_right(parts, turned=False):
    high, low = parts
    return jnp.concatenate([high, low, high], axis=1 if turned else 0)


def long_times(left, right, turned=False):
    dims = (((1,), (1 if turned else 0,)), ((), ()))
    return lax.dot_general(left, right, dims, preferred_element_type=f32)


def symmetric_times(left, right):
    width = left.shape[0]
    most = width // (2 * lanes) * (2 * lanes)
    wide = long_times(left, right[:most], True)
    if most == width:
        return wide
    rest = long_times(left[most:], right[most:], True)
    return jnp.concatenate([wide, jnp.concatenate([wide[most:].T, rest], axis=0)], axis=1)


def set_state(sh, sl, aa, ba, bb):
    width = aa.shape[0]
    first, second = slice(0, width), slice(width, 2 * width)
    for rows, columns, mat in ((first, first, aa), (second, first, ba), (first, second, ba.T), (second, second, bb)):
        sh[rows, columns], sl[rows, columns] = parts_of(mat)


def eliminate(node, sh, sl):
    diag, g_mat, h_mat = node
    left = long_left(parts_of(jnp.concatenate([g_mat, h_mat], axis=1)))
    passed = -long_times(left, long_right((sh[...], sl[...])))
    return passed, diag - symmetric_times(left, long_right(parts_of(passed), True))


def place_now(length):
    return lax.rem(lax.axis_index(axis) + row_offset, length)


def fetch(sems, *pairs):
    copies = [pltpu.make_async_copy(source, target, sems.at[i]) for i, (source, target) in enumerate(pairs)]
    for copy in copies:
        copy.start()
    for copy in copies:
        copy.wait()


def own_kernel(inv_ref, low_ref, up_ref, sym_ref, part_ref, node_ref, rooms, lines, sems, out_sems):
    width = inv_ref.shape[1]
    ps, pf = sym_rows(width), full_rows(width)
    loads = [
        pltpu.make_async_copy(ref.at[0], rooms.at[i], sems.at[i]) for i, ref in enumerate((inv_ref, low_ref, up_ref))
    ]
    for load in loads:
        load.start()
    stores = []

    def store(at, rows, *refs):
        for ref in refs:
            where = pl.ds(at, rows)
            stores.append(pltpu.make_async_copy(lines.at[where, :], ref.at[where, :], out_sems.at[len(stores)]))
            stores[-1].start()

    loads[0].wait()
    inverse = rooms[0]
    put_sym(lines, 0, inverse)
    store(0, ps, sym_ref, part_ref, node_ref)
    inv_parts = parts_of(inverse)
    loads[1].wait()
    put_full(lines, ps, times(inv_parts, parts_of(rooms[1])))
    store(ps, pf, part_ref, node_ref)
    loads[2].wait()
    put_full(lines, ps + pf, times(inv_parts, parts_of(rooms[2])))
    store(ps + pf, pf, node_ref)
    for copy in stores:
        copy.wait()


def get_node(ref, width):
    ps, pf = sym_rows(width), full_rows(width)
    return get_sym(ref, 0, width), get_full(ref, ps, width), get_full(ref, ps + pf, width)


def put_state(ref, aa, ba, bb):
    ps = sym_rows(aa.shape[0])
    put_sym(ref, 0, aa)
    put_sym(ref, ps, bb)
    put_full(ref, 2 * ps, ba)


def roles_of(length):
    place = place_now(length)
    return place == 0, place == group, place == 2 * group, place == 3 * group


def mid_kernel(length, part, came_root, out, sym_ref):
    width = out.shape[1]
    ps = sym_rows(width)
    _, _, at_mid, _ = roles_of(length)

    @pl.when(jnp.logical_not(at_mid))
    def _():
        sym_ref[...] = part[pl.ds(0, ps), :]

    @pl.when(at_mid)
    def _():
        own_parts = parts_of(get_full(part, ps, width))
        cross = -times(own_parts, parts_of(get_sym(came_root, 0, width)))
        own = get_sym(part, 0, width) - times(own_parts, parts_of(cross), True)
        put_sym(sym_ref, 0, own)
        out[0] = cross
        out[1] = own


def low_kernel(length, node, came_part, _after, out):
    width = out.shape[1]
    ps = sym_rows(width)
    _, at_low, _, _ = roles_of(length)

    @pl.when(at_low)
    def _():
        own_d, own_g, own_h = get_node(node, width)
        h_parts = parts_of(own_h)
        out[0] = times(h_parts, parts_of(get_full(came_part, ps, width))) - own_g
        passed = times(h_parts, parts_of(get_sym(came_part, 0, width)))
        out[1] = own_d + times(parts_of(passed), h_parts, True)


def hand_over(rooms, sems, diag_ref, cross_ref, diag, cross):
    rooms[0], rooms[1] = diag, cross
    fetch(sems, (rooms.at[0], diag_ref.at[0]), (rooms.at[1], cross_ref.at[0]))


def first_kernel(length, at_m, root_mid, came_node, diag_ref, cross_ref, sh, sl, aa_ref, bb_ref, rooms, sems):
    width = rooms.shape[1]
    _, _, at_mid, _ = roles_of(length)

    @pl.when(at_mid)
    def _():
        mid_cross, mid = at_m[0], at_m[1]
        set_state(sh, sl, get_sym(root_mid, 0, width), mid_cross, mid)
        passed, own = eliminate(get_node(came_node, width), sh, sl)
        put_sym(aa_ref, 0, own)
        put_sym(bb_ref, 0, mid)
        set_state(sh, sl, own, passed[:, width:].T, mid)
        hand_over(rooms, sems, diag_ref, cross_ref, mid, mid_cross)


def second_kernel(
    length, at_l, came_sym, mid_zero, part, came_part, _diag, _cross, _sh, _sl, _aa, _bb,
    diag_ref, cross_ref, sh, sl, aa_ref, bb_ref, rooms, sems,
):
    width = rooms.shape[1]
    ps = sym_rows(width)
    at_zero, at_low, _, at_high = roles_of(length)

    @pl.when(at_low)
    def _():
        root = get_sym(came_sym, 0, width)
        passed = parts_of(at_l[0])
        cross = times(passed, parts_of(root))
        own = at_l[1] + symmetric_times(long_left(parts_of(cross)), long_right(passed, True))
        aa_ref[...] = came_sym[...]
        put_sym(bb_ref, 0, own)
        set_state(sh, sl, root, cross, own)
        hand_over(rooms, sems, diag_ref, cross_ref, own, cross)

    def above(mid_ref, node_ref):
        own_d, own_g = get_sym(node_ref, 0, width), parts_of(get_full(node_ref, ps, width))
        mid = get_sym(mid_ref, 0, width)
        cross = -times(own_g, parts_of(mid))
        return mid, cross, own_d - times(own_g, parts_of(cross), True)

    @pl.when(at_high)
    def _():
        mid, cross, own = above(came_sym, part)
        aa_ref[...] = came_sym[...]
        put_sym(bb_ref, 0, own)
        set_state(sh, sl, mid, cross, own)
        hand_over(rooms, sems, diag_ref, cross_ref, own, cross)

    @pl.when(at_zero)
    def _():
        _, _, own = above(mid_zero, came_part)
        zeros = jnp.zeros((width, width), f32)
        put_sym(aa_ref, 0, own)
        bb_ref[...] = jnp.zeros((ps, lanes), f32)
        set_state(sh, sl, own, zeros, zeros)
        hand_over(rooms, sems, diag_ref, cross_ref, get_sym(part, 0, width), zeros)


def state_kernel(aa_ref, ba_ref, bb_ref, sh, sl, aa_out, bb_out):
    aa, bb = aa_ref[...], bb_ref[...]
    put_sym(aa_out, 0, aa)
    put_sym(bb_out, 0, bb)
    set_state(sh, sl, aa, ba_ref[...], bb)


def halve_kernel(length, sh, sl, aa_ref, bb_ref, *refs):
    fours, (low_ref, low_cross_ref, high_ref) = refs[:-3], refs[-3:]
    width = sh.shape[0] // 2
    ps = sym_rows(width)
    place = place_now(length)

    def work(four):
        passed, own = eliminate(get_node(four, width), sh, sl)
        put_full(low_cross_ref, 0, passed[:, :width])
        put_full(high_ref, 2 * ps, passed[:, width:].T)
        low_ref[pl.ds(0, ps), :] = aa_ref[...]
        put_sym(low_ref, ps, own)
        high_ref[pl.ds(0, ps), :] = low_ref[pl.ds(ps, ps), :]
        high_ref[pl.ds(ps, ps), :] = bb_ref[...]

    served = lax.rem(place, group) == 0
    if len(fours) == 1:
        pl.when(served)(lambda: work(fours[0]))
    else:
        at_mid = place == 2 * group
        pl.when(at_mid)(lambda: work(fours[1]))
        pl.when(jnp.logical_and(served, jnp.logical_not(at_mid)))(lambda: work(fours[0]))


def offset_of(length):
    return lax.rem(place_now(length), group)


def near_kernel(length, late, node, *refs):
    f_high, f_low, rest_ref = refs[-3:]
    width = rest_ref.shape[0]
    offset = offset_of(length)
    turn = lax.rem(offset, group // 2)
    first, second = slice(0, width), slice(width, 2 * width)

    def put(rows, columns, mat):
        f_high[rows, columns], f_low[rows, columns] = parts_of(mat)

    def odd(below, two):
        d_own, g_own, h_own = get_node(node, width)
        d_two, g_two, h_two = get_node(two, width)
        inward, outward = (h_own, g_own) if below else (g_own, h_own)
        inward = parts_of(inward)
        to_low, to_high = times(inward, parts_of(g_two)), times(inward, parts_of(h_two))
        put(first, first, to_low - outward if below else to_low)
        put(first, second, to_high if below else to_high - outward)
        link = -times(inward, parts_of(d_two))
        rest_ref[:, first] = d_own - times(inward, parts_of(link), True)
        if not below:
            put(second, first, -g_two)
            put(second, second, -h_two)
            rest_ref[:, second] = link

    if late:
        pl.when(offset == group - 1)(lambda: odd(False, refs[0]))
        return
    came_near, came_far = refs[:2]
    pl.when(turn == 1)(lambda: odd(True, came_near))
    pl.when(offset == 3)(lambda: odd(False, came_far))

    @pl.when(turn == 2)
    def _():
        d_own, g_own, h_own = get_node(node, width)
        put(first, first, -g_own)
        put(first, second, -h_own)
        rest_ref[:, first] = d_own


def choose_kernel(length, one, one_cross, three, three_cross, five, seven, _after, out_ref):
    offset = offset_of(length)
    for at, ends, cross in ((1, one, one_cross), (3, three, three_cross)):

        @pl.when(offset == at)
        def _(ends=ends, cross=cross):
            rows = ends.shape[0]
            out_ref[pl.ds(0, rows), :] = ends[...]
            out_ref[pl.ds(rows, cross.shape[0]), :] = cross[...]

    for at, ref in ((5, five), (7, seven)):

        @pl.when(offset == at)
        def _(ref=ref):
            out_ref[...] = ref[...]


def lower_kernel(length, parity, state, fh, fl, rest, _diag, _cross, diag_ref, cross_ref, diag_out, cross_out, sh, sl, sems):
    width = rest.shape[0]
    ps = sym_rows(width)
    offset = offset_of(length)
    turn = lax.rem(offset, group // 2)
    first, second = slice(0, width), slice(width, 2 * width)
    diag_copy = pltpu.make_async_copy(diag_out, diag_ref.at[0], sems.at[0])
    cross_copy = pltpu.make_async_copy(cross_out, cross_ref.at[0], sems.at[1])

    def passed_on():
        set_state(sh, sl, get_sym(state, 0, width), get_full(state, 2 * ps, width), get_sym(state, ps, width))
        left = long_left((fh[first, :], fl[first, :]))
        return long_times(left, long_right((sh[...], sl[...])))

    if parity == 0:

        @pl.when(offset == group // 2)
        def _():
            cross_out[...] = get_full(state, 2 * ps, width)
            cross_copy.start()
            diag_out[...] = get_sym(state, ps, width)
            diag_copy.start()
            diag_copy.wait()
            cross_copy.wait()

    @pl.when(turn == (1 if parity else 2))
    def _():
        passed = passed_on()
        cross_out[...] = passed[:, first]
        cross_copy.start()
        right = long_right((fh[first, :], fl[first, :]), True)
        diag_out[...] = rest[:, first] + symmetric_times(long_left(parts_of(passed)), right)
        diag_copy.start()
        diag_copy.wait()
        cross_copy.wait()

    if parity == 1:

        @pl.when(turn == 3)
        def _():
            left = long_left(parts_of(passed_on()))
            whole = long_times(left, long_right((fh[...], fl[...]), True), True) + rest[...]
            diag_out[...], cross_out[...] = whole[:, first], whole[:, second]
            diag_copy.start()
            cross_copy.start()
            diag_copy.wait()
            cross_copy.wait()


def sent(array, length, *moves):
    device = lambda position: (position - row_offset) % length
    pairs = [(device(p), device(p + by)) for by, wanted in moves for p in range(length) if wanted(p)]
    return lax.ppermute(array, axis, pairs)


def upper_levels(inverse, lowers, uppers, length):
    width = inverse.shape[0]
    place = (lax.axis_index(axis) + row_offset) % length
    product = functools.partial(jnp.dot, precision=lax.Precision.HIGHEST, preferred_element_type=f32)
    node_g, node_h = product(inverse, lowers), product(inverse, uppers)
    everywhere = lambda p: True
    zeros = jnp.zeros((width, width), f32)
    sigma = jnp.where(place == 0, inverse, zeros)
    low_own, high_own, cross = zeros, zeros, zeros
    stride = length // 2
    while stride >= group:
        from_low, owned_high = (sent(x, length, (stride, everywhere)) for x in (sigma, high_own))
        from_high, owned_low = (sent(x, length, (-stride, everywhere)) for x in (sigma, low_own))
        has_upper = place + stride < length
        sigma_high = jnp.where(has_upper, from_high, zeros)
        sigma_ba = jnp.where(has_upper, owned_high.T + owned_low, zeros)
        active = place % (2 * stride) == stride
        low = -(product(node_g, from_low) + product(node_h, sigma_ba))
        high = -(product(node_g, sigma_ba.T) + product(node_h, sigma_high))
        own = inverse - product(node_g, low.T) - product(node_h, high.T)
        sigma = jnp.where(active, own, sigma)
        low_own = jnp.where(active, low, zeros)
        high_own = jnp.where(active, high, zeros)
        cross = jnp.where(active, low, cross)
        stride //= 2
    newest = lambda p: p % (2 * group) == group
    below_aa, below_ba, below_bb = (sent(x, length, (group, newest)) for x in (sigma, high_own.T, sigma_high))
    return sigma, cross, tuple(
        jnp.where(active, *pair) for pair in ((from_low, below_aa), (low_own, below_ba), (sigma, below_bb))
    )


def body(inv_diag, low_coupling, up_coupling):
    width = inv_diag.shape[1]
    length = lax.axis_size(axis)
    span = 4 * group
    is_open = length == span
    ps, pf = sym_rows(width), full_rows(width)
    node_rows, state_rows = ps + 2 * pf, 2 * ps + pf
    rows_of = lambda rows: jax.ShapeDtypeStruct((rows, lanes), f32)
    square = (width, width)
    whole = jax.ShapeDtypeStruct((1,) + square, f32)
    vmem, anywhere = pl.BlockSpec(memory_space=pltpu.VMEM), pl.BlockSpec(memory_space=pl.ANY)
    room = lambda *shape, kind=f32: pltpu.VMEM(shape, kind)
    sems = pltpu.SemaphoreType.DMA((4,))
    run = lambda kernel, mib, **more: pl.pallas_call(
        kernel, compiler_params=pltpu.CompilerParams(vmem_limit_bytes=mib * 2**20),
        cost_estimate=pl.CostEstimate(flops=1, bytes_accessed=1, transcendentals=0), **more
    )
    at = lambda turn: (lambda p: p % span == turn)
    inner = lambda offset: (lambda p: p % group == offset)
    mid, half = 2 * group, group // 2

    sym, part, node = run(
        own_kernel, 60, out_shape=(rows_of(ps), rows_of(ps + pf), rows_of(node_rows)),
        in_specs=[anywhere] * 3, out_specs=[anywhere] * 3,
        scratch_shapes=[room(3, *square), room(node_rows, lanes), sems, pltpu.SemaphoreType.DMA((6,))], name="own",
    )(inv_diag, low_coupling, up_coupling)

    close = ((-1, inner(2)), (-1, inner(6)))
    away = ((1, inner(2)), (group // 2, inner(6)))
    half_state = (jax.ShapeDtypeStruct((2 * width, 2 * width), bf16),) * 2 + (rows_of(ps),) * 2
    rooms = [room(2, *square), sems]
    if is_open:
        to_mid = lambda p: p == mid - half
        came_far = sent(
            node, length, (half, lambda p: inner(half)(p) and not to_mid(p)), (group, at(group)), *away
        )
        came_near = sent(node, length, (half, to_mid), *close)
        came_part = sent(part, length, (-group, at(mid)), (group, at(3 * group)))
        root_mid = sent(sym, length, (mid, at(0)))
        two = jax.ShapeDtypeStruct((2,) + square, f32)
        at_m, mid_sym = run(
            functools.partial(mid_kernel, length), 16, out_shape=(two, rows_of(ps)),
            in_specs=[vmem] * 2, out_specs=[vmem] * 2, name="middle",
        )(part, root_mid)
        came_sym = sent(mid_sym, length, (group, at(mid)), (group, at(0)))
        mid_zero = sent(mid_sym, length, (mid, at(mid)))
        at_l = run(
            functools.partial(low_kernel, length), 16, out_shape=two,
            in_specs=[vmem] * 2 + [anywhere], out_specs=vmem, name="low",
        )(node, came_part, mid_sym)
        made = run(
            functools.partial(first_kernel, length), 16, out_shape=(whole,) * 2 + half_state,
            in_specs=[vmem] * 3, out_specs=[anywhere] * 2 + [vmem] * 4, scratch_shapes=rooms, name="first",
        )(at_m, root_mid, came_far)
        diag, cross, *ends = run(
            functools.partial(second_kernel, length), 16, out_shape=(whole,) * 2 + half_state,
            in_specs=[vmem] * 5 + [anywhere] * 2 + [vmem] * 4, out_specs=[anywhere] * 2 + [vmem] * 4,
            scratch_shapes=rooms, input_output_aliases={5 + i: i for i in range(6)}, name="second",
        )(at_l, came_sym, mid_zero, part, came_part, *made)
        fours = (came_far, came_near)
    else:
        came_far = sent(node, length, (half, inner(half)), *away)
        came_near = sent(node, length, *close)
        diag, cross, below = upper_levels(inv_diag[0], low_coupling[0], up_coupling[0], length)
        diag, cross = diag[None], cross[None]
        ends = run(
            state_kernel, 16, out_shape=half_state, in_specs=[vmem] * 3, out_specs=[vmem] * 4, name="state",
        )(*below)
        fours = (came_far,)
    low_half, low_cross, high_half = run(
        functools.partial(halve_kernel, length), 16,
        out_shape=(rows_of(2 * ps), rows_of(pf), rows_of(state_rows)),
        in_specs=[vmem] * (4 + len(fours)), out_specs=[vmem] * 3, name="halve",
    )(*ends, *fours)
    three_cross = sent(low_cross, length, (-5, inner(0)))
    to_five = sent(high_half, length, (-3, inner(0)))
    to_one = sent(low_half, length, (-7, inner(0)))
    to_three = sent(low_half, length, (-5, inner(0)))
    to_seven = sent(high_half, length, (-1, inner(0)))
    one_cross = sent(three_cross, length, (-2, inner(3)))
    later, _ = lax.optimization_barrier((came_far, three_cross))
    came_back = sent(later, length, (-3, inner(2)))

    shapes = (jax.ShapeDtypeStruct((2 * width, 2 * width), bf16),) * 2 + (jax.ShapeDtypeStruct((width, 2 * width), f32),)
    composed = run(
        functools.partial(near_kernel, length, False), 16, out_shape=shapes,
        in_specs=[vmem] * 3, out_specs=[vmem] * 3, name="near",
    )(node, came_near, came_far)
    f_high, f_low, rest = run(
        functools.partial(near_kernel, length, True), 16, out_shape=shapes,
        in_specs=[vmem] * 2 + [vmem] * 3, out_specs=[vmem] * 3, name="back",
        input_output_aliases={2: 0, 3: 1, 4: 2},
    )(node, came_back, *composed)

    state = run(
        functools.partial(choose_kernel, length), 16,
        out_shape=rows_of(state_rows), in_specs=[vmem] * 6 + [anywhere], out_specs=vmem, name="choose",
    )(to_one, one_cross, to_three, three_cross, to_five, to_seven, composed[2])
    state_next = sent(state, length, (1, inner(1)), (1, inner(3)), (1, inner(5)))

    for parity, came in ((1, state), (0, state_next)):
        diag, cross = run(
            functools.partial(lower_kernel, length, parity), 20,
            out_shape=(whole, whole), in_specs=[vmem] * 4 + [anywhere] * 2, out_specs=[anywhere] * 2,
            scratch_shapes=[room(*square)] * 2 + [room(2 * width, 2 * width, kind=bf16)] * 2 + [sems],
            input_output_aliases={4: 0, 5: 1},
            name="lower",
        )(came, f_high, f_low, rest, diag, cross)
    return diag, cross


def solution(mesh):
    placed = (P(axis, None, None),) * 3
    return jax.shard_map(
        body, mesh=mesh, in_specs=placed, out_specs=placed[:2], check_vma=False
    )
```

```python
import functools

import jax
import jax.numpy as jnp
from jax import lax
from jax.experimental import pallas as pl
from jax.experimental.pallas import tpu as pltpu
from jax.sharding import PartitionSpec as P

row_offset = 3
lanes = 128
group = 8
axis = "tm"
bf16 = jnp.bfloat16
f32 = jnp.float32


def sym_rows(width):
    blocks = width // lanes
    pairs = blocks // 2
    return (blocks * (blocks - 1) // 2 + blocks - pairs) * lanes + 8 * pairs


def full_rows(width):
    return width * (width // lanes)


def tri():
    r = lax.broadcasted_iota(jnp.int32, (lanes, lanes), 0)
    c = lax.broadcasted_iota(jnp.int32, (lanes, lanes), 1)
    return r, c


def put_sym(ref, at, mat):
    blocks = mat.shape[0] // lanes
    block = lambda i, j: mat[i * lanes : (i + 1) * lanes, j * lanes : (j + 1) * lanes]
    for i in range(blocks):
        for j in range(i):
            ref[pl.ds(at, lanes), :] = block(i, j)
            at += lanes
    r, c = tri()
    for i in range(0, blocks - 1, 2):
        one, two = block(i, i), block(i + 1, i + 1)
        ref[pl.ds(at, lanes), :] = jnp.where(r >= c, one, two)
        at += lanes
        line = jnp.sum(jnp.where(r == c, two, 0.0), axis=0, keepdims=True)
        ref[pl.ds(at, 8), :] = jnp.broadcast_to(line, (8, lanes))
        at += 8
    if blocks % 2:
        ref[pl.ds(at, lanes), :] = block(blocks - 1, blocks - 1)


def get_sym(ref, at, width):
    blocks = width // lanes
    got = {}
    for i in range(blocks):
        for j in range(i):
            got[i, j] = ref[pl.ds(at, lanes), :]
            got[j, i] = got[i, j].T
            at += lanes
    r, c = tri()
    for i in range(0, blocks - 1, 2):
        both = ref[pl.ds(at, lanes), :]
        turned = both.T
        at += lanes
        line = ref[pl.ds(at, 8), :][0:1, :]
        at += 8
        got[i, i] = jnp.where(r >= c, both, turned)
        got[i + 1, i + 1] = jnp.where(r == c, line, jnp.where(r < c, both, turned))
    if blocks % 2:
        got[blocks - 1, blocks - 1] = ref[pl.ds(at, lanes), :]
    return jnp.concatenate(
        [jnp.concatenate([got[i, j] for j in range(blocks)], axis=1) for i in range(blocks)], axis=0
    )


def put_full(ref, at, mat):
    width = mat.shape[0]
    for j in range(width // lanes):
        ref[pl.ds(at + j * width, width), :] = mat[:, j * lanes : (j + 1) * lanes]


def get_full(ref, at, width):
    return jnp.concatenate(
        [ref[pl.ds(at + j * width, width), :] for j in range(width // lanes)], axis=1
    )


def parts_of(mat):
    high = mat.astype(bf16)
    return high, (mat - high.astype(f32)).astype(bf16)


def times(left, right, turned=False):
    dims = (((1,), (1 if turned else 0,)), ((), ()))
    dot = lambda a, b: lax.dot_general(a, b, dims, preferred_element_type=f32)
    return dot(left[0], right[0]) + (dot(left[0], right[1]) + dot(left[1], right[0]))


def long_left(parts):
    high, low = parts
    return jnp.concatenate([high, high, low], axis=1)


def long_right(parts, turned=False):
    high, low = parts
    return jnp.concatenate([high, low, high], axis=1 if turned else 0)


def long_times(left, right, turned=False):
    dims = (((1,), (1 if turned else 0,)), ((), ()))
    return lax.dot_general(left, right, dims, preferred_element_type=f32)


def symmetric_times(left, right):
    high, low = left
    width = high.shape[0]
    most = width // (2 * lanes) * (2 * lanes)

    def part(rows, columns):
        both = long_times(jnp.concatenate([high[rows], low[rows]], axis=0), right[0][columns], True)
        count = both.shape[0] // 2
        return (both[:count] + both[count:]) + long_times(high[rows], right[1][columns], True)

    wide = part(slice(0, width), slice(0, most))
    if most == width:
        return wide
    rest = part(slice(most, width), slice(most, width))
    return jnp.concatenate([wide, jnp.concatenate([wide[most:].T, rest], axis=0)], axis=1)


def beside(left, right):
    return tuple(jnp.concatenate(pair, axis=1) for pair in zip(left, right))


def set_state(sh, sl, aa, ba, bb):
    width = aa.shape[0]
    first, second = slice(0, width), slice(width, 2 * width)
    for rows, columns, mat in ((first, first, aa), (second, first, ba), (first, second, ba.T), (second, second, bb)):
        sh[rows, columns], sl[rows, columns] = parts_of(mat)


def eliminate(node, sh, sl):
    diag, g_mat, h_mat = node
    left = parts_of(jnp.concatenate([g_mat, h_mat], axis=1))
    passed = -times(left, (sh[...], sl[...]))
    return passed, diag - symmetric_times(left, parts_of(passed))


def place_now(length):
    return lax.rem(lax.axis_index(axis) + row_offset, length)


def fetch(sems, *pairs):
    copies = [pltpu.make_async_copy(source, target, sems.at[i]) for i, (source, target) in enumerate(pairs)]
    for copy in copies:
        copy.start()
    for copy in copies:
        copy.wait()


def own_kernel(inv_ref, low_ref, up_ref, sym_ref, part_ref, node_ref, rooms, lines, sems, out_sems):
    width = inv_ref.shape[1]
    ps, pf = sym_rows(width), full_rows(width)
    loads = [
        pltpu.make_async_copy(ref.at[0], rooms.at[i], sems.at[i]) for i, ref in enumerate((inv_ref, low_ref, up_ref))
    ]
    for load in loads:
        load.start()
    stores = []

    def store(at, rows, *refs):
        for ref in refs:
            where = pl.ds(at, rows)
            stores.append(pltpu.make_async_copy(lines.at[where, :], ref.at[where, :], out_sems.at[len(stores)]))
            stores[-1].start()

    loads[0].wait()
    inverse = rooms[0]
    put_sym(lines, 0, inverse)
    store(0, ps, sym_ref, part_ref, node_ref)
    inv_parts = parts_of(inverse)
    loads[1].wait()
    put_full(lines, ps, times(inv_parts, parts_of(rooms[1])))
    store(ps, pf, part_ref, node_ref)
    loads[2].wait()
    put_full(lines, ps + pf, times(inv_parts, parts_of(rooms[2])))
    store(ps + pf, pf, node_ref)
    for copy in stores:
        copy.wait()


def get_node(ref, width):
    ps, pf = sym_rows(width), full_rows(width)
    return get_sym(ref, 0, width), get_full(ref, ps, width), get_full(ref, ps + pf, width)


def put_state(ref, aa, ba, bb):
    ps = sym_rows(aa.shape[0])
    put_sym(ref, 0, aa)
    put_sym(ref, ps, bb)
    put_full(ref, 2 * ps, ba)


def roles_of(length):
    place = place_now(length)
    return place == 0, place == group, place == 2 * group, place == 3 * group


def ready_kernel(length, node, diag_ref, g_ref, high_ref, low_ref):
    width = diag_ref.shape[0]
    ps, pf = sym_rows(width), full_rows(width)
    at_zero, at_low, at_mid, at_high = roles_of(length)

    @pl.when(jnp.logical_or(jnp.logical_or(at_zero, at_low), jnp.logical_or(at_mid, at_high)))
    def _():
        diag_ref[...] = get_sym(node, 0, width)
        g_mat = get_full(node, ps, width)
        g_ref[...] = g_mat

        @pl.when(at_low)
        def _():
            high_ref[...], low_ref[...] = parts_of(get_full(node, ps + pf, width))

        @pl.when(jnp.logical_not(at_low))
        def _():
            high_ref[...], low_ref[...] = parts_of(g_mat)


def mid_kernel(length, node, diag, g_high, g_low, came_root, out, sym_ref):
    width = out.shape[1]
    ps = sym_rows(width)
    _, _, at_mid, _ = roles_of(length)

    @pl.when(jnp.logical_not(at_mid))
    def _():
        sym_ref[...] = node[pl.ds(0, ps), :]

    @pl.when(at_mid)
    def _():
        left = g_high[...], g_low[...]
        cross = -times(left, parts_of(get_sym(came_root, 0, width)))
        own = diag[...] - symmetric_times(left, parts_of(cross))
        put_sym(sym_ref, 0, own)
        out[0] = cross
        out[1] = own


def first_kernel(length, at_m, root_mid, came_node, kept, sh, sl, aa_ref, bb_ref):
    width = kept.shape[1]
    _, _, at_mid, _ = roles_of(length)

    @pl.when(at_mid)
    def _():
        mid_cross, mid = at_m[0], at_m[1]
        kept[0], kept[1] = mid, mid_cross
        set_state(sh, sl, get_sym(root_mid, 0, width), mid_cross, mid)
        passed, own = eliminate(get_node(came_node, width), sh, sl)
        put_sym(aa_ref, 0, own)
        put_sym(bb_ref, 0, mid)
        set_state(sh, sl, own, passed[:, width:].T, mid)


def second_kernel(
    length, diag, g_ref, high, low, came_part, came_sym, mid_high, _kept, _sh, _sl, _aa, _bb, kept, sh, sl, aa_ref, bb_ref
):
    width = kept.shape[1]
    ps = sym_rows(width)
    at_zero, at_low, _, at_high = roles_of(length)

    @pl.when(at_low)
    def _():
        h_parts = high[...], low[...]
        mid_both = jnp.concatenate([get_full(came_part, ps, width), get_sym(came_part, 0, width)], axis=1)
        both = times(h_parts, parts_of(mid_both))
        e_parts = parts_of(both[:, :width] - g_ref[...])
        root = get_sym(came_sym, 0, width)
        cross = times(e_parts, parts_of(root))
        own = diag[...] + symmetric_times(
            beside(parts_of(both[:, width:]), parts_of(cross)), beside(h_parts, e_parts)
        )
        aa_ref[...] = came_sym[...]
        put_sym(bb_ref, 0, own)
        set_state(sh, sl, root, cross, own)
        kept[0], kept[1] = own, cross

    def above(mid, own_diag, own_g):
        cross = -times(own_g, parts_of(mid))
        return cross, own_diag - symmetric_times(own_g, parts_of(cross))

    @pl.when(at_high)
    def _():
        mid = get_sym(mid_high, 0, width)
        cross, own = above(mid, diag[...], (high[...], low[...]))
        aa_ref[...] = mid_high[...]
        put_sym(bb_ref, 0, own)
        set_state(sh, sl, mid, cross, own)
        kept[0], kept[1] = own, cross

    @pl.when(at_zero)
    def _():
        high_g = parts_of(get_full(came_part, ps, width))
        _, own = above(get_sym(came_sym, 0, width), get_sym(came_part, 0, width), high_g)
        zeros = jnp.zeros((width, width), f32)
        put_sym(aa_ref, 0, own)
        bb_ref[...] = jnp.zeros((ps, lanes), f32)
        set_state(sh, sl, own, zeros, zeros)
        kept[0], kept[1] = diag[...], zeros


def state_kernel(aa_ref, ba_ref, bb_ref, sh, sl, aa_out, bb_out):
    aa, bb = aa_ref[...], bb_ref[...]
    put_sym(aa_out, 0, aa)
    put_sym(bb_out, 0, bb)
    set_state(sh, sl, aa, ba_ref[...], bb)


def halve_kernel(length, sh, sl, aa_ref, bb_ref, *refs):
    fours, (low_ref, low_cross_ref, high_ref) = refs[:-3], refs[-3:]
    width = sh.shape[0] // 2
    ps = sym_rows(width)
    place = place_now(length)

    def work(four):
        passed, own = eliminate(get_node(four, width), sh, sl)
        put_full(low_cross_ref, 0, passed[:, :width])
        put_full(high_ref, 2 * ps, passed[:, width:].T)
        low_ref[pl.ds(0, ps), :] = aa_ref[...]
        put_sym(low_ref, ps, own)
        high_ref[pl.ds(0, ps), :] = low_ref[pl.ds(ps, ps), :]
        high_ref[pl.ds(ps, ps), :] = bb_ref[...]

    served = lax.rem(place, group) == 0
    if len(fours) == 1:
        pl.when(served)(lambda: work(fours[0]))
    else:
        at_mid = place == 2 * group
        pl.when(at_mid)(lambda: work(fours[1]))
        pl.when(jnp.logical_and(served, jnp.logical_not(at_mid)))(lambda: work(fours[0]))


def offset_of(length):
    return lax.rem(place_now(length), group)


def near_kernel(length, late, node, *refs):
    f_high, f_low, rest_ref = refs[-3:]
    width = rest_ref.shape[0]
    offset = offset_of(length)
    turn = lax.rem(offset, group // 2)
    first, second = slice(0, width), slice(width, 2 * width)

    def put(rows, columns, mat):
        f_high[rows, columns], f_low[rows, columns] = parts_of(mat)

    def odd(below, two):
        d_own, g_own, h_own = get_node(node, width)
        d_two, g_two, h_two = get_node(two, width)
        inward, outward = (h_own, g_own) if below else (g_own, h_own)
        inward = parts_of(inward)
        to_low, to_high = times(inward, parts_of(g_two)), times(inward, parts_of(h_two))
        put(first, first, to_low - outward if below else to_low)
        put(first, second, to_high if below else to_high - outward)
        link = -times(inward, parts_of(d_two))
        rest_ref[:, first] = d_own - times(inward, parts_of(link), True)
        if not below:
            put(second, first, -g_two)
            put(second, second, -h_two)
            rest_ref[:, second] = link

    if late:
        pl.when(offset == group - 1)(lambda: odd(False, refs[0]))
        return
    came_near, came_far = refs[:2]
    pl.when(turn == 1)(lambda: odd(True, came_near))
    pl.when(offset == 3)(lambda: odd(False, came_far))

    @pl.when(turn == 2)
    def _():
        d_own, g_own, h_own = get_node(node, width)
        put(first, first, -g_own)
        put(first, second, -h_own)
        rest_ref[:, first] = d_own


def choose_kernel(length, one, one_cross, three, three_cross, five, _after, out_ref):
    offset = offset_of(length)
    for at, ends, cross in ((1, one, one_cross), (3, three, three_cross)):

        @pl.when(offset == at)
        def _(ends=ends, cross=cross):
            rows = ends.shape[0]
            out_ref[pl.ds(0, rows), :] = ends[...]
            out_ref[pl.ds(rows, cross.shape[0]), :] = cross[...]

    @pl.when(offset == 5)
    def _():
        out_ref[...] = five[...]


def lower_kernel(length, parity, state, seven, fh, fl, rest, kept, *refs):
    diag_ref, cross_ref, diag_out, cross_out, sh, sl, sems = refs[-7:]
    width = rest.shape[0]
    ps = sym_rows(width)
    offset = offset_of(length)
    turn = lax.rem(offset, group // 2)
    first, second = slice(0, width), slice(width, 2 * width)
    diag_copy = pltpu.make_async_copy(diag_out, diag_ref.at[0], sems.at[0])
    cross_copy = pltpu.make_async_copy(cross_out, cross_ref.at[0], sems.at[1])

    def finish():
        diag_copy.start()
        diag_copy.wait()
        cross_copy.wait()

    def passed_on(state):
        set_state(sh, sl, get_sym(state, 0, width), get_full(state, 2 * ps, width), get_sym(state, ps, width))
        return times((fh[first, :], fl[first, :]), (sh[...], sl[...]))

    @pl.when(turn == (1 if parity else 2))
    def _():
        passed = passed_on(state)
        cross_out[...] = passed[:, first]
        cross_copy.start()
        diag_out[...] = rest[:, first] + symmetric_times(parts_of(passed), (fh[first, :], fl[first, :]))
        finish()

    if parity == 0:

        @pl.when(offset == group // 2)
        def _():
            cross_out[...] = get_full(state, 2 * ps, width)
            cross_copy.start()
            diag_out[...] = get_sym(state, ps, width)
            finish()

    else:

        for at, ref in ((3, state), (group - 1, seven)):

            @pl.when(offset == at)
            def _(ref=ref):
                left = long_left(parts_of(passed_on(ref)))
                whole = long_times(left, long_right((fh[...], fl[...]), True), True) + rest[...]
                diag_out[...], cross_out[...] = whole[:, first], whole[:, second]
                cross_copy.start()
                finish()

        @pl.when(offset == 0)
        def _():
            diag_out[...], cross_out[...] = kept[0], kept[1]
            cross_copy.start()
            finish()


def sent(array, length, *moves):
    device = lambda position: (position - row_offset) % length
    pairs = [(device(p), device(p + by)) for by, wanted in moves for p in range(length) if wanted(p)]
    return lax.ppermute(array, axis, pairs)


def upper_levels(inverse, lowers, uppers, length):
    width = inverse.shape[0]
    place = (lax.axis_index(axis) + row_offset) % length
    product = functools.partial(jnp.dot, precision=lax.Precision.HIGHEST, preferred_element_type=f32)
    node_g, node_h = product(inverse, lowers), product(inverse, uppers)
    everywhere = lambda p: True
    zeros = jnp.zeros((width, width), f32)
    sigma = jnp.where(place == 0, inverse, zeros)
    low_own, high_own, cross = zeros, zeros, zeros
    stride = length // 2
    while stride >= group:
        from_low, owned_high = (sent(x, length, (stride, everywhere)) for x in (sigma, high_own))
        from_high, owned_low = (sent(x, length, (-stride, everywhere)) for x in (sigma, low_own))
        has_upper = place + stride < length
        sigma_high = jnp.where(has_upper, from_high, zeros)
        sigma_ba = jnp.where(has_upper, owned_high.T + owned_low, zeros)
        active = place % (2 * stride) == stride
        low = -(product(node_g, from_low) + product(node_h, sigma_ba))
        high = -(product(node_g, sigma_ba.T) + product(node_h, sigma_high))
        own = inverse - product(node_g, low.T) - product(node_h, high.T)
        sigma = jnp.where(active, own, sigma)
        low_own = jnp.where(active, low, zeros)
        high_own = jnp.where(active, high, zeros)
        cross = jnp.where(active, low, cross)
        stride //= 2
    newest = lambda p: p % (2 * group) == group
    below_aa, below_ba, below_bb = (sent(x, length, (group, newest)) for x in (sigma, high_own.T, sigma_high))
    return sigma, cross, tuple(
        jnp.where(active, *pair) for pair in ((from_low, below_aa), (low_own, below_ba), (sigma, below_bb))
    )


def body(inv_diag, low_coupling, up_coupling):
    width = inv_diag.shape[1]
    length = lax.axis_size(axis)
    span = 4 * group
    is_open = length == span
    ps, pf = sym_rows(width), full_rows(width)
    node_rows, state_rows = ps + 2 * pf, 2 * ps + pf
    rows_of = lambda rows: jax.ShapeDtypeStruct((rows, lanes), f32)
    square = (width, width)
    whole = jax.ShapeDtypeStruct((1,) + square, f32)
    vmem, anywhere = pl.BlockSpec(memory_space=pltpu.VMEM), pl.BlockSpec(memory_space=pl.ANY)
    room = lambda *shape, kind=f32: pltpu.VMEM(shape, kind)
    sems = pltpu.SemaphoreType.DMA((4,))
    run = lambda kernel, mib, flops=1, **more: pl.pallas_call(
        kernel, compiler_params=pltpu.CompilerParams(vmem_limit_bytes=mib * 2**20),
        cost_estimate=pl.CostEstimate(flops=flops, bytes_accessed=1, transcendentals=0), **more
    )
    at = lambda turn: (lambda p: p % span == turn)
    inner = lambda offset: (lambda p: p % group == offset)
    mid, half = 2 * group, group // 2

    sym, part, node = run(
        own_kernel, 60, out_shape=(rows_of(ps), rows_of(ps + pf), rows_of(node_rows)),
        in_specs=[anywhere] * 3, out_specs=[anywhere] * 3,
        scratch_shapes=[room(3, *square), room(node_rows, lanes), sems, pltpu.SemaphoreType.DMA((6,))], name="own",
    )(inv_diag, low_coupling, up_coupling)

    close = ((-1, inner(2)), (-1, inner(6)))
    away = ((1, inner(2)), (group // 2, inner(6)))
    half_state = (jax.ShapeDtypeStruct((2 * width, 2 * width), bf16),) * 2 + (rows_of(ps),) * 2
    if is_open:
        to_mid = lambda p: p == mid - half
        came_far = sent(
            node, length, (half, lambda p: inner(half)(p) and not to_mid(p)), (group, at(group)), *away
        )
        came_near = sent(node, length, (half, to_mid), *close)
        came_part = sent(part, length, (-group, at(mid)), (group, at(3 * group)))
        root_mid = sent(sym, length, (mid, at(0)))
        two = jax.ShapeDtypeStruct((2,) + square, f32)
        one = jax.ShapeDtypeStruct(square, f32)
        ready = run(
            functools.partial(ready_kernel, length), 16,
            out_shape=(one, one) + (jax.ShapeDtypeStruct(square, bf16),) * 2,
            in_specs=[vmem], out_specs=[vmem] * 4, name="ready",
        )(node)
        at_m, mid_sym = run(
            functools.partial(mid_kernel, length), 16, 4 * 10**9, out_shape=(two, rows_of(ps)),
            in_specs=[vmem] * 5, out_specs=[vmem] * 2, name="middle",
        )(node, ready[0], *ready[2:], root_mid)
        came_sym = sent(mid_sym, length, (mid, at(mid)), (group, at(0)))
        mid_high = sent(mid_sym, length, (group, at(mid)))
        made = run(
            functools.partial(first_kernel, length), 16, out_shape=(two,) + half_state,
            in_specs=[vmem] * 3, out_specs=[vmem] * 5, name="first",
        )(at_m, root_mid, came_far)
        kept, *ends = run(
            functools.partial(second_kernel, length), 16, out_shape=(two,) + half_state,
            in_specs=[vmem] * 12, out_specs=[vmem] * 5,
            input_output_aliases={7 + i: i for i in range(5)}, name="second",
        )(*ready, came_part, came_sym, mid_high, *made)
        fours = (came_far, came_near)
    else:
        came_far = sent(node, length, (half, inner(half)), *away)
        came_near = sent(node, length, *close)
        diag, cross, below = upper_levels(inv_diag[0], low_coupling[0], up_coupling[0], length)
        kept = jnp.stack([diag, cross])
        ends = run(
            state_kernel, 16, out_shape=half_state, in_specs=[vmem] * 3, out_specs=[vmem] * 4, name="state",
        )(*below)
        fours = (came_far,)
    low_half, low_cross, high_half = run(
        functools.partial(halve_kernel, length), 16,
        out_shape=(rows_of(2 * ps), rows_of(pf), rows_of(state_rows)),
        in_specs=[vmem] * (4 + len(fours)), out_specs=[vmem] * 3, name="halve",
    )(*ends, *fours)
    three_cross = sent(low_cross, length, (-5, inner(0)))
    to_five = sent(high_half, length, (-3, inner(0)))
    to_one = sent(low_half, length, (-7, inner(0)))
    to_three = sent(low_half, length, (-5, inner(0)))
    one_cross = sent(three_cross, length, (-2, inner(3)))
    to_seven = sent(high_half, length, (-1, inner(0)))
    later, _ = lax.optimization_barrier((came_far, three_cross))
    came_back = sent(later, length, (-3, inner(2)))

    shapes = (jax.ShapeDtypeStruct((2 * width, 2 * width), bf16),) * 2 + (jax.ShapeDtypeStruct((width, 2 * width), f32),)
    composed = run(
        functools.partial(near_kernel, length, False), 16, out_shape=shapes,
        in_specs=[vmem] * 3, out_specs=[vmem] * 3, name="near",
    )(node, came_near, came_far)
    f_high, f_low, rest = run(
        functools.partial(near_kernel, length, True), 16, out_shape=shapes,
        in_specs=[vmem] * 2 + [vmem] * 3, out_specs=[vmem] * 3, name="back",
        input_output_aliases={2: 0, 3: 1, 4: 2},
    )(node, came_back, *composed)

    state = run(
        functools.partial(choose_kernel, length), 16, 4 * 10**9,
        out_shape=rows_of(state_rows), in_specs=[vmem] * 5 + [anywhere], out_specs=vmem, name="choose",
    )(to_one, one_cross, to_three, three_cross, to_five, composed[2])
    state_next = sent(state, length, (1, inner(1)), (1, inner(3)), (1, inner(5)))

    outputs = ()
    for parity, came in ((1, state), (0, state_next)):
        outputs = run(
            functools.partial(lower_kernel, length, parity), 20,
            out_shape=(whole, whole), in_specs=[vmem] * 6 + [anywhere] * len(outputs), out_specs=[anywhere] * 2,
            scratch_shapes=[room(*square)] * 2 + [room(2 * width, 2 * width, kind=bf16)] * 2 + [sems],
            input_output_aliases={6 + i: i for i in range(len(outputs))}, name="lower",
        )(came, to_seven, f_high, f_low, rest, kept, *outputs)
    return outputs


def solution(mesh):
    placed = (P(axis, None, None),) * 3
    return jax.shard_map(
        body, mesh=mesh, in_specs=placed, out_specs=placed[:2], check_vma=False
    )
```

```python
import functools

import jax
import jax.numpy as jnp
from jax import lax
from jax.experimental import pallas as pl
from jax.experimental.pallas import tpu as pltpu
from jax.sharding import PartitionSpec as P

row_offset = 3
lanes = 128
group = 8
axis = "tm"
bf16 = jnp.bfloat16
f32 = jnp.float32


def sym_rows(width):
    blocks = width // lanes
    pairs = blocks // 2
    return (blocks * (blocks - 1) // 2 + blocks - pairs) * lanes + 8 * pairs


def full_rows(width):
    return width * (width // lanes)


def tri():
    r = lax.broadcasted_iota(jnp.int32, (lanes, lanes), 0)
    c = lax.broadcasted_iota(jnp.int32, (lanes, lanes), 1)
    return r, c


def put_sym(ref, at, mat):
    blocks = mat.shape[0] // lanes
    block = lambda i, j: mat[i * lanes : (i + 1) * lanes, j * lanes : (j + 1) * lanes]
    for i in range(blocks):
        for j in range(i):
            ref[pl.ds(at, lanes), :] = block(i, j)
            at += lanes
    r, c = tri()
    for i in range(0, blocks - 1, 2):
        one, two = block(i, i), block(i + 1, i + 1)
        ref[pl.ds(at, lanes), :] = jnp.where(r >= c, one, two)
        at += lanes
        line = jnp.sum(jnp.where(r == c, two, 0.0), axis=0, keepdims=True)
        ref[pl.ds(at, 8), :] = jnp.broadcast_to(line, (8, lanes))
        at += 8
    if blocks % 2:
        ref[pl.ds(at, lanes), :] = block(blocks - 1, blocks - 1)


def get_sym(ref, at, width):
    blocks = width // lanes
    got = {}
    for i in range(blocks):
        for j in range(i):
            got[i, j] = ref[pl.ds(at, lanes), :]
            got[j, i] = got[i, j].T
            at += lanes
    r, c = tri()
    for i in range(0, blocks - 1, 2):
        both = ref[pl.ds(at, lanes), :]
        turned = both.T
        at += lanes
        line = ref[pl.ds(at, 8), :][0:1, :]
        at += 8
        got[i, i] = jnp.where(r >= c, both, turned)
        got[i + 1, i + 1] = jnp.where(r == c, line, jnp.where(r < c, both, turned))
    if blocks % 2:
        got[blocks - 1, blocks - 1] = ref[pl.ds(at, lanes), :]
    return jnp.concatenate(
        [jnp.concatenate([got[i, j] for j in range(blocks)], axis=1) for i in range(blocks)], axis=0
    )


def put_full(ref, at, mat):
    width = mat.shape[0]
    for j in range(width // lanes):
        ref[pl.ds(at + j * width, width), :] = mat[:, j * lanes : (j + 1) * lanes]


def get_full(ref, at, width):
    return jnp.concatenate(
        [ref[pl.ds(at + j * width, width), :] for j in range(width // lanes)], axis=1
    )


def parts_of(mat):
    high = mat.astype(bf16)
    return high, (mat - high.astype(f32)).astype(bf16)


def times(left, right, turned=False):
    dims = (((1,), (1 if turned else 0,)), ((), ()))
    dot = lambda a, b: lax.dot_general(a, b, dims, preferred_element_type=f32)
    return dot(left[0], right[0]) + (dot(left[0], right[1]) + dot(left[1], right[0]))


def long_left(parts):
    high, low = parts
    return jnp.concatenate([high, high, low], axis=1)


def long_right(parts, turned=False):
    high, low = parts
    return jnp.concatenate([high, low, high], axis=1 if turned else 0)


def long_times(left, right, turned=False):
    dims = (((1,), (1 if turned else 0,)), ((), ()))
    return lax.dot_general(left, right, dims, preferred_element_type=f32)


def symmetric_times(left, right):
    high, low = left
    width = high.shape[0]
    most = width // (2 * lanes) * (2 * lanes)

    def part(rows, columns):
        both = long_times(jnp.concatenate([high[rows], low[rows]], axis=0), right[0][columns], True)
        count = both.shape[0] // 2
        return (both[:count] + both[count:]) + long_times(high[rows], right[1][columns], True)

    wide = part(slice(0, width), slice(0, most))
    if most == width:
        return wide
    rest = part(slice(most, width), slice(most, width))
    return jnp.concatenate([wide, jnp.concatenate([wide[most:].T, rest], axis=0)], axis=1)


def beside(left, right):
    return tuple(jnp.concatenate(pair, axis=1) for pair in zip(left, right))


def set_state(sh, sl, aa, ba, bb):
    width = aa.shape[0]
    first, second = slice(0, width), slice(width, 2 * width)
    for rows, columns, mat in ((first, first, aa), (second, first, ba), (first, second, ba.T), (second, second, bb)):
        sh[rows, columns], sl[rows, columns] = parts_of(mat)


def eliminate(node, sh, sl):
    diag, g_mat, h_mat = node
    left = parts_of(jnp.concatenate([g_mat, h_mat], axis=1))
    passed = -times(left, (sh[...], sl[...]))
    return passed, diag - symmetric_times(left, parts_of(passed))


def place_now(length):
    return lax.rem(lax.axis_index(axis) + row_offset, length)


def fetch(sems, *pairs):
    copies = [pltpu.make_async_copy(source, target, sems.at[i]) for i, (source, target) in enumerate(pairs)]
    for copy in copies:
        copy.start()
    for copy in copies:
        copy.wait()


def own_kernel(inv_ref, low_ref, up_ref, sym_ref, g_ref, node_ref, rooms, lines, sems, out_sems):
    width = inv_ref.shape[1]
    ps, pf = sym_rows(width), full_rows(width)
    loads = [
        pltpu.make_async_copy(ref.at[0], rooms.at[i], sems.at[i]) for i, ref in enumerate((inv_ref, low_ref, up_ref))
    ]
    for load in loads:
        load.start()
    stores = []

    def store(at, rows, *refs):
        where = pl.ds(at, rows)
        for ref in refs:
            target = ref.at[where, :] if ref is node_ref else ref
            stores.append(pltpu.make_async_copy(lines.at[where, :], target, out_sems.at[len(stores)]))
            stores[-1].start()

    loads[0].wait()
    inverse = rooms[0]
    put_sym(lines, 0, inverse)
    store(0, ps, sym_ref, node_ref)
    inv_parts = parts_of(inverse)
    loads[1].wait()
    put_full(lines, ps, times(inv_parts, parts_of(rooms[1])))
    store(ps, pf, g_ref, node_ref)
    loads[2].wait()
    up_high, up_low = parts_of(rooms[2])
    most = width // (2 * lanes) * (2 * lanes)
    for begin, end in ((0, most), (most, width)):
        if begin < end:
            product = times(inv_parts, (up_high[:, begin:end], up_low[:, begin:end]))
            for j in range(begin // lanes, end // lanes):
                lines[pl.ds(ps + pf + j * width, width), :] = product[:, j * lanes - begin : (j + 1) * lanes - begin]
            store(ps + pf + begin // lanes * width, (end - begin) // lanes * width, node_ref)
    for copy in stores:
        copy.wait()


def get_node(ref, width):
    ps, pf = sym_rows(width), full_rows(width)
    return get_sym(ref, 0, width), get_full(ref, ps, width), get_full(ref, ps + pf, width)


def put_state(ref, aa, ba, bb):
    ps = sym_rows(aa.shape[0])
    put_sym(ref, 0, aa)
    put_sym(ref, ps, bb)
    put_full(ref, 2 * ps, ba)


def roles_of(length):
    place = place_now(length)
    return place == 0, place == group, place == 2 * group, place == 3 * group


def ready_kernel(length, node, diag_ref, g_ref, high_ref, low_ref):
    width = diag_ref.shape[0]
    ps, pf = sym_rows(width), full_rows(width)
    at_zero, at_low, at_mid, at_high = roles_of(length)

    @pl.when(jnp.logical_or(jnp.logical_or(at_zero, at_low), jnp.logical_or(at_mid, at_high)))
    def _():
        diag_ref[...] = get_sym(node, 0, width)
        g_mat = get_full(node, ps, width)
        g_ref[...] = g_mat

        @pl.when(at_low)
        def _():
            high_ref[...], low_ref[...] = parts_of(get_full(node, ps + pf, width))

        @pl.when(jnp.logical_not(at_low))
        def _():
            high_ref[...], low_ref[...] = parts_of(g_mat)


def mid_kernel(length, node, diag, g_high, g_low, came_root, out, sym_ref):
    width = out.shape[1]
    ps = sym_rows(width)
    _, _, at_mid, _ = roles_of(length)

    @pl.when(jnp.logical_not(at_mid))
    def _():
        sym_ref[...] = node[pl.ds(0, ps), :]

    @pl.when(at_mid)
    def _():
        left = g_high[...], g_low[...]
        cross = -times(left, parts_of(get_sym(came_root, 0, width)))
        own = diag[...] - symmetric_times(left, parts_of(cross))
        put_sym(sym_ref, 0, own)
        out[0] = cross
        out[1] = own


def first_kernel(length, at_m, root_mid, came_node, kept, sh, sl, aa_ref, bb_ref):
    width = kept.shape[1]
    _, _, at_mid, _ = roles_of(length)

    @pl.when(at_mid)
    def _():
        mid_cross, mid = at_m[0], at_m[1]
        kept[0], kept[1] = mid, mid_cross
        set_state(sh, sl, get_sym(root_mid, 0, width), mid_cross, mid)
        passed, own = eliminate(get_node(came_node, width), sh, sl)
        put_sym(aa_ref, 0, own)
        put_sym(bb_ref, 0, mid)
        set_state(sh, sl, own, passed[:, width:].T, mid)


def second_kernel(
    length, diag, g_ref, high, low, came_d, came_g, came_sym, mid_high, _kept, _sh, _sl, _aa, came_bb, kept, sh, sl, aa_ref, bb_ref, own_ref
):
    width = kept.shape[1]
    ps = sym_rows(width)
    at_zero, at_low, at_mid, at_high = roles_of(length)

    @pl.when(at_mid)
    def _():
        own_ref[...] = came_bb[...]

    @pl.when(at_low)
    def _():
        h_parts = high[...], low[...]
        mid_both = jnp.concatenate([get_full(came_g, 0, width), get_sym(came_d, 0, width)], axis=1)
        both = times(h_parts, parts_of(mid_both))
        e_parts = parts_of(both[:, :width] - g_ref[...])
        root = get_sym(came_sym, 0, width)
        cross = times(e_parts, parts_of(root))
        own = diag[...] + symmetric_times(
            beside(parts_of(both[:, width:]), parts_of(cross)), beside(h_parts, e_parts)
        )
        aa_ref[...] = came_sym[...]
        put_sym(bb_ref, 0, own)
        own_ref[...] = bb_ref[...]
        set_state(sh, sl, root, cross, own)
        kept[0], kept[1] = own, cross

    def above(mid, own_diag, own_g):
        cross = -times(own_g, parts_of(mid))
        return cross, own_diag - symmetric_times(own_g, parts_of(cross))

    @pl.when(at_high)
    def _():
        mid = get_sym(mid_high, 0, width)
        cross, own = above(mid, diag[...], (high[...], low[...]))
        aa_ref[...] = mid_high[...]
        put_sym(bb_ref, 0, own)
        own_ref[...] = bb_ref[...]
        set_state(sh, sl, mid, cross, own)
        kept[0], kept[1] = own, cross

    @pl.when(at_zero)
    def _():
        high_g = parts_of(get_full(came_g, 0, width))
        _, own = above(get_sym(came_sym, 0, width), get_sym(came_d, 0, width), high_g)
        zeros = jnp.zeros((width, width), f32)
        put_sym(aa_ref, 0, own)
        bb_ref[...] = jnp.zeros((ps, lanes), f32)
        set_state(sh, sl, own, zeros, zeros)
        put_sym(own_ref, 0, diag[...])
        kept[0], kept[1] = diag[...], zeros


def state_kernel(aa_ref, ba_ref, bb_ref, own_ref, sh, sl, aa_out, bb_out, own_out):
    aa, bb = aa_ref[...], bb_ref[...]
    put_sym(aa_out, 0, aa)
    put_sym(bb_out, 0, bb)
    put_sym(own_out, 0, own_ref[...])
    set_state(sh, sl, aa, ba_ref[...], bb)


def four_for(length, fours, work):
    place = place_now(length)
    served = lax.rem(place, group) == 0
    if len(fours) == 1:
        pl.when(served)(lambda: work(fours[0]))
    else:
        at_mid = place == 2 * group
        pl.when(at_mid)(lambda: work(fours[1]))
        pl.when(jnp.logical_and(served, jnp.logical_not(at_mid)))(lambda: work(fours[0]))


def cross_kernel(length, sh, sl, *refs):
    fours, (low_ref, high_ref, passed_high, passed_low) = refs[:-4], refs[-4:]
    width = sh.shape[0] // 2

    def work(four):
        _, g_mat, h_mat = get_node(four, width)
        passed = -times(parts_of(jnp.concatenate([g_mat, h_mat], axis=1)), (sh[...], sl[...]))
        put_full(low_ref, 0, passed[:, :width])
        put_full(high_ref, 0, passed[:, width:].T)
        passed_high[...], passed_low[...] = parts_of(passed)

    four_for(length, fours, work)


def ends_kernel(length, passed_high, passed_low, aa_ref, bb_ref, cross_ref, *refs):
    fours, (low_ends, high_ends, mid_ref, high_ref) = refs[:-4], refs[-4:]
    ps = mid_ref.shape[0]
    width = passed_high.shape[0]

    def work(four):
        diag, g_mat, h_mat = get_node(four, width)
        left = parts_of(jnp.concatenate([g_mat, h_mat], axis=1))
        put_sym(mid_ref, 0, diag - symmetric_times(left, (passed_high[...], passed_low[...])))
        for ref, at in ((low_ends, ps), (high_ends, 0), (high_ref, 0)):
            ref[pl.ds(at, ps), :] = mid_ref[...]
        low_ends[pl.ds(0, ps), :] = aa_ref[...]
        high_ends[pl.ds(ps, ps), :] = bb_ref[...]
        high_ref[pl.ds(ps, ps), :] = bb_ref[...]
        high_ref[pl.ds(2 * ps, cross_ref.shape[0]), :] = cross_ref[...]

    four_for(length, fours, work)


def offset_of(length):
    return lax.rem(place_now(length), group)


def near_kernel(length, late, node, *refs):
    f_high, f_low, rest_ref = refs[-3:]
    width = rest_ref.shape[0]
    offset = offset_of(length)
    turn = lax.rem(offset, group // 2)
    first, second = slice(0, width), slice(width, 2 * width)

    def put(rows, columns, mat):
        f_high[rows, columns], f_low[rows, columns] = parts_of(mat)

    def odd(below, two):
        d_own, g_own, h_own = get_node(node, width)
        d_two, g_two, h_two = get_node(two, width)
        inward, outward = (h_own, g_own) if below else (g_own, h_own)
        inward = parts_of(inward)
        to_low, to_high = times(inward, parts_of(g_two)), times(inward, parts_of(h_two))
        put(first, first, to_low - outward if below else to_low)
        put(first, second, to_high if below else to_high - outward)
        link = -times(inward, parts_of(d_two))
        rest_ref[:, first] = d_own - times(inward, parts_of(link), True)
        if not below:
            put(second, first, -g_two)
            put(second, second, -h_two)
            rest_ref[:, second] = link

    if late:
        pl.when(offset == group - 1)(lambda: odd(False, refs[0]))
        return
    came_near, came_far = refs[:2]
    pl.when(turn == 1)(lambda: odd(True, came_near))
    pl.when(offset == 3)(lambda: odd(False, came_far))

    @pl.when(turn == 2)
    def _():
        d_own, g_own, h_own = get_node(node, width)
        put(first, first, -g_own)
        put(first, second, -h_own)
        rest_ref[:, first] = d_own


def choose_kernel(length, first, third, fifth, *refs):
    out_ref = refs[-1]
    offset = offset_of(length)
    refs = iter(refs)
    for at, count in ((1, first), (3, third), (5, fifth)):
        parts = [next(refs) for _ in range(count)]

        @pl.when(offset == at)
        def _(parts=parts):
            begin = 0
            for part in parts:
                rows = part.shape[0]
                out_ref[pl.ds(begin, rows), :] = part[...]
                begin += rows


def passed_ends(fh, fl, ref, width):
    first, second = slice(0, width), slice(width, 2 * width)
    low, high = (get_sym(ref, at, width) for at in (0, sym_rows(width)))
    return jnp.concatenate(
        [times((fh[first, part], fl[first, part]), parts_of(mat)) for part, mat in ((first, low), (second, high))], axis=1
    )


def passed_cross(fh, fl, ref, at, width):
    first, second = slice(0, width), slice(width, 2 * width)
    cross = parts_of(get_full(ref, at, width))
    return jnp.concatenate(
        [times((fh[first, second], fl[first, second]), cross), times((fh[first, first], fl[first, first]), cross, True)],
        axis=1,
    )


def begin_kernel(length, early, early_next, fh, fl, out, room):
    width = out.shape[0]
    offset = offset_of(length)
    turn = lax.rem(offset, group // 2)
    odd = lax.rem(offset, 2) == 1

    @pl.when(odd)
    def _():
        room[...] = early[...]

    @pl.when(jnp.logical_not(odd))
    def _():
        room[...] = early_next[...]

    @pl.when(jnp.logical_and(turn > 0, offset < 3))
    def _():
        out[...] = passed_ends(fh, fl, room, width)

    @pl.when(jnp.logical_and(turn > 0, offset >= 3))
    def _():
        out[...] = passed_cross(fh, fl, room, 0, width)


def lower_kernel(length, parity, begun, early, late, seven, fh, fl, rest, kept, *refs):
    diag_ref, cross_ref, diag_out, cross_out, passed, sems = refs[-6:]
    width = rest.shape[0]
    ps = sym_rows(width)
    offset = offset_of(length)
    turn = lax.rem(offset, group // 2)
    first, second = slice(0, width), slice(width, 2 * width)
    diag_copy = pltpu.make_async_copy(diag_out, diag_ref.at[0], sems.at[0])
    cross_copy = pltpu.make_async_copy(cross_out, cross_ref.at[0], sems.at[1])

    def finish():
        diag_copy.start()
        diag_copy.wait()
        cross_copy.wait()

    @pl.when(offset == (1 if parity else 2))
    def _():
        passed[...] = begun[...] + passed_cross(fh, fl, late, 0, width)

    @pl.when(jnp.logical_or(offset == (5 if parity else 6), offset == (3 if parity else 6)))
    def _():
        passed[...] = begun[...] + passed_ends(fh, fl, late, width)

    @pl.when(turn == (1 if parity else 2))
    def _():
        cross_out[...] = passed[:, first]
        cross_copy.start()
        diag_out[...] = rest[:, first] + symmetric_times(parts_of(passed[...]), (fh[first, :], fl[first, :]))
        finish()

    if parity == 0:

        @pl.when(offset == group // 2)
        def _():
            cross_out[...] = get_full(early, 0, width)
            cross_copy.start()
            diag_out[...] = get_sym(late, ps, width)
            finish()

    else:

        @pl.when(offset == group - 1)
        def _():
            passed[...] = passed_ends(fh, fl, seven, width) + passed_cross(fh, fl, seven, 2 * ps, width)

        @pl.when(turn == 3)
        def _():
            left = long_left(parts_of(passed[...]))
            whole = long_times(left, long_right((fh[...], fl[...]), True), True) + rest[...]
            diag_out[...], cross_out[...] = whole[:, first], whole[:, second]
            cross_copy.start()
            finish()

        @pl.when(offset == 0)
        def _():
            diag_out[...], cross_out[...] = kept[0], kept[1]
            cross_copy.start()
            finish()


def sent(array, length, *moves):
    device = lambda position: (position - row_offset) % length
    pairs = [(device(p), device(p + by)) for by, wanted in moves for p in range(length) if wanted(p)]
    return lax.ppermute(array, axis, pairs)


def upper_levels(inverse, lowers, uppers, length):
    width = inverse.shape[0]
    place = (lax.axis_index(axis) + row_offset) % length
    product = functools.partial(jnp.dot, precision=lax.Precision.HIGHEST, preferred_element_type=f32)
    node_g, node_h = product(inverse, lowers), product(inverse, uppers)
    everywhere = lambda p: True
    zeros = jnp.zeros((width, width), f32)
    sigma = jnp.where(place == 0, inverse, zeros)
    low_own, high_own, cross = zeros, zeros, zeros
    stride = length // 2
    while stride >= group:
        from_low, owned_high = (sent(x, length, (stride, everywhere)) for x in (sigma, high_own))
        from_high, owned_low = (sent(x, length, (-stride, everywhere)) for x in (sigma, low_own))
        has_upper = place + stride < length
        sigma_high = jnp.where(has_upper, from_high, zeros)
        sigma_ba = jnp.where(has_upper, owned_high.T + owned_low, zeros)
        active = place % (2 * stride) == stride
        low = -(product(node_g, from_low) + product(node_h, sigma_ba))
        high = -(product(node_g, sigma_ba.T) + product(node_h, sigma_high))
        own = inverse - product(node_g, low.T) - product(node_h, high.T)
        sigma = jnp.where(active, own, sigma)
        low_own = jnp.where(active, low, zeros)
        high_own = jnp.where(active, high, zeros)
        cross = jnp.where(active, low, cross)
        stride //= 2
    newest = lambda p: p % (2 * group) == group
    below_aa, below_ba, below_bb = (sent(x, length, (group, newest)) for x in (sigma, high_own.T, sigma_high))
    return sigma, cross, tuple(
        jnp.where(active, *pair) for pair in ((from_low, below_aa), (low_own, below_ba), (sigma, below_bb))
    )


def body(inv_diag, low_coupling, up_coupling):
    width = inv_diag.shape[1]
    length = lax.axis_size(axis)
    span = 4 * group
    is_open = length == span
    ps, pf = sym_rows(width), full_rows(width)
    node_rows, state_rows = ps + 2 * pf, 2 * ps + pf
    rows_of = lambda rows: jax.ShapeDtypeStruct((rows, lanes), f32)
    square = (width, width)
    whole = jax.ShapeDtypeStruct((1,) + square, f32)
    vmem, anywhere = pl.BlockSpec(memory_space=pltpu.VMEM), pl.BlockSpec(memory_space=pl.ANY)
    room = lambda *shape, kind=f32: pltpu.VMEM(shape, kind)
    sems = pltpu.SemaphoreType.DMA((4,))
    run = lambda kernel, mib, flops=1, **more: pl.pallas_call(
        kernel, compiler_params=pltpu.CompilerParams(vmem_limit_bytes=mib * 2**20),
        cost_estimate=pl.CostEstimate(flops=flops, bytes_accessed=1, transcendentals=0), **more
    )
    at = lambda turn: (lambda p: p % span == turn)
    inner = lambda offset: (lambda p: p % group == offset)
    mid, half = 2 * group, group // 2

    sym, g_only, node = run(
        own_kernel, 60, out_shape=(rows_of(ps), rows_of(pf), rows_of(node_rows)),
        in_specs=[anywhere] * 3, out_specs=[anywhere] * 3,
        scratch_shapes=[room(3, *square), room(node_rows, lanes), sems, pltpu.SemaphoreType.DMA((6,))], name="own",
    )(inv_diag, low_coupling, up_coupling)

    close = ((-1, inner(2)), (-1, inner(6)))
    away = ((1, inner(2)), (group // 2, inner(6)))
    half_state = (jax.ShapeDtypeStruct((2 * width, 2 * width), bf16),) * 2 + (rows_of(ps),) * 2
    if is_open:
        to_mid = lambda p: p == mid - half
        came_far = sent(
            node, length, (half, lambda p: inner(half)(p) and not to_mid(p)), (group, at(group)), *away
        )
        came_near = sent(node, length, (half, to_mid), *close)
        came_g = sent(g_only, length, (-group, at(mid)), (group, at(3 * group)))
        came_d = sent(sym, length, (mid, at(0)), (-group, at(mid)), (group, at(3 * group)))
        two = jax.ShapeDtypeStruct((2,) + square, f32)
        one = jax.ShapeDtypeStruct(square, f32)
        ready = run(
            functools.partial(ready_kernel, length), 16,
            out_shape=(one, one) + (jax.ShapeDtypeStruct(square, bf16),) * 2,
            in_specs=[vmem], out_specs=[vmem] * 4, name="ready",
        )(node)
        at_m, mid_sym = run(
            functools.partial(mid_kernel, length), 16, 4 * 10**9, out_shape=(two, rows_of(ps)),
            in_specs=[vmem] * 5, out_specs=[vmem] * 2, name="middle",
        )(node, ready[0], *ready[2:], came_d)
        came_sym = sent(mid_sym, length, (mid, at(mid)), (group, at(0)))
        mid_high = sent(mid_sym, length, (group, at(mid)))
        made = run(
            functools.partial(first_kernel, length), 16, out_shape=(two,) + half_state,
            in_specs=[vmem] * 3, out_specs=[vmem] * 5, name="first",
        )(at_m, came_d, came_far)
        kept, *ends, ended = run(
            functools.partial(second_kernel, length), 16, 5 * 10**9, out_shape=(two,) + half_state + (rows_of(ps),),
            in_specs=[vmem] * 13, out_specs=[vmem] * 6,
            input_output_aliases={8 + i: i for i in range(5)}, name="second",
        )(*ready, came_d, came_g, came_sym, mid_high, *made)
        fours = (came_far, came_near)
    else:
        came_far = sent(node, length, (half, inner(half)), *away)
        came_near = sent(node, length, *close)
        diag, cross, below = upper_levels(inv_diag[0], low_coupling[0], up_coupling[0], length)
        kept = jnp.stack([diag, cross])
        *ends, ended = run(
            state_kernel, 16, out_shape=half_state + (rows_of(ps),), in_specs=[vmem] * 4, out_specs=[vmem] * 5,
            name="state",
        )(*below, diag)
        fours = (came_far,)
    one_end = sent(ended, length, (1, inner(0)))
    served = len(fours)
    low_cross, high_cross, *passed = run(
        functools.partial(cross_kernel, length), 16,
        out_shape=(rows_of(pf),) * 2 + (jax.ShapeDtypeStruct((width, 2 * width), bf16),) * 2,
        in_specs=[vmem] * (2 + served), out_specs=[vmem] * 4, name="halve",
    )(*ends[:2], *fours)
    three_cross = sent(low_cross, length, (-5, inner(0)))
    five_cross = sent(high_cross, length, (-3, inner(0)))
    low_ends, high_ends, half_mid, high_half = run(
        functools.partial(ends_kernel, length), 16,
        out_shape=(rows_of(2 * ps),) * 2 + (rows_of(ps), rows_of(state_rows)),
        in_specs=[vmem] * (5 + served), out_specs=[vmem] * 4, name="halves",
    )(*passed, *ends[2:], high_cross, *fours)
    five_ends = sent(high_ends, length, (-3, inner(0)))
    one_mid = sent(half_mid, length, (-7, inner(0)))
    three_ends = sent(low_ends, length, (-5, inner(0)))
    shapes = (jax.ShapeDtypeStruct((2 * width, 2 * width), bf16),) * 2 + (jax.ShapeDtypeStruct((width, 2 * width), f32),)
    composed = run(
        functools.partial(near_kernel, length, False), 16, 4 * 10**9, out_shape=shapes,
        in_specs=[vmem] * 3 + [anywhere], out_specs=[vmem] * 3, name="near",
    )(node, came_near, came_far, one_end)
    by_three, _ = lax.optimization_barrier((three_cross, composed[2]))
    one_cross = sent(by_three, length, (-2, inner(3)))
    to_seven = sent(high_half, length, (-1, inner(0)))
    later, _ = lax.optimization_barrier((came_far, three_cross))
    came_back = sent(later, length, (-3, inner(2)))

    f_high, f_low, rest = run(
        functools.partial(near_kernel, length, True), 16, out_shape=shapes,
        in_specs=[vmem] * 2 + [vmem] * 3, out_specs=[vmem] * 3, name="back",
        input_output_aliases={2: 0, 3: 1, 4: 2},
    )(node, came_back, *composed)

    def chosen(name, flops, *groups, after=()):
        return run(
            functools.partial(choose_kernel, length, *map(len, groups)), 16, flops,
            out_shape=rows_of(2 * ps), in_specs=[vmem] * sum(map(len, groups)) + [anywhere] * len(after),
            out_specs=vmem, name=name,
        )(*(array for arrays in groups for array in arrays), *after)

    early = chosen("early", 1, (one_end, one_mid), (three_cross,), (five_cross,), after=(composed[2],))
    onward = ((1, inner(1)), (1, inner(3)), (1, inner(5)))
    early_next = sent(early, length, *onward)
    begun = run(
        functools.partial(begin_kernel, length), 16, out_shape=jax.ShapeDtypeStruct((width, 2 * width), f32),
        in_specs=[vmem] * 4, out_specs=vmem, scratch_shapes=[room(2 * ps, lanes)], name="begin",
    )(early, early_next, *composed[:2])

    late = chosen("late", 4 * 10**9, (one_cross,), (three_ends,), (five_ends,), after=(early,))
    late_next = sent(late, length, *onward)

    outputs = ()
    for parity, came in ((1, (early, late)), (0, (early_next, late_next))):
        outputs = run(
            functools.partial(lower_kernel, length, parity), 20,
            out_shape=(whole, whole), in_specs=[vmem] * 8 + [anywhere] * len(outputs), out_specs=[anywhere] * 2,
            scratch_shapes=[room(*square)] * 2 + [room(width, 2 * width), sems],
            input_output_aliases={8 + i: i for i in range(len(outputs))}, name="lower",
        )(begun, *came, to_seven, f_high, f_low, rest, kept, *outputs)
    return outputs


def solution(mesh):
    placed = (P(axis, None, None),) * 3
    return jax.shard_map(
        body, mesh=mesh, in_specs=placed, out_specs=placed[:2], check_vma=False
    )
```

```python
import functools

import jax
import jax.numpy as jnp
from jax import lax
from jax.experimental import pallas as pl
from jax.experimental.pallas import tpu as pltpu
from jax.sharding import PartitionSpec as P

row_offset = 3
lanes = 128
group = 8
axis = "tm"
bf16 = jnp.bfloat16
f32 = jnp.float32


def sym_rows(width):
    blocks = width // lanes
    pairs = blocks // 2
    return (blocks * (blocks - 1) // 2 + blocks - pairs) * lanes + 8 * pairs


def full_rows(width):
    return width * (width // lanes)


def tri():
    r = lax.broadcasted_iota(jnp.int32, (lanes, lanes), 0)
    c = lax.broadcasted_iota(jnp.int32, (lanes, lanes), 1)
    return r, c


def put_sym(ref, at, mat):
    blocks = mat.shape[0] // lanes
    block = lambda i, j: mat[i * lanes : (i + 1) * lanes, j * lanes : (j + 1) * lanes]
    for i in range(blocks):
        for j in range(i):
            ref[pl.ds(at, lanes), :] = block(i, j)
            at += lanes
    r, c = tri()
    for i in range(0, blocks - 1, 2):
        one, two = block(i, i), block(i + 1, i + 1)
        ref[pl.ds(at, lanes), :] = jnp.where(r >= c, one, two)
        at += lanes
        line = jnp.sum(jnp.where(r == c, two, 0.0), axis=0, keepdims=True)
        ref[pl.ds(at, 8), :] = jnp.broadcast_to(line, (8, lanes))
        at += 8
    if blocks % 2:
        ref[pl.ds(at, lanes), :] = block(blocks - 1, blocks - 1)


def get_sym(ref, at, width):
    blocks = width // lanes
    got = {}
    for i in range(blocks):
        for j in range(i):
            got[i, j] = ref[pl.ds(at, lanes), :]
            got[j, i] = got[i, j].T
            at += lanes
    r, c = tri()
    for i in range(0, blocks - 1, 2):
        both = ref[pl.ds(at, lanes), :]
        turned = both.T
        at += lanes
        line = ref[pl.ds(at, 8), :][0:1, :]
        at += 8
        got[i, i] = jnp.where(r >= c, both, turned)
        got[i + 1, i + 1] = jnp.where(r == c, line, jnp.where(r < c, both, turned))
    if blocks % 2:
        got[blocks - 1, blocks - 1] = ref[pl.ds(at, lanes), :]
    return jnp.concatenate(
        [jnp.concatenate([got[i, j] for j in range(blocks)], axis=1) for i in range(blocks)], axis=0
    )


def put_full(ref, at, mat):
    width = mat.shape[0]
    for j in range(width // lanes):
        ref[pl.ds(at + j * width, width), :] = mat[:, j * lanes : (j + 1) * lanes]


def get_full(ref, at, width):
    return jnp.concatenate(
        [ref[pl.ds(at + j * width, width), :] for j in range(width // lanes)], axis=1
    )


def parts_of(mat):
    high = mat.astype(bf16)
    return high, (mat - high.astype(f32)).astype(bf16)


def times(left, right, turned=False):
    dims = (((1,), (1 if turned else 0,)), ((), ()))
    dot = lambda a, b: lax.dot_general(a, b, dims, preferred_element_type=f32)
    return dot(left[0], right[0]) + (dot(left[0], right[1]) + dot(left[1], right[0]))


def long_left(parts):
    high, low = parts
    return jnp.concatenate([high, high, low], axis=1)


def long_right(parts, turned=False):
    high, low = parts
    return jnp.concatenate([high, low, high], axis=1 if turned else 0)


def long_times(left, right, turned=False):
    dims = (((1,), (1 if turned else 0,)), ((), ()))
    return lax.dot_general(left, right, dims, preferred_element_type=f32)


def symmetric_times(left, right):
    high, low = left
    width = high.shape[0]
    most = width // (2 * lanes) * (2 * lanes)

    def part(rows, columns):
        both = long_times(jnp.concatenate([high[rows], low[rows]], axis=0), right[0][columns], True)
        count = both.shape[0] // 2
        return (both[:count] + both[count:]) + long_times(high[rows], right[1][columns], True)

    wide = part(slice(0, width), slice(0, most))
    if most == width:
        return wide
    rest = part(slice(most, width), slice(most, width))
    return jnp.concatenate([wide, jnp.concatenate([wide[most:].T, rest], axis=0)], axis=1)


def beside(left, right):
    return tuple(jnp.concatenate(pair, axis=1) for pair in zip(left, right))


def set_state(sh, sl, aa, ba, bb):
    width = aa.shape[0]
    first, second = slice(0, width), slice(width, 2 * width)
    for rows, columns, mat in ((first, first, aa), (second, first, ba), (first, second, ba.T), (second, second, bb)):
        sh[rows, columns], sl[rows, columns] = parts_of(mat)


def eliminate(node, sh, sl):
    diag, g_mat, h_mat = node
    left = parts_of(jnp.concatenate([g_mat, h_mat], axis=1))
    passed = -times(left, (sh[...], sl[...]))
    return passed, diag - symmetric_times(left, parts_of(passed))


def place_now(length):
    return lax.rem(lax.axis_index(axis) + row_offset, length)


def fetch(sems, *pairs):
    copies = [pltpu.make_async_copy(source, target, sems.at[i]) for i, (source, target) in enumerate(pairs)]
    for copy in copies:
        copy.start()
    for copy in copies:
        copy.wait()


def own_kernel(inv_ref, low_ref, up_ref, sym_ref, g_ref, node_ref, rooms, lines, sems, out_sems):
    width = inv_ref.shape[1]
    ps, pf = sym_rows(width), full_rows(width)
    loads = [
        pltpu.make_async_copy(ref.at[0], rooms.at[i], sems.at[i]) for i, ref in enumerate((inv_ref, low_ref, up_ref))
    ]
    for load in loads:
        load.start()
    stores = []

    def store(at, rows, *refs):
        where = pl.ds(at, rows)
        for ref in refs:
            target = ref.at[where, :] if ref is node_ref else ref
            stores.append(pltpu.make_async_copy(lines.at[where, :], target, out_sems.at[len(stores)]))
            stores[-1].start()

    loads[0].wait()
    inverse = rooms[0]
    put_sym(lines, 0, inverse)
    store(0, ps, sym_ref, node_ref)
    inv_parts = parts_of(inverse)
    loads[1].wait()
    put_full(lines, ps, times(inv_parts, parts_of(rooms[1])))
    store(ps, pf, g_ref, node_ref)
    loads[2].wait()
    up_high, up_low = parts_of(rooms[2])
    most = width // (2 * lanes) * (2 * lanes)
    for begin, end in ((0, most), (most, width)):
        if begin < end:
            product = times(inv_parts, (up_high[:, begin:end], up_low[:, begin:end]))
            for j in range(begin // lanes, end // lanes):
                lines[pl.ds(ps + pf + j * width, width), :] = product[:, j * lanes - begin : (j + 1) * lanes - begin]
            store(ps + pf + begin // lanes * width, (end - begin) // lanes * width, node_ref)
    for copy in stores:
        copy.wait()


def get_node(ref, width):
    ps, pf = sym_rows(width), full_rows(width)
    return get_sym(ref, 0, width), get_full(ref, ps, width), get_full(ref, ps + pf, width)


def put_state(ref, aa, ba, bb):
    ps = sym_rows(aa.shape[0])
    put_sym(ref, 0, aa)
    put_sym(ref, ps, bb)
    put_full(ref, 2 * ps, ba)


def roles_of(length):
    place = place_now(length)
    return place == 0, place == group, place == 2 * group, place == 3 * group


def ready_kernel(length, node, diag_ref, g_ref, high_ref, low_ref):
    width = diag_ref.shape[0]
    ps, pf = sym_rows(width), full_rows(width)
    at_zero, at_low, at_mid, at_high = roles_of(length)

    @pl.when(jnp.logical_or(jnp.logical_or(at_zero, at_low), jnp.logical_or(at_mid, at_high)))
    def _():
        diag_ref[...] = get_sym(node, 0, width)
        g_mat = get_full(node, ps, width)
        g_ref[...] = g_mat

        @pl.when(at_low)
        def _():
            high_ref[...], low_ref[...] = parts_of(get_full(node, ps + pf, width))

        @pl.when(jnp.logical_not(at_low))
        def _():
            high_ref[...], low_ref[...] = parts_of(g_mat)


def mid_kernel(length, node, diag, g_high, g_low, came_root, out, sym_ref):
    width = out.shape[1]
    ps = sym_rows(width)
    _, _, at_mid, _ = roles_of(length)

    @pl.when(jnp.logical_not(at_mid))
    def _():
        sym_ref[...] = node[pl.ds(0, ps), :]

    @pl.when(at_mid)
    def _():
        left = g_high[...], g_low[...]
        cross = -times(left, parts_of(get_sym(came_root, 0, width)))
        own = diag[...] - symmetric_times(left, parts_of(cross))
        put_sym(sym_ref, 0, own)
        out[0] = cross
        out[1] = own


def first_kernel(length, at_m, root_mid, came_node, kept, sh, sl, aa_ref, bb_ref):
    width = kept.shape[1]
    _, _, at_mid, _ = roles_of(length)

    @pl.when(at_mid)
    def _():
        mid_cross, mid = at_m[0], at_m[1]
        kept[0], kept[1] = mid, mid_cross
        set_state(sh, sl, get_sym(root_mid, 0, width), mid_cross, mid)
        passed, own = eliminate(get_node(came_node, width), sh, sl)
        put_sym(aa_ref, 0, own)
        put_sym(bb_ref, 0, mid)
        set_state(sh, sl, own, passed[:, width:].T, mid)


def second_kernel(
    length, diag, g_ref, high, low, came_d, came_g, came_sym, mid_high, _kept, _sh, _sl, _aa, came_bb, kept, sh, sl, aa_ref, bb_ref, own_ref
):
    width = kept.shape[1]
    ps = sym_rows(width)
    at_zero, at_low, at_mid, at_high = roles_of(length)

    @pl.when(at_mid)
    def _():
        own_ref[...] = came_bb[...]

    @pl.when(at_low)
    def _():
        h_parts = high[...], low[...]
        mid_both = jnp.concatenate([get_full(came_g, 0, width), get_sym(came_d, 0, width)], axis=1)
        both = times(h_parts, parts_of(mid_both))
        e_parts = parts_of(both[:, :width] - g_ref[...])
        root = get_sym(came_sym, 0, width)
        cross = times(e_parts, parts_of(root))
        own = diag[...] + symmetric_times(
            beside(parts_of(both[:, width:]), parts_of(cross)), beside(h_parts, e_parts)
        )
        aa_ref[...] = came_sym[...]
        put_sym(bb_ref, 0, own)
        own_ref[...] = bb_ref[...]
        set_state(sh, sl, root, cross, own)
        kept[0], kept[1] = own, cross

    def above(mid, own_diag, own_g):
        cross = -times(own_g, parts_of(mid))
        return cross, own_diag - symmetric_times(own_g, parts_of(cross))

    @pl.when(at_high)
    def _():
        mid = get_sym(mid_high, 0, width)
        cross, own = above(mid, diag[...], (high[...], low[...]))
        aa_ref[...] = mid_high[...]
        put_sym(bb_ref, 0, own)
        own_ref[...] = bb_ref[...]
        set_state(sh, sl, mid, cross, own)
        kept[0], kept[1] = own, cross

    @pl.when(at_zero)
    def _():
        high_g = parts_of(get_full(came_g, 0, width))
        _, own = above(get_sym(came_sym, 0, width), get_sym(came_d, 0, width), high_g)
        zeros = jnp.zeros((width, width), f32)
        put_sym(aa_ref, 0, own)
        bb_ref[...] = jnp.zeros((ps, lanes), f32)
        set_state(sh, sl, own, zeros, zeros)
        put_sym(own_ref, 0, diag[...])
        kept[0], kept[1] = diag[...], zeros


def state_kernel(aa_ref, ba_ref, bb_ref, own_ref, sh, sl, aa_out, bb_out, own_out):
    aa, bb = aa_ref[...], bb_ref[...]
    put_sym(aa_out, 0, aa)
    put_sym(bb_out, 0, bb)
    put_sym(own_out, 0, own_ref[...])
    set_state(sh, sl, aa, ba_ref[...], bb)


def four_for(length, fours, work):
    place = place_now(length)
    served = lax.rem(place, group) == 0
    if len(fours) == 1:
        pl.when(served)(lambda: work(fours[0]))
    else:
        at_mid = place == 2 * group
        pl.when(at_mid)(lambda: work(fours[1]))
        pl.when(jnp.logical_and(served, jnp.logical_not(at_mid)))(lambda: work(fours[0]))


def cross_kernel(length, sh, sl, *refs):
    fours, (low_ref, high_ref, passed_high, passed_low) = refs[:-4], refs[-4:]
    width = sh.shape[0] // 2

    def work(four):
        _, g_mat, h_mat = get_node(four, width)
        passed = -times(parts_of(jnp.concatenate([g_mat, h_mat], axis=1)), (sh[...], sl[...]))
        put_full(low_ref, 0, passed[:, :width])
        put_full(high_ref, 0, passed[:, width:].T)
        passed_high[...], passed_low[...] = parts_of(passed)

    four_for(length, fours, work)


def ends_kernel(length, passed_high, passed_low, aa_ref, bb_ref, cross_ref, *refs):
    fours, (low_ends, high_ends, mid_ref, high_ref) = refs[:-4], refs[-4:]
    ps = mid_ref.shape[0]
    width = passed_high.shape[0]

    def work(four):
        diag, g_mat, h_mat = get_node(four, width)
        left = parts_of(jnp.concatenate([g_mat, h_mat], axis=1))
        put_sym(mid_ref, 0, diag - symmetric_times(left, (passed_high[...], passed_low[...])))
        for ref, at in ((low_ends, ps), (high_ends, 0), (high_ref, 0)):
            ref[pl.ds(at, ps), :] = mid_ref[...]
        low_ends[pl.ds(0, ps), :] = aa_ref[...]
        high_ends[pl.ds(ps, ps), :] = bb_ref[...]
        high_ref[pl.ds(ps, ps), :] = bb_ref[...]
        high_ref[pl.ds(2 * ps, cross_ref.shape[0]), :] = cross_ref[...]

    four_for(length, fours, work)


def offset_of(length):
    return lax.rem(place_now(length), group)


def near_kernel(length, late, node, *refs):
    f_high, f_low, rest_ref = refs[-3:]
    width = rest_ref.shape[0]
    offset = offset_of(length)
    turn = lax.rem(offset, group // 2)
    first, second = slice(0, width), slice(width, 2 * width)

    def put(rows, columns, mat):
        f_high[rows, columns], f_low[rows, columns] = parts_of(mat)

    def odd(below, two):
        d_own, g_own, h_own = get_node(node, width)
        d_two, g_two, h_two = get_node(two, width)
        inward, outward = (h_own, g_own) if below else (g_own, h_own)
        inward = parts_of(inward)
        to_low, to_high = times(inward, parts_of(g_two)), times(inward, parts_of(h_two))
        put(first, first, to_low - outward if below else to_low)
        put(first, second, to_high if below else to_high - outward)
        link = -times(inward, parts_of(d_two))
        rest_ref[:, first] = d_own - times(inward, parts_of(link), True)
        if not below:
            put(second, first, -g_two)
            put(second, second, -h_two)
            rest_ref[:, second] = link

    if late:
        pl.when(offset == group - 1)(lambda: odd(False, refs[0]))
        return
    came_near, came_far = refs[:2]
    pl.when(turn == 1)(lambda: odd(True, came_near))
    pl.when(offset == 3)(lambda: odd(False, came_far))

    @pl.when(turn == 2)
    def _():
        d_own, g_own, h_own = get_node(node, width)
        put(first, first, -g_own)
        put(first, second, -h_own)
        rest_ref[:, first] = d_own


def choose_kernel(length, first, third, fifth, *refs):
    out_ref = refs[-1]
    offset = offset_of(length)
    refs = iter(refs)
    for at, count in ((1, first), (3, third), (5, fifth)):
        parts = [next(refs) for _ in range(count)]

        @pl.when(offset == at)
        def _(parts=parts):
            begin = 0
            for part in parts:
                rows = part.shape[0]
                out_ref[pl.ds(begin, rows), :] = part[...]
                begin += rows


def lower_kernel(length, parity, early, late, seven, fh, fl, rest, kept, *refs):
    diag_ref, cross_ref, diag_out, cross_out, sh, sl, sems = refs[-7:]
    width = rest.shape[0]
    ps = sym_rows(width)
    offset = offset_of(length)
    turn = lax.rem(offset, group // 2)
    first, second = slice(0, width), slice(width, 2 * width)
    diag_copy = pltpu.make_async_copy(diag_out, diag_ref.at[0], sems.at[0])
    cross_copy = pltpu.make_async_copy(cross_out, cross_ref.at[0], sems.at[1])

    def finish():
        diag_copy.start()
        diag_copy.wait()
        cross_copy.wait()

    def load(ends, cross, at=0):
        set_state(sh, sl, get_sym(ends, 0, width), get_full(cross, at, width), get_sym(ends, ps, width))

    pl.when(jnp.logical_and(turn == (1 if parity else 2), offset < 3))(lambda: load(early, late))
    pl.when(jnp.logical_and(turn == (1 if parity else 2), offset > 4))(lambda: load(late, early))

    def passed_on():
        return times((fh[first, :], fl[first, :]), (sh[...], sl[...]))

    @pl.when(turn == (1 if parity else 2))
    def _():
        passed = passed_on()
        cross_out[...] = passed[:, first]
        cross_copy.start()
        diag_out[...] = rest[:, first] + symmetric_times(parts_of(passed), (fh[first, :], fl[first, :]))
        finish()

    if parity == 0:

        @pl.when(offset == group // 2)
        def _():
            cross_out[...] = get_full(early, 0, width)
            cross_copy.start()
            diag_out[...] = get_sym(late, ps, width)
            finish()

    else:

        pl.when(offset == 3)(lambda: load(late, early))
        pl.when(offset == group - 1)(lambda: load(seven, seven, 2 * ps))

        @pl.when(turn == 3)
        def _():
            left = long_left(parts_of(passed_on()))
            whole = long_times(left, long_right((fh[...], fl[...]), True), True) + rest[...]
            diag_out[...], cross_out[...] = whole[:, first], whole[:, second]
            cross_copy.start()
            finish()

        @pl.when(offset == 0)
        def _():
            diag_out[...], cross_out[...] = kept[0], kept[1]
            cross_copy.start()
            finish()


def sent(array, length, *moves):
    device = lambda position: (position - row_offset) % length
    pairs = [(device(p), device(p + by)) for by, wanted in moves for p in range(length) if wanted(p)]
    return lax.ppermute(array, axis, pairs)


def upper_levels(inverse, lowers, uppers, length):
    width = inverse.shape[0]
    place = (lax.axis_index(axis) + row_offset) % length
    product = functools.partial(jnp.dot, precision=lax.Precision.HIGHEST, preferred_element_type=f32)
    node_g, node_h = product(inverse, lowers), product(inverse, uppers)
    everywhere = lambda p: True
    zeros = jnp.zeros((width, width), f32)
    sigma = jnp.where(place == 0, inverse, zeros)
    low_own, high_own, cross = zeros, zeros, zeros
    stride = length // 2
    while stride >= group:
        from_low, owned_high = (sent(x, length, (stride, everywhere)) for x in (sigma, high_own))
        from_high, owned_low = (sent(x, length, (-stride, everywhere)) for x in (sigma, low_own))
        has_upper = place + stride < length
        sigma_high = jnp.where(has_upper, from_high, zeros)
        sigma_ba = jnp.where(has_upper, owned_high.T + owned_low, zeros)
        active = place % (2 * stride) == stride
        low = -(product(node_g, from_low) + product(node_h, sigma_ba))
        high = -(product(node_g, sigma_ba.T) + product(node_h, sigma_high))
        own = inverse - product(node_g, low.T) - product(node_h, high.T)
        sigma = jnp.where(active, own, sigma)
        low_own = jnp.where(active, low, zeros)
        high_own = jnp.where(active, high, zeros)
        cross = jnp.where(active, low, cross)
        stride //= 2
    newest = lambda p: p % (2 * group) == group
    below_aa, below_ba, below_bb = (sent(x, length, (group, newest)) for x in (sigma, high_own.T, sigma_high))
    return sigma, cross, tuple(
        jnp.where(active, *pair) for pair in ((from_low, below_aa), (low_own, below_ba), (sigma, below_bb))
    )


def body(inv_diag, low_coupling, up_coupling):
    width = inv_diag.shape[1]
    length = lax.axis_size(axis)
    span = 4 * group
    is_open = length == span
    ps, pf = sym_rows(width), full_rows(width)
    node_rows, state_rows = ps + 2 * pf, 2 * ps + pf
    rows_of = lambda rows: jax.ShapeDtypeStruct((rows, lanes), f32)
    square = (width, width)
    whole = jax.ShapeDtypeStruct((1,) + square, f32)
    vmem, anywhere = pl.BlockSpec(memory_space=pltpu.VMEM), pl.BlockSpec(memory_space=pl.ANY)
    room = lambda *shape, kind=f32: pltpu.VMEM(shape, kind)
    sems = pltpu.SemaphoreType.DMA((4,))
    run = lambda kernel, mib, flops=1, **more: pl.pallas_call(
        kernel, compiler_params=pltpu.CompilerParams(vmem_limit_bytes=mib * 2**20),
        cost_estimate=pl.CostEstimate(flops=flops, bytes_accessed=1, transcendentals=0), **more
    )
    at = lambda turn: (lambda p: p % span == turn)
    inner = lambda offset: (lambda p: p % group == offset)
    mid, half = 2 * group, group // 2

    sym, g_only, node = run(
        own_kernel, 60, out_shape=(rows_of(ps), rows_of(pf), rows_of(node_rows)),
        in_specs=[anywhere] * 3, out_specs=[anywhere] * 3,
        scratch_shapes=[room(3, *square), room(node_rows, lanes), sems, pltpu.SemaphoreType.DMA((6,))], name="own",
    )(inv_diag, low_coupling, up_coupling)

    close = ((-1, inner(2)), (-1, inner(6)))
    away = ((1, inner(2)), (group // 2, inner(6)))
    half_state = (jax.ShapeDtypeStruct((2 * width, 2 * width), bf16),) * 2 + (rows_of(ps),) * 2
    if is_open:
        to_mid = lambda p: p == mid - half
        came_far = sent(
            node, length, (half, lambda p: inner(half)(p) and not to_mid(p)), (group, at(group)), *away
        )
        came_near = sent(node, length, (half, to_mid), *close)
        came_g = sent(g_only, length, (-group, at(mid)), (group, at(3 * group)))
        came_d = sent(sym, length, (mid, at(0)), (-group, at(mid)), (group, at(3 * group)))
        two = jax.ShapeDtypeStruct((2,) + square, f32)
        one = jax.ShapeDtypeStruct(square, f32)
        ready = run(
            functools.partial(ready_kernel, length), 16,
            out_shape=(one, one) + (jax.ShapeDtypeStruct(square, bf16),) * 2,
            in_specs=[vmem], out_specs=[vmem] * 4, name="ready",
        )(node)
        at_m, mid_sym = run(
            functools.partial(mid_kernel, length), 16, 4 * 10**9, out_shape=(two, rows_of(ps)),
            in_specs=[vmem] * 5, out_specs=[vmem] * 2, name="middle",
        )(node, ready[0], *ready[2:], came_d)
        came_sym = sent(mid_sym, length, (mid, at(mid)), (group, at(0)))
        mid_high = sent(mid_sym, length, (group, at(mid)))
        made = run(
            functools.partial(first_kernel, length), 16, out_shape=(two,) + half_state,
            in_specs=[vmem] * 3, out_specs=[vmem] * 5, name="first",
        )(at_m, came_d, came_far)
        kept, *ends, ended = run(
            functools.partial(second_kernel, length), 16, 5 * 10**9, out_shape=(two,) + half_state + (rows_of(ps),),
            in_specs=[vmem] * 13, out_specs=[vmem] * 6,
            input_output_aliases={8 + i: i for i in range(5)}, name="second",
        )(*ready, came_d, came_g, came_sym, mid_high, *made)
        fours = (came_far, came_near)
    else:
        came_far = sent(node, length, (half, inner(half)), *away)
        came_near = sent(node, length, *close)
        diag, cross, below = upper_levels(inv_diag[0], low_coupling[0], up_coupling[0], length)
        kept = jnp.stack([diag, cross])
        *ends, ended = run(
            state_kernel, 16, out_shape=half_state + (rows_of(ps),), in_specs=[vmem] * 4, out_specs=[vmem] * 5,
            name="state",
        )(*below, diag)
        fours = (came_far,)
    one_end = sent(ended, length, (1, inner(0)))
    served = len(fours)
    low_cross, high_cross, *passed = run(
        functools.partial(cross_kernel, length), 16,
        out_shape=(rows_of(pf),) * 2 + (jax.ShapeDtypeStruct((width, 2 * width), bf16),) * 2,
        in_specs=[vmem] * (2 + served), out_specs=[vmem] * 4, name="halve",
    )(*ends[:2], *fours)
    three_cross = sent(low_cross, length, (-5, inner(0)))
    five_cross = sent(high_cross, length, (-3, inner(0)))
    low_ends, high_ends, half_mid, high_half = run(
        functools.partial(ends_kernel, length), 16,
        out_shape=(rows_of(2 * ps),) * 2 + (rows_of(ps), rows_of(state_rows)),
        in_specs=[vmem] * (5 + served), out_specs=[vmem] * 4, name="halves",
    )(*passed, *ends[2:], high_cross, *fours)
    five_ends = sent(high_ends, length, (-3, inner(0)))
    one_mid = sent(half_mid, length, (-7, inner(0)))
    three_ends = sent(low_ends, length, (-5, inner(0)))
    shapes = (jax.ShapeDtypeStruct((2 * width, 2 * width), bf16),) * 2 + (jax.ShapeDtypeStruct((width, 2 * width), f32),)
    composed = run(
        functools.partial(near_kernel, length, False), 16, 4 * 10**9, out_shape=shapes,
        in_specs=[vmem] * 3 + [anywhere], out_specs=[vmem] * 3, name="near",
    )(node, came_near, came_far, one_end)
    by_three, _ = lax.optimization_barrier((three_cross, composed[2]))
    one_cross = sent(by_three, length, (-2, inner(3)))
    to_seven = sent(high_half, length, (-1, inner(0)))
    later, _ = lax.optimization_barrier((came_far, three_cross))
    came_back = sent(later, length, (-3, inner(2)))

    f_high, f_low, rest = run(
        functools.partial(near_kernel, length, True), 16, out_shape=shapes,
        in_specs=[vmem] * 2 + [vmem] * 3, out_specs=[vmem] * 3, name="back",
        input_output_aliases={2: 0, 3: 1, 4: 2},
    )(node, came_back, *composed)

    def chosen(name, flops, *groups, after=()):
        return run(
            functools.partial(choose_kernel, length, *map(len, groups)), 16, flops,
            out_shape=rows_of(2 * ps), in_specs=[vmem] * sum(map(len, groups)) + [anywhere] * len(after),
            out_specs=vmem, name=name,
        )(*(array for arrays in groups for array in arrays), *after)

    early = chosen("early", 1, (one_end, one_mid), (three_cross,), (five_cross,), after=(composed[2],))
    late = chosen("late", 4 * 10**9, (one_cross,), (three_ends,), (five_ends,), after=(early,))
    early_next, late_next = (sent(x, length, (1, inner(1)), (1, inner(3)), (1, inner(5))) for x in (early, late))

    outputs = ()
    for parity, came in ((1, (early, late)), (0, (early_next, late_next))):
        outputs = run(
            functools.partial(lower_kernel, length, parity), 20,
            out_shape=(whole, whole), in_specs=[vmem] * 7 + [anywhere] * len(outputs), out_specs=[anywhere] * 2,
            scratch_shapes=[room(*square)] * 2 + [room(2 * width, 2 * width, kind=bf16)] * 2 + [sems],
            input_output_aliases={7 + i: i for i in range(len(outputs))}, name="lower",
        )(*came, to_seven, f_high, f_low, rest, kept, *outputs)
    return outputs


def solution(mesh):
    placed = (P(axis, None, None),) * 3
    return jax.shard_map(
        body, mesh=mesh, in_specs=placed, out_specs=placed[:2], check_vma=False
    )
```

```python
import functools

import jax
import jax.numpy as jnp
from jax import lax
from jax.experimental import pallas as pl
from jax.experimental.pallas import tpu as pltpu
from jax.sharding import PartitionSpec as P

row_offset = 3
lanes = 128
group = 8
axis = "tm"
bf16 = jnp.bfloat16
f32 = jnp.float32


def sym_rows(width):
    blocks = width // lanes
    pairs = blocks // 2
    return (blocks * (blocks - 1) // 2 + blocks - pairs) * lanes + 8 * pairs


def full_rows(width):
    return width * (width // lanes)


def tri():
    r = lax.broadcasted_iota(jnp.int32, (lanes, lanes), 0)
    c = lax.broadcasted_iota(jnp.int32, (lanes, lanes), 1)
    return r, c


def put_sym(ref, at, mat):
    blocks = mat.shape[0] // lanes
    block = lambda i, j: mat[i * lanes : (i + 1) * lanes, j * lanes : (j + 1) * lanes]
    for i in range(blocks):
        for j in range(i):
            ref[pl.ds(at, lanes), :] = block(i, j)
            at += lanes
    r, c = tri()
    for i in range(0, blocks - 1, 2):
        one, two = block(i, i), block(i + 1, i + 1)
        ref[pl.ds(at, lanes), :] = jnp.where(r >= c, one, two)
        at += lanes
        line = jnp.sum(jnp.where(r == c, two, 0.0), axis=0, keepdims=True)
        ref[pl.ds(at, 8), :] = jnp.broadcast_to(line, (8, lanes))
        at += 8
    if blocks % 2:
        ref[pl.ds(at, lanes), :] = block(blocks - 1, blocks - 1)


def get_sym(ref, at, width):
    blocks = width // lanes
    got = {}
    for i in range(blocks):
        for j in range(i):
            got[i, j] = ref[pl.ds(at, lanes), :]
            got[j, i] = got[i, j].T
            at += lanes
    r, c = tri()
    for i in range(0, blocks - 1, 2):
        both = ref[pl.ds(at, lanes), :]
        turned = both.T
        at += lanes
        line = ref[pl.ds(at, 8), :][0:1, :]
        at += 8
        got[i, i] = jnp.where(r >= c, both, turned)
        got[i + 1, i + 1] = jnp.where(r == c, line, jnp.where(r < c, both, turned))
    if blocks % 2:
        got[blocks - 1, blocks - 1] = ref[pl.ds(at, lanes), :]
    return jnp.concatenate(
        [jnp.concatenate([got[i, j] for j in range(blocks)], axis=1) for i in range(blocks)], axis=0
    )


def put_full(ref, at, mat):
    width = mat.shape[0]
    for j in range(width // lanes):
        ref[pl.ds(at + j * width, width), :] = mat[:, j * lanes : (j + 1) * lanes]


def get_full(ref, at, width):
    return jnp.concatenate(
        [ref[pl.ds(at + j * width, width), :] for j in range(width // lanes)], axis=1
    )


def parts_of(mat):
    high = mat.astype(bf16)
    return high, (mat - high.astype(f32)).astype(bf16)


def times(left, right, turned=False):
    dims = (((1,), (1 if turned else 0,)), ((), ()))
    dot = lambda a, b: lax.dot_general(a, b, dims, preferred_element_type=f32)
    return dot(left[0], right[0]) + (dot(left[0], right[1]) + dot(left[1], right[0]))


def long_left(parts):
    high, low = parts
    return jnp.concatenate([high, high, low], axis=1)


def long_right(parts, turned=False):
    high, low = parts
    return jnp.concatenate([high, low, high], axis=1 if turned else 0)


def long_times(left, right, turned=False):
    dims = (((1,), (1 if turned else 0,)), ((), ()))
    return lax.dot_general(left, right, dims, preferred_element_type=f32)


def symmetric_times(left, right):
    high, low = left
    width = high.shape[0]
    most = width // (2 * lanes) * (2 * lanes)

    def part(rows, columns):
        both = long_times(jnp.concatenate([high[rows], low[rows]], axis=0), right[0][columns], True)
        count = both.shape[0] // 2
        return (both[:count] + both[count:]) + long_times(high[rows], right[1][columns], True)

    wide = part(slice(0, width), slice(0, most))
    if most == width:
        return wide
    rest = part(slice(most, width), slice(most, width))
    return jnp.concatenate([wide, jnp.concatenate([wide[most:].T, rest], axis=0)], axis=1)


def beside(left, right):
    return tuple(jnp.concatenate(pair, axis=1) for pair in zip(left, right))


def set_state(sh, sl, aa, ba, bb):
    width = aa.shape[0]
    first, second = slice(0, width), slice(width, 2 * width)
    for rows, columns, mat in ((first, first, aa), (second, first, ba), (first, second, ba.T), (second, second, bb)):
        sh[rows, columns], sl[rows, columns] = parts_of(mat)


def eliminate(node, sh, sl):
    diag, g_mat, h_mat = node
    left = parts_of(jnp.concatenate([g_mat, h_mat], axis=1))
    passed = -times(left, (sh[...], sl[...]))
    return passed, diag - symmetric_times(left, parts_of(passed))


def place_now(length):
    return lax.rem(lax.axis_index(axis) + row_offset, length)


def fetch(sems, *pairs):
    copies = [pltpu.make_async_copy(source, target, sems.at[i]) for i, (source, target) in enumerate(pairs)]
    for copy in copies:
        copy.start()
    for copy in copies:
        copy.wait()


def own_kernel(inv_ref, low_ref, up_ref, sym_ref, g_ref, node_ref, rooms, lines, sems, out_sems):
    width = inv_ref.shape[1]
    ps, pf = sym_rows(width), full_rows(width)
    loads = [
        pltpu.make_async_copy(ref.at[0], rooms.at[i], sems.at[i]) for i, ref in enumerate((inv_ref, low_ref, up_ref))
    ]
    for load in loads:
        load.start()
    stores = []

    def store(at, rows, *refs):
        where = pl.ds(at, rows)
        for ref in refs:
            target = ref.at[where, :] if ref is node_ref else ref
            stores.append(pltpu.make_async_copy(lines.at[where, :], target, out_sems.at[len(stores)]))
            stores[-1].start()

    loads[0].wait()
    inverse = rooms[0]
    put_sym(lines, 0, inverse)
    store(0, ps, sym_ref, node_ref)
    inv_parts = parts_of(inverse)
    loads[1].wait()
    put_full(lines, ps, times(inv_parts, parts_of(rooms[1])))
    store(ps, pf, g_ref, node_ref)
    loads[2].wait()
    up_high, up_low = parts_of(rooms[2])
    most = width // (2 * lanes) * (2 * lanes)
    for begin, end in ((0, most), (most, width)):
        if begin < end:
            product = times(inv_parts, (up_high[:, begin:end], up_low[:, begin:end]))
            for j in range(begin // lanes, end // lanes):
                lines[pl.ds(ps + pf + j * width, width), :] = product[:, j * lanes - begin : (j + 1) * lanes - begin]
            store(ps + pf + begin // lanes * width, (end - begin) // lanes * width, node_ref)
    for copy in stores:
        copy.wait()


def get_node(ref, width):
    ps, pf = sym_rows(width), full_rows(width)
    return get_sym(ref, 0, width), get_full(ref, ps, width), get_full(ref, ps + pf, width)


def put_state(ref, aa, ba, bb):
    ps = sym_rows(aa.shape[0])
    put_sym(ref, 0, aa)
    put_sym(ref, ps, bb)
    put_full(ref, 2 * ps, ba)


def roles_of(length):
    place = place_now(length)
    return place == 0, place == group, place == 2 * group, place == 3 * group


def ready_kernel(length, node, diag_ref, g_ref, high_ref, low_ref):
    width = diag_ref.shape[0]
    ps, pf = sym_rows(width), full_rows(width)
    at_zero, at_low, at_mid, at_high = roles_of(length)

    @pl.when(jnp.logical_or(jnp.logical_or(at_zero, at_low), jnp.logical_or(at_mid, at_high)))
    def _():
        diag_ref[...] = get_sym(node, 0, width)
        g_mat = get_full(node, ps, width)
        g_ref[...] = g_mat

        @pl.when(at_low)
        def _():
            high_ref[...], low_ref[...] = parts_of(get_full(node, ps + pf, width))

        @pl.when(jnp.logical_not(at_low))
        def _():
            high_ref[...], low_ref[...] = parts_of(g_mat)


def mid_kernel(length, node, diag, g_high, g_low, came_root, out, sym_ref):
    width = out.shape[1]
    ps = sym_rows(width)
    _, _, at_mid, _ = roles_of(length)

    @pl.when(jnp.logical_not(at_mid))
    def _():
        sym_ref[...] = node[pl.ds(0, ps), :]

    @pl.when(at_mid)
    def _():
        left = g_high[...], g_low[...]
        cross = -times(left, parts_of(get_sym(came_root, 0, width)))
        own = diag[...] - symmetric_times(left, parts_of(cross))
        put_sym(sym_ref, 0, own)
        out[0] = cross
        out[1] = own


def first_kernel(length, at_m, root_mid, came_node, kept, sh, sl, aa_ref, bb_ref):
    width = kept.shape[1]
    _, _, at_mid, _ = roles_of(length)

    @pl.when(at_mid)
    def _():
        mid_cross, mid = at_m[0], at_m[1]
        kept[0], kept[1] = mid, mid_cross
        set_state(sh, sl, get_sym(root_mid, 0, width), mid_cross, mid)
        passed, own = eliminate(get_node(came_node, width), sh, sl)
        put_sym(aa_ref, 0, own)
        put_sym(bb_ref, 0, mid)
        set_state(sh, sl, own, passed[:, width:].T, mid)


def second_kernel(
    length, diag, g_ref, high, low, came_d, came_g, came_sym, mid_high, came_kept, came_sh, came_sl, came_aa, came_bb, kept, sh, sl, aa_ref, bb_ref, own_ref
):
    width = kept.shape[1]
    ps = sym_rows(width)
    at_zero, at_low, at_mid, at_high = roles_of(length)

    @pl.when(at_mid)
    def _():
        own_ref[...] = came_bb[...]
        for ref, came in ((kept, came_kept), (sh, came_sh), (sl, came_sl), (aa_ref, came_aa), (bb_ref, came_bb)):
            ref[...] = came[...]

    @pl.when(at_low)
    def _():
        h_parts = high[...], low[...]
        mid_both = jnp.concatenate([get_full(came_g, 0, width), get_sym(came_d, 0, width)], axis=1)
        both = times(h_parts, parts_of(mid_both))
        e_parts = parts_of(both[:, :width] - g_ref[...])
        root = get_sym(came_sym, 0, width)
        cross = times(e_parts, parts_of(root))
        own = diag[...] + symmetric_times(
            beside(parts_of(both[:, width:]), parts_of(cross)), beside(h_parts, e_parts)
        )
        aa_ref[...] = came_sym[...]
        put_sym(bb_ref, 0, own)
        own_ref[...] = bb_ref[...]
        set_state(sh, sl, root, cross, own)
        kept[0], kept[1] = own, cross

    def above(mid, own_diag, own_g):
        cross = -times(own_g, parts_of(mid))
        return cross, own_diag - symmetric_times(own_g, parts_of(cross))

    @pl.when(at_high)
    def _():
        mid = get_sym(mid_high, 0, width)
        cross, own = above(mid, diag[...], (high[...], low[...]))
        aa_ref[...] = mid_high[...]
        put_sym(bb_ref, 0, own)
        own_ref[...] = bb_ref[...]
        set_state(sh, sl, mid, cross, own)
        kept[0], kept[1] = own, cross

    @pl.when(at_zero)
    def _():
        high_g = parts_of(get_full(came_g, 0, width))
        _, own = above(get_sym(came_sym, 0, width), get_sym(came_d, 0, width), high_g)
        zeros = jnp.zeros((width, width), f32)
        put_sym(aa_ref, 0, own)
        bb_ref[...] = jnp.zeros((ps, lanes), f32)
        set_state(sh, sl, own, zeros, zeros)
        put_sym(own_ref, 0, diag[...])
        kept[0], kept[1] = diag[...], zeros


def state_kernel(aa_ref, ba_ref, bb_ref, own_ref, sh, sl, aa_out, bb_out, own_out):
    aa, bb = aa_ref[...], bb_ref[...]
    put_sym(aa_out, 0, aa)
    put_sym(bb_out, 0, bb)
    put_sym(own_out, 0, own_ref[...])
    set_state(sh, sl, aa, ba_ref[...], bb)


def four_for(length, fours, work):
    place = place_now(length)
    served = lax.rem(place, group) == 0
    if len(fours) == 1:
        pl.when(served)(lambda: work(fours[0]))
    else:
        at_mid = place == 2 * group
        pl.when(at_mid)(lambda: work(fours[1]))
        pl.when(jnp.logical_and(served, jnp.logical_not(at_mid)))(lambda: work(fours[0]))


def cross_kernel(length, sh, sl, *refs):
    fours, (low_ref, high_ref, passed_high, passed_low) = refs[:-4], refs[-4:]
    width = sh.shape[0] // 2

    def work(four):
        _, g_mat, h_mat = get_node(four, width)
        passed = -times(parts_of(jnp.concatenate([g_mat, h_mat], axis=1)), (sh[...], sl[...]))
        put_full(low_ref, 0, passed[:, :width])
        put_full(high_ref, 0, passed[:, width:].T)
        passed_high[...], passed_low[...] = parts_of(passed)

    four_for(length, fours, work)


def ends_kernel(length, passed_high, passed_low, aa_ref, bb_ref, cross_ref, *refs):
    fours, (low_ends, high_ends, mid_ref, high_ref) = refs[:-4], refs[-4:]
    ps = mid_ref.shape[0]
    width = passed_high.shape[0]

    def work(four):
        diag, g_mat, h_mat = get_node(four, width)
        left = parts_of(jnp.concatenate([g_mat, h_mat], axis=1))
        put_sym(mid_ref, 0, diag - symmetric_times(left, (passed_high[...], passed_low[...])))
        for ref, at in ((low_ends, ps), (high_ends, 0), (high_ref, 0)):
            ref[pl.ds(at, ps), :] = mid_ref[...]
        low_ends[pl.ds(0, ps), :] = aa_ref[...]
        high_ends[pl.ds(ps, ps), :] = bb_ref[...]
        high_ref[pl.ds(ps, ps), :] = bb_ref[...]
        high_ref[pl.ds(2 * ps, cross_ref.shape[0]), :] = cross_ref[...]

    four_for(length, fours, work)


def offset_of(length):
    return lax.rem(place_now(length), group)


def near_kernel(length, late, node, *refs):
    f_high, f_low, rest_ref = refs[-3:]
    width = rest_ref.shape[0]
    offset = offset_of(length)
    turn = lax.rem(offset, group // 2)
    first, second = slice(0, width), slice(width, 2 * width)

    def put(rows, columns, mat):
        f_high[rows, columns], f_low[rows, columns] = parts_of(mat)

    def odd(below, two):
        d_own, g_own, h_own = get_node(node, width)
        d_two, g_two, h_two = get_node(two, width)
        inward, outward = (h_own, g_own) if below else (g_own, h_own)
        inward = parts_of(inward)
        to_low, to_high = times(inward, parts_of(g_two)), times(inward, parts_of(h_two))
        put(first, first, to_low - outward if below else to_low)
        put(first, second, to_high if below else to_high - outward)
        link = -times(inward, parts_of(d_two))
        rest_ref[:, first] = d_own - times(inward, parts_of(link), True)
        if not below:
            put(second, first, -g_two)
            put(second, second, -h_two)
            rest_ref[:, second] = link

    if late:
        pl.when(offset == group - 1)(lambda: odd(False, refs[0]))

        @pl.when(offset != group - 1)
        def _():
            for ref, came in zip(refs[-3:], refs[1:4]):
                ref[...] = came[...]

        return
    came_near, came_far = refs[:2]
    pl.when(turn == 1)(lambda: odd(True, came_near))
    pl.when(offset == 3)(lambda: odd(False, came_far))

    @pl.when(turn == 2)
    def _():
        d_own, g_own, h_own = get_node(node, width)
        put(first, first, -g_own)
        put(first, second, -h_own)
        rest_ref[:, first] = d_own


def choose_kernel(length, first, third, fifth, *refs):
    out_ref = refs[-1]
    offset = offset_of(length)
    refs = iter(refs)
    for at, count in ((1, first), (3, third), (5, fifth)):
        parts = [next(refs) for _ in range(count)]

        @pl.when(offset == at)
        def _(parts=parts):
            begin = 0
            for part in parts:
                rows = part.shape[0]
                out_ref[pl.ds(begin, rows), :] = part[...]
                begin += rows


def lower_kernel(length, parity, early, late, seven, fh, fl, rest, kept, *refs):
    diag_ref, cross_ref, diag_out, cross_out, sh, sl, sems = refs[-7:]
    width = rest.shape[0]
    ps = sym_rows(width)
    offset = offset_of(length)
    turn = lax.rem(offset, group // 2)
    first, second = slice(0, width), slice(width, 2 * width)
    diag_copy = pltpu.make_async_copy(diag_out, diag_ref.at[0], sems.at[0])
    cross_copy = pltpu.make_async_copy(cross_out, cross_ref.at[0], sems.at[1])

    def finish():
        diag_copy.start()
        diag_copy.wait()
        cross_copy.wait()

    def load(ends, cross, at=0):
        set_state(sh, sl, get_sym(ends, 0, width), get_full(cross, at, width), get_sym(ends, ps, width))

    pl.when(jnp.logical_and(turn == (1 if parity else 2), offset < 3))(lambda: load(early, late))
    pl.when(jnp.logical_and(turn == (1 if parity else 2), offset > 4))(lambda: load(late, early))

    def passed_on():
        return times((fh[first, :], fl[first, :]), (sh[...], sl[...]))

    @pl.when(turn == (1 if parity else 2))
    def _():
        passed = passed_on()
        cross_out[...] = passed[:, first]
        cross_copy.start()
        diag_out[...] = rest[:, first] + symmetric_times(parts_of(passed), (fh[first, :], fl[first, :]))
        finish()

    if parity == 0:

        @pl.when(offset == group // 2)
        def _():
            cross_out[...] = get_full(early, 0, width)
            cross_copy.start()
            diag_out[...] = get_sym(late, ps, width)
            finish()

    else:

        pl.when(offset == 3)(lambda: load(late, early))
        pl.when(offset == group - 1)(lambda: load(seven, seven, 2 * ps))

        @pl.when(turn == 3)
        def _():
            left = long_left(parts_of(passed_on()))
            whole = long_times(left, long_right((fh[...], fl[...]), True), True) + rest[...]
            diag_out[...], cross_out[...] = whole[:, first], whole[:, second]
            cross_copy.start()
            finish()

        @pl.when(offset == 0)
        def _():
            diag_out[...], cross_out[...] = kept[0], kept[1]
            cross_copy.start()
            finish()


def sent(array, length, *moves):
    device = lambda position: (position - row_offset) % length
    pairs = [(device(p), device(p + by)) for by, wanted in moves for p in range(length) if wanted(p)]
    return lax.ppermute(array, axis, pairs)


def upper_levels(inverse, lowers, uppers, length):
    width = inverse.shape[0]
    place = (lax.axis_index(axis) + row_offset) % length
    product = functools.partial(jnp.dot, precision=lax.Precision.HIGHEST, preferred_element_type=f32)
    node_g, node_h = product(inverse, lowers), product(inverse, uppers)
    everywhere = lambda p: True
    zeros = jnp.zeros((width, width), f32)
    sigma = jnp.where(place == 0, inverse, zeros)
    low_own, high_own, cross = zeros, zeros, zeros
    stride = length // 2
    while stride >= group:
        from_low, owned_high = (sent(x, length, (stride, everywhere)) for x in (sigma, high_own))
        from_high, owned_low = (sent(x, length, (-stride, everywhere)) for x in (sigma, low_own))
        has_upper = place + stride < length
        sigma_high = jnp.where(has_upper, from_high, zeros)
        sigma_ba = jnp.where(has_upper, owned_high.T + owned_low, zeros)
        active = place % (2 * stride) == stride
        low = -(product(node_g, from_low) + product(node_h, sigma_ba))
        high = -(product(node_g, sigma_ba.T) + product(node_h, sigma_high))
        own = inverse - product(node_g, low.T) - product(node_h, high.T)
        sigma = jnp.where(active, own, sigma)
        low_own = jnp.where(active, low, zeros)
        high_own = jnp.where(active, high, zeros)
        cross = jnp.where(active, low, cross)
        stride //= 2
    newest = lambda p: p % (2 * group) == group
    below_aa, below_ba, below_bb = (sent(x, length, (group, newest)) for x in (sigma, high_own.T, sigma_high))
    return sigma, cross, tuple(
        jnp.where(active, *pair) for pair in ((from_low, below_aa), (low_own, below_ba), (sigma, below_bb))
    )


def body(inv_diag, low_coupling, up_coupling):
    width = inv_diag.shape[1]
    length = lax.axis_size(axis)
    span = 4 * group
    is_open = length == span
    ps, pf = sym_rows(width), full_rows(width)
    node_rows, state_rows = ps + 2 * pf, 2 * ps + pf
    rows_of = lambda rows: jax.ShapeDtypeStruct((rows, lanes), f32)
    square = (width, width)
    whole = jax.ShapeDtypeStruct((1,) + square, f32)
    vmem, anywhere = pl.BlockSpec(memory_space=pltpu.VMEM), pl.BlockSpec(memory_space=pl.ANY)
    room = lambda *shape, kind=f32: pltpu.VMEM(shape, kind)
    sems = pltpu.SemaphoreType.DMA((4,))
    run = lambda kernel, mib, flops=1, **more: pl.pallas_call(
        kernel, compiler_params=pltpu.CompilerParams(vmem_limit_bytes=mib * 2**20),
        cost_estimate=pl.CostEstimate(flops=flops, bytes_accessed=1, transcendentals=0), **more
    )
    at = lambda turn: (lambda p: p % span == turn)
    inner = lambda offset: (lambda p: p % group == offset)
    mid, half = 2 * group, group // 2

    sym, g_only, node = run(
        own_kernel, 60, out_shape=(rows_of(ps), rows_of(pf), rows_of(node_rows)),
        in_specs=[anywhere] * 3, out_specs=[anywhere] * 3,
        scratch_shapes=[room(3, *square), room(node_rows, lanes), sems, pltpu.SemaphoreType.DMA((6,))], name="own",
    )(inv_diag, low_coupling, up_coupling)

    close = ((-1, inner(2)), (-1, inner(6)))
    away = ((1, inner(2)), (group // 2, inner(6)))
    half_state = (jax.ShapeDtypeStruct((2 * width, 2 * width), bf16),) * 2 + (rows_of(ps),) * 2
    if is_open:
        to_mid = lambda p: p == mid - half
        came_far = sent(
            node, length, (half, lambda p: inner(half)(p) and not to_mid(p)), (group, at(group)), *away
        )
        came_near = sent(node, length, (half, to_mid), *close)
        came_g = sent(g_only, length, (-group, at(mid)), (group, at(3 * group)))
        came_d = sent(sym, length, (mid, at(0)), (-group, at(mid)), (group, at(3 * group)))
        two = jax.ShapeDtypeStruct((2,) + square, f32)
        one = jax.ShapeDtypeStruct(square, f32)
        ready = run(
            functools.partial(ready_kernel, length), 16,
            out_shape=(one, one) + (jax.ShapeDtypeStruct(square, bf16),) * 2,
            in_specs=[vmem], out_specs=[vmem] * 4, name="ready",
        )(node)
        at_m, mid_sym = run(
            functools.partial(mid_kernel, length), 16, 4 * 10**9, out_shape=(two, rows_of(ps)),
            in_specs=[vmem] * 5, out_specs=[vmem] * 2, name="middle",
        )(node, ready[0], *ready[2:], came_d)
        came_sym = sent(mid_sym, length, (mid, at(mid)), (group, at(0)))
        mid_high = sent(mid_sym, length, (group, at(mid)))
        made = run(
            functools.partial(first_kernel, length), 16, out_shape=(two,) + half_state,
            in_specs=[vmem] * 3, out_specs=[vmem] * 5, name="first",
        )(at_m, came_d, came_far)
        kept, *ends, ended = run(
            functools.partial(second_kernel, length), 16, 5 * 10**9, out_shape=(two,) + half_state + (rows_of(ps),),
            in_specs=[vmem] * 13, out_specs=[vmem] * 6,
            input_output_aliases={8 + i: i for i in range(5)}, name="second",
        )(*ready, came_d, came_g, came_sym, mid_high, *made)
        fours = (came_far, came_near)
    else:
        came_far = sent(node, length, (half, inner(half)), *away)
        came_near = sent(node, length, *close)
        diag, cross, below = upper_levels(inv_diag[0], low_coupling[0], up_coupling[0], length)
        kept = jnp.stack([diag, cross])
        *ends, ended = run(
            state_kernel, 16, out_shape=half_state + (rows_of(ps),), in_specs=[vmem] * 4, out_specs=[vmem] * 5,
            name="state",
        )(*below, diag)
        fours = (came_far,)
    one_end = sent(ended, length, (1, inner(0)))
    served = len(fours)
    low_cross, high_cross, *passed = run(
        functools.partial(cross_kernel, length), 16,
        out_shape=(rows_of(pf),) * 2 + (jax.ShapeDtypeStruct((width, 2 * width), bf16),) * 2,
        in_specs=[vmem] * (2 + served), out_specs=[vmem] * 4, name="halve",
    )(*ends[:2], *fours)
    three_cross = sent(low_cross, length, (-5, inner(0)))
    five_cross = sent(high_cross, length, (-3, inner(0)))
    low_ends, high_ends, half_mid, high_half = run(
        functools.partial(ends_kernel, length), 16,
        out_shape=(rows_of(2 * ps),) * 2 + (rows_of(ps), rows_of(state_rows)),
        in_specs=[vmem] * (5 + served), out_specs=[vmem] * 4, name="halves",
    )(*passed, *ends[2:], high_cross, *fours)
    five_ends = sent(high_ends, length, (-3, inner(0)))
    one_mid = sent(half_mid, length, (-7, inner(0)))
    three_ends = sent(low_ends, length, (-5, inner(0)))
    shapes = (jax.ShapeDtypeStruct((2 * width, 2 * width), bf16),) * 2 + (jax.ShapeDtypeStruct((width, 2 * width), f32),)
    composed = run(
        functools.partial(near_kernel, length, False), 16, 4 * 10**9, out_shape=shapes,
        in_specs=[vmem] * 3 + [anywhere], out_specs=[vmem] * 3, name="near",
    )(node, came_near, came_far, one_end)
    by_three, _ = lax.optimization_barrier((three_cross, composed[2]))
    one_cross = sent(by_three, length, (-2, inner(3)))
    to_seven = sent(high_half, length, (-1, inner(0)))
    later, _ = lax.optimization_barrier((came_far, three_cross))
    came_back = sent(later, length, (-3, inner(2)))

    f_high, f_low, rest = run(
        functools.partial(near_kernel, length, True), 16, out_shape=shapes,
        in_specs=[vmem] * 2 + [vmem] * 3, out_specs=[vmem] * 3, name="back",
        input_output_aliases={2: 0, 3: 1, 4: 2},
    )(node, came_back, *composed)

    def chosen(name, flops, *groups, after=()):
        return run(
            functools.partial(choose_kernel, length, *map(len, groups)), 16, flops,
            out_shape=rows_of(2 * ps), in_specs=[vmem] * sum(map(len, groups)) + [anywhere] * len(after),
            out_specs=vmem, name=name,
        )(*(array for arrays in groups for array in arrays), *after)

    early = chosen("early", 1, (one_end, one_mid), (three_cross,), (five_cross,), after=(composed[2],))
    late = chosen("late", 4 * 10**9, (one_cross,), (three_ends,), (five_ends,), after=(early,))
    early_next, late_next = (sent(x, length, (1, inner(1)), (1, inner(3)), (1, inner(5))) for x in (early, late))

    outputs = ()
    for parity, came in ((1, (early, late)), (0, (early_next, late_next))):
        outputs = run(
            functools.partial(lower_kernel, length, parity), 20,
            out_shape=(whole, whole), in_specs=[vmem] * 7 + [anywhere] * len(outputs), out_specs=[anywhere] * 2,
            scratch_shapes=[room(*square)] * 2 + [room(2 * width, 2 * width, kind=bf16)] * 2 + [sems],
            input_output_aliases={7 + i: i for i in range(len(outputs))}, name="lower",
        )(*came, to_seven, f_high, f_low, rest, kept, *outputs)
    return outputs


def solution(mesh):
    placed = (P(axis, None, None),) * 3
    return jax.shard_map(
        body, mesh=mesh, in_specs=placed, out_specs=placed[:2], check_vma=False
    )
```
